32 devices in a mesh: sec: 2 (over y), ty: 16 (over z, x, core).
Axes of the slice: x: 2, y: 2, z: 4, core: 2. Of those that a mesh axis runs over, the one named last changes fastest.
Arguments:
- points: float32 [4, 32768], P(None, ('sec', 'ty')), parts along dimension 1, may hold values from -88 to 2136, as said below
- source: bfloat16 [1024, 2048], P(('sec', 'ty')), parts along dimension 0, may hold values from -4 to 4
- slab_first: int32 [32], P(('sec', 'ty')), parts along dimension 0, may hold values from 0 to 29, as said below
- slab_count: int32 [32], P(('sec', 'ty')), parts along dimension 0, may hold values from 3 to 6, as said below
Outputs:
- rendered: bfloat16 [1024, 2048], P(('sec', 'ty')), parts along dimension 0
- vertex_affines: float32 [6, 128, 256], P(None, ('sec', 'ty')), parts along dimension 1
The draws below stay inside these ranges and needn't reach their ends.
There are 2 independent parts, one for each index of `sec`. The reference program is written for one: setup_inputs(seed, part) draws one part's arguments, and reference() takes and returns one part's arrays. A program takes and returns all parts, laid end to end along the dimension named above; each array names one. Nothing has to cross between parts.
Inputs may be any that keep to these rules, and one draw needn't show every extreme that they name: `points`: for tile t, rows 0 and 1 are fixed positions: each 16 x 16 pixel cell of rows t*32 to (t+1)*32 and columns 0 to 2048 holds 4 of them, listed cell by cell, cells in row-major order; rows 2 and 3 are the matching moving positions. Source block j is rows j*16 to (j+1)*16 - 1. Tile t samples blocks slab_first[t] to slab_first[t] + slab_count[t] - 1, all within rows (t-1)*32 to (t+2)*32 - 1. slab_count reaches 6 on some tile in every draw.
All inputs are finite; a program needn't handle non-finite values.
Results may differ from the reference program's by a relative error of at most 0.008.
Values may be sent and summed in bfloat16 or wider, within the bound.
No kernel may reach another device: no remote copies, remote signals or barrier semaphores. Data moves between devices by JAX's collectives and lax.ppermute only.
A program may use at most 64 MiB of HBM per device.

```python
import jax
import jax.numpy as jnp
from jax import lax

W = 2048
BH = 16
NB = 2
PC = 4
SP = 8
H = 32
K = 6
P_SIZE = 1024
VR = 4
VC = 256
ROWS = 512
N_TY = 16


def strip_shifts(key):
    first_key, second_key = jax.random.split(jax.random.fold_in(key, 31))
    strip_ids = jnp.arange(N_TY, dtype=jnp.int32)
    shifts = jax.random.randint(first_key, (N_TY,), -1, 2, dtype=jnp.int32)
    chosen = jax.random.randint(second_key, (), 1, N_TY - 2, dtype=jnp.int32)
    shifts = jnp.where(strip_ids == chosen, -1, jnp.where(strip_ids == chosen + 1, 1, shifts))
    shifts = jnp.where(strip_ids == 0, jnp.maximum(shifts, 0), shifts)
    shifts = jnp.where(strip_ids == N_TY - 1, jnp.minimum(shifts, 0), shifts)
    return shifts


def slab_bounds(key):
    shifts = strip_shifts(key)
    strip_ids = jnp.arange(N_TY, dtype=jnp.int32)
    from_above = jnp.concatenate([shifts[:1], shifts[:-1]])
    from_below = jnp.concatenate([shifts[1:], shifts[-1:]])
    lowest = jnp.minimum(jnp.minimum(from_above, shifts), from_below)
    highest = jnp.maximum(jnp.maximum(from_above, shifts), from_below)
    first_slab = jnp.maximum(0, jnp.maximum((strip_ids - 1) * NB, (strip_ids + lowest) * NB - 1))
    end_slab = jnp.minimum(N_TY * NB, jnp.minimum((strip_ids + 2) * NB, (strip_ids + 1 + highest) * NB + 1))
    return (first_slab, end_slab - first_slab)


def draw_slab_first(key, part):
    return slab_bounds(key)[0]


def draw_slab_count(key, part):
    return slab_bounds(key)[1]


def draw_points(key, part):
    shifts = strip_shifts(key).astype(jnp.float32)
    subkeys = jax.random.split(jax.random.fold_in(key, 57), 5)
    cell_cols = W // 16
    point_id = jnp.arange(N_TY * P_SIZE, dtype=jnp.int32)
    strip_id = point_id // P_SIZE
    cell_id = point_id % P_SIZE // PC
    base_x = (cell_id % cell_cols * 16).astype(jnp.float32)
    base_y = (strip_id * H + cell_id // cell_cols * 16).astype(jnp.float32)
    jitter = jax.random.uniform(subkeys[0], (2, N_TY * P_SIZE), minval=0.0, maxval=16.0)
    fixed_x = base_x + jitter[0]
    fixed_y = base_y + jitter[1]
    stretch = jax.random.uniform(subkeys[1], (N_TY,), minval=-0.03, maxval=0.03)
    sideways = jax.random.uniform(subkeys[2], (N_TY,), minval=-16.0, maxval=16.0)
    shear_y = jax.random.uniform(subkeys[3], (N_TY,), minval=-0.004, maxval=0.004)
    wobble = jnp.clip(jax.random.normal(subkeys[4], (2, N_TY * P_SIZE)), -3.0, 3.0)
    centre = W / 2.0
    moved_x = centre + (1.0 + stretch[strip_id]) * (fixed_x - centre) + sideways[strip_id] + wobble[0]
    moved_y = fixed_y + shifts[strip_id] * H + shear_y[strip_id] * (fixed_x - centre) + wobble[1]
    return jnp.stack([fixed_x, fixed_y, moved_x, moved_y]).astype(jnp.float32)


def block_scale(own_key, shape, cuts, low, high):
    gain = 1.0
    for dim, blocks in cuts:
        draws = jax.random.uniform(jax.random.fold_in(jax.random.fold_in(own_key, 6), dim), (blocks,), jnp.float32, low / len(cuts), high / len(cuts))
        gain = gain * jnp.repeat(jnp.exp(draws), shape[dim] // blocks).reshape((-1,) + (1,) * (len(shape) - 1 - dim))
    return gain


def bell_draw(own_key, extent, deviation, most, cuts=(), kind=jnp.bfloat16):
    drawn = deviation * jax.random.normal(own_key, extent, jnp.float32)
    if cuts:
        drawn = drawn * block_scale(own_key, extent, cuts, -0.22, 0.18)
    return jnp.clip(drawn, -most, most).astype(kind)


def setup_inputs(seed: int = 0, part: int = 0) -> dict:
    splits = jax.random.split(jax.random.key(seed), 5)
    part_splits = jax.random.split(jax.random.fold_in(splits[4], part), 5)
    points = draw_points(jax.random.fold_in(jax.random.fold_in(splits[4], part), 71), part)
    source = bell_draw(part_splits[1], (ROWS, W), 1.0, 4.0, ((0, 16),))
    slab_first = draw_slab_first(jax.random.fold_in(jax.random.fold_in(splits[4], part), 71), part)
    slab_count = draw_slab_count(jax.random.fold_in(jax.random.fold_in(splits[4], part), 71), part)
    return {"points": points, "source": source, "slab_first": slab_first, "slab_count": slab_count}


PRECISE = lax.Precision.HIGHEST
RIDGE_TERM = 0.01


def solve_affine(moments, vertex_x, vertex_y):
    mass = moments[0]
    mean_px = moments[1] / mass
    mean_py = moments[2] / mass
    mean_qx = moments[3] / mass
    mean_qy = moments[4] / mass
    cov_xx = moments[5] / mass - mean_px * mean_px + RIDGE_TERM
    cov_xy = moments[6] / mass - mean_px * mean_py
    cov_yy = moments[7] / mass - mean_py * mean_py + RIDGE_TERM
    cross_xx = moments[8] / mass - mean_qx * mean_px
    cross_xy = moments[9] / mass - mean_qx * mean_py
    cross_yx = moments[10] / mass - mean_qy * mean_px
    cross_yy = moments[11] / mass - mean_qy * mean_py
    determ = cov_xx * cov_yy - cov_xy * cov_xy
    lin_xx = (cross_xx * cov_yy - cross_xy * cov_xy) / determ
    lin_xy = (cross_xy * cov_xx - cross_xx * cov_xy) / determ
    lin_yx = (cross_yx * cov_yy - cross_yy * cov_xy) / determ
    lin_yy = (cross_yy * cov_xx - cross_yx * cov_xy) / determ
    delta_x = vertex_x - mean_px
    delta_y = vertex_y - mean_py
    shift_x = mean_qx + lin_xx * delta_x + lin_xy * delta_y - vertex_x
    shift_y = mean_qy + lin_yx * delta_x + lin_yy * delta_y - vertex_y
    return jnp.stack([lin_xx, lin_xy, lin_yx, lin_yy, shift_x, shift_y])


def block_moments(pts, usable, strip_id):
    block_count = W // 128
    per_block = VC // block_count
    cell_rows = pts.shape[1] // (block_count * 8 * PC)
    grid = pts.reshape(4, cell_rows, block_count, 8 * PC)
    live = usable.reshape(cell_rows, block_count, 8 * PC)
    grid = jnp.pad(grid, ((0, 0), (0, 0), (1, 1), (0, 0)))
    live = jnp.pad(live, ((0, 0), (1, 1), (0, 0)))
    near = jnp.concatenate([grid[:, :, 0:block_count], grid[:, :, 1:block_count + 1],
                            grid[:, :, 2:block_count + 2]], axis=3)
    near_live = jnp.concatenate([live[:, 0:block_count], live[:, 1:block_count + 1],
                                 live[:, 2:block_count + 2]], axis=2)
    near = jnp.transpose(near, (0, 2, 1, 3)).reshape(4, block_count, cell_rows * 24 * PC)
    near_live = jnp.transpose(near_live, (1, 0, 2)).reshape(block_count, cell_rows * 24 * PC)
    centre_y = strip_id.astype(jnp.float32) * H + H / 2.0
    anchor = jnp.arange(block_count, dtype=jnp.float32) * 128.0 + 64.0
    fixed_x = (near[0] - anchor[:, None]) / H
    fixed_y = (near[1] - centre_y) / H
    moved_x = (near[2] - anchor[:, None]) / H
    moved_y = (near[3] - centre_y) / H
    unit_row = jnp.ones_like(fixed_x)
    features = jnp.stack([unit_row, fixed_x, fixed_y, moved_x, moved_y, fixed_x * fixed_x, fixed_x * fixed_y,
                          fixed_y * fixed_y, moved_x * fixed_x, moved_x * fixed_y, moved_y * fixed_x,
                          moved_y * fixed_y], axis=1) * near_live[:, None, :]
    vertex_col = jnp.arange(VC, dtype=jnp.float32).reshape(block_count, per_block) * SP + SP / 2.0
    vertex_row = jnp.arange(VR, dtype=jnp.float32) * SP + SP / 2.0 - H / 2.0
    gap_x = (near[0][:, :, None] - vertex_col[:, None, :]) / H
    gap_y = fixed_y[:, :, None] - (vertex_row / H)[None, None, :]
    weight_x = jnp.exp(-2.0 * gap_x * gap_x)
    weight_y = jnp.exp(-2.0 * gap_y * gap_y)
    weighted = features[:, :, None, :] * jnp.transpose(weight_y, (0, 2, 1))[:, None, :, :]
    moments = jnp.einsum("bkrm,bmc->bkrc", weighted, weight_x, precision=PRECISE)
    return jnp.transpose(moments, (1, 2, 0, 3)).reshape(12, VR, VC)


def vertex_frame():
    block_count = W // 128
    per_block = VC // block_count
    anchor = jnp.arange(block_count, dtype=jnp.float32) * 128.0 + 64.0
    vertex_col = jnp.arange(VC, dtype=jnp.float32) * SP + SP / 2.0
    vertex_row = jnp.arange(VR, dtype=jnp.float32) * SP + SP / 2.0 - H / 2.0
    column_anchor = jnp.repeat(anchor, per_block)
    vertex_x = jnp.broadcast_to(((vertex_col - column_anchor) / H)[None, :], (VR, VC))
    vertex_y = jnp.broadcast_to((vertex_row / H)[:, None], (VR, VC))
    return vertex_x, vertex_y


def tent_tables():
    row_local = jnp.arange(H, dtype=jnp.float32)
    ext_row = (jnp.arange(VR + 2, dtype=jnp.float32) - 1.0) * SP + SP / 2.0
    tent_rows = jnp.maximum(0.0, 1.0 - jnp.abs(row_local[:, None] - ext_row[None, :]) / SP)
    column = jnp.clip(jnp.arange(W, dtype=jnp.float32), SP / 2.0, W - SP / 2.0)
    vertex_col = jnp.arange(VC, dtype=jnp.float32) * SP + SP / 2.0
    tent_cols = jnp.maximum(0.0, 1.0 - jnp.abs(column[None, :] - vertex_col[:, None]) / SP)
    return tent_rows, tent_cols


def displace(near_shift, tent_rows, tent_cols):
    first_part = jnp.dot(jnp.dot(tent_rows, near_shift[0], precision=PRECISE), tent_cols, precision=PRECISE)
    second_part = jnp.dot(jnp.dot(tent_rows, near_shift[1], precision=PRECISE), tent_cols, precision=PRECISE)
    return jnp.stack([first_part, second_part])


def render_strip(slab_rows, first_slab, slab_total, disp, strip_id):
    block_count = W // 128
    samp_y = jnp.arange(H, dtype=jnp.float32)[:, None] + H * disp[1]
    samp_x = jnp.arange(W, dtype=jnp.float32)[None, :] + H * disp[0]
    slot_ids = jnp.arange(K, dtype=jnp.int32)
    slot_row = (first_slab + slot_ids) * BH - strip_id * H
    row_pos = (slot_row[:, None] + jnp.arange(BH, dtype=jnp.int32)[None, :]).reshape(K * BH).astype(jnp.float32)
    slot_live = jnp.repeat((slot_ids < slab_total).astype(jnp.float32), BH)
    padded = jnp.pad(slab_rows, ((0, 0), (64, 192)))
    blocks = padded.reshape(K * BH, block_count + 2, 128)
    windows = jnp.concatenate([blocks[:, :block_count], blocks[:, 1:block_count + 1]], axis=2)
    windows = jnp.transpose(windows, (1, 0, 2))
    block_y = samp_y.reshape(H, block_count, 128).transpose(1, 0, 2).reshape(block_count, H * 128)
    block_x = samp_x.reshape(H, block_count, 128).transpose(1, 0, 2).reshape(block_count, H * 128)
    block_ids = jnp.arange(block_count, dtype=jnp.int32)

    def one_block(packed):
        along_y, along_x, window, block_id = packed
        col_pos = block_id.astype(jnp.float32) * 128.0 - 64.0 + jnp.arange(256, dtype=jnp.float32)
        across = jnp.maximum(0.0, 1.0 - jnp.abs(along_x[:, None] - col_pos[None, :])).astype(jnp.bfloat16)
        mixed_rows = jnp.dot(across.astype(jnp.float32), jnp.transpose(window.astype(jnp.float32)), precision=PRECISE)
        tent_y = jnp.maximum(0.0, 1.0 - jnp.abs(along_y[:, None] - row_pos[None, :])) * slot_live
        return jnp.sum(mixed_rows * tent_y, axis=1)

    pieces = lax.map(one_block, (block_y, block_x, windows, block_ids))
    return pieces.reshape(block_count, H, 128).transpose(1, 0, 2).reshape(H, W).astype(jnp.bfloat16)


def reference(points, source, slab_first, slab_count):
    strip_ids = jnp.arange(N_TY, dtype=jnp.int32)
    padded_pts = jnp.pad(points, ((0, 0), (P_SIZE, P_SIZE)))
    vertex_x, vertex_y = vertex_frame()

    def fit_strip(strip_id):
        nearby = lax.dynamic_slice_in_dim(padded_pts, strip_id * P_SIZE, 3 * P_SIZE, 1)
        owners = strip_id - 1 + jnp.arange(3 * P_SIZE, dtype=jnp.int32) // P_SIZE
        usable = ((owners >= 0) & (owners < N_TY)).astype(jnp.float32)
        return solve_affine(block_moments(nearby, usable, strip_id), vertex_x, vertex_y)

    affines = lax.map(fit_strip, strip_ids)
    vertex_affines = jnp.transpose(affines, (1, 0, 2, 3)).reshape(6, N_TY * VR, VC)
    flat_shift = vertex_affines[4:6]
    extended = jnp.concatenate([flat_shift[:, :1], flat_shift, flat_shift[:, -1:]], axis=1)
    source_pad = jnp.pad(source, ((0, K * BH), (0, 0)))
    tent_rows, tent_cols = tent_tables()

    def render_one(strip_id):
        near_shift = lax.dynamic_slice_in_dim(extended, strip_id * VR, VR + 2, 1)
        disp = displace(near_shift, tent_rows, tent_cols)
        first_slab = slab_first[strip_id]
        slab_total = slab_count[strip_id]
        slab_rows = lax.dynamic_slice_in_dim(source_pad, (first_slab * BH).astype(jnp.int32), K * BH, 0)
        return render_strip(slab_rows, first_slab, slab_total, disp, strip_id)

    rendered = lax.map(render_one, strip_ids).reshape(N_TY * H, W)
    return rendered, vertex_affines
```

```python
import functools

import jax
import jax.numpy as jnp
import numpy as np
from jax import lax
from jax.experimental import pallas as pl
from jax.experimental.pallas import tpu as pltpu
from jax.sharding import PartitionSpec as P

BH = 16
PC = 4
SP = 8
VR = 4
LANES = 128
CELL = 16
RIDGE_TERM = 0.01
FEATS = 12
ER = 8
NF = FEATS * ER
GROUP_PX = LANES // PC * CELL
NV = GROUP_PX // SP + 2 * LANES // SP
EXP2_SCALE = 2.0 * float(np.log2(np.e))
TAPS = 8
TOP_PAD = 8
LOW_PAD = 16


def fiota(shape, dim):
    return lax.broadcasted_iota(jnp.int32, shape, dim).astype(jnp.float32)


def local_points(pts, tile, cell_cols, height):
    lane = lax.broadcasted_iota(jnp.int32, (1, pts.shape[1]), 1)
    cell = lane // PC
    base_x = (cell % cell_cols * CELL).astype(jnp.float32)
    base_y = (tile * height + cell // cell_cols * CELL).astype(jnp.float32)
    fixed_x, fixed_y = pts[0:1], pts[1:2]
    return jnp.concatenate(
        [fixed_x - base_x, fixed_y - base_y, pts[2:3] - fixed_x, pts[3:4] - fixed_y], axis=0
    )


def split_pair(value):
    high = value.astype(jnp.bfloat16).astype(jnp.float32)
    return high, value - high


def pack_kernel(own_ref, mate_ref, source_ref, packed_ref):
    height, width = source_ref.shape
    half = packed_ref.shape[1]
    tile = lax.axis_index("ty")
    for part in range(width // half):
        packed_ref[part * height : (part + 1) * height, :] = source_ref[:, part * half : (part + 1) * half]
    rows = []
    for ref, owner in ((own_ref, tile), (mate_ref, tile + 1 - 2 * (tile % 2))):
        rows.extend(split_pair(local_points(ref[...], owner, width // CELL, height)))
    base = width // half * height
    packed_ref[base : base + 16, :] = jnp.concatenate(rows, axis=0).astype(jnp.bfloat16)


def main_kernel(
    strips,
    first_ref,
    count_ref,
    own_ref,
    mate_ref,
    source_ref,
    mate_source_ref,
    packed_ref,
    far_ref,
    out_ref,
    affine_ref,
    feat_ref,
    weight_ref,
    slab_ref,
    shift_ref,
    mixed_ref,
    bound_ref,
):
    height, width = source_ref.shape
    tile_len = own_ref.shape[1]
    cell_cols = width // CELL
    cell_rows = height // CELL
    groups = width // GROUP_PX
    blocks = width // LANES
    halves = blocks // 8
    tile = lax.axis_index("ty")
    odd = tile % 2
    toward = 1 - 2 * odd
    mate = tile + toward
    partner = tile - toward
    partner_mate = tile - 2 * toward
    beyond = tile + 2 * toward

    slots_from = first_ref[0] * BH - (tile - 1) * height
    slots_to = slots_from + count_ref[0] * BH
    left_half = lax.broadcasted_iota(jnp.int32, (1, LANES), 1) < LANES // 2
    pitch = slab_ref.shape[0] // (TOP_PAD + 3 * height + LOW_PAD)
    for edge in (TOP_PAD - 2, TOP_PAD - 1, TOP_PAD + 3 * height, TOP_PAD + 3 * height + 1):
        slab_ref[edge * pitch : (edge + 1) * pitch, :] = jnp.zeros((pitch, LANES), jnp.float32)

    half_cols = packed_ref.shape[1]

    def place(load, row_start, chunk):
        local = row_start + chunk * 16
        row = lax.broadcasted_iota(jnp.int32, (16, 1), 0) + local
        live = ((row >= slots_from) & (row < slots_to)).astype(jnp.float32)
        before = jnp.zeros((16, LANES), jnp.float32)
        for b in range(blocks + 1):
            if b < blocks:
                now = pltpu.roll(load(b).astype(jnp.float32) * live, LANES // 2, axis=1)
            else:
                now = jnp.zeros((16, LANES), jnp.float32)
            merged = jnp.where(left_half, before, now)
            start = (TOP_PAD + local) * pitch + b
            slab_ref[pl.ds(start, 16, stride=pitch), :] = merged
            before = now

    for chunk in range(height // 16):
        rows = slice(chunk * 16, chunk * 16 + 16)
        place(lambda b: source_ref[rows, b * LANES : (b + 1) * LANES], height, chunk)
        place(lambda b: mate_source_ref[rows, b * LANES : (b + 1) * LANES], height + toward * height, chunk)

        def from_packed(b):
            part = b * LANES // half_cols
            lane = b * LANES - part * half_cols
            return packed_ref[part * height + chunk * 16 : part * height + chunk * 16 + 16, lane : lane + LANES]

        place(from_packed, height - toward * height, chunk)

    point_rows = packed_ref[packed_ref.shape[0] - 16 :, :].astype(jnp.float32)
    far_rows = far_ref[...].astype(jnp.float32)
    sets = (
        (local_points(own_ref[...], tile, cell_cols, height), tile),
        (local_points(mate_ref[...], mate, cell_cols, height), mate),
        (point_rows[0:4] + point_rows[4:8], partner),
        (point_rows[8:12] + point_rows[12:16], partner_mate),
        (far_rows[0:4] + far_rows[4:8], beyond),
    )
    ext_row = lax.broadcasted_iota(jnp.int32, (ER, 1), 0)
    vertex_y = (fiota((ER, 1), 0) * SP + (SP / 2.0 - SP - height / 2.0)) / height
    ext_tile = tile + jnp.where(ext_row == 0, -1, jnp.where(ext_row == VR + 1, 1, 0))
    scale = float(np.sqrt(EXP2_SCALE))
    lane_px = fiota((1, LANES), 1)
    lane_px = (lax.broadcasted_iota(jnp.int32, (1, LANES), 1) // PC * CELL).astype(jnp.float32) - GROUP_PX / 2.0
    vertex_ids = lax.broadcasted_iota(jnp.int32, (NV, LANES), 0)
    point_block = lax.broadcasted_iota(jnp.int32, (NV, LANES), 1) // (LANES // CELL * PC)
    band = (jnp.abs(vertex_ids // (LANES // SP) - 1 - point_block) <= 1).astype(jnp.float32)
    vertex_scaled = (fiota((NV, 1), 0) * SP + (SP / 2.0 - LANES - GROUP_PX / 2.0)) * (scale / height)
    zero_rows = jnp.zeros((LANES - NV, weight_ref.shape[2]), jnp.bfloat16)

    totals = []
    for g in range(groups):
        weight_ref[g, NV:LANES, :] = zero_rows
        weight_ref[g, LANES + NV :, :] = zero_rows
        for s, (pts, owner) in enumerate(sets):
            usable = (jnp.abs(owner - ext_tile) <= 1) & (owner >= 0) & (owner < strips)
            usable = usable.astype(jnp.float32)
            for c in range(cell_rows):
                lanes = slice(c * cell_cols * PC + g * LANES, c * cell_cols * PC + (g + 1) * LANES)
                chunk = slice((s * cell_rows + c) * LANES, (s * cell_rows + c + 1) * LANES)
                px = (pts[0:1, lanes] + lane_px) / height
                py = (pts[1:2, lanes] + ((owner - tile) * height + c * CELL).astype(jnp.float32)) / height - 0.5
                dx = pts[2:3, lanes] / height
                dy = pts[3:4, lanes] / height
                gap_y = (py - vertex_y) * scale
                wy = jnp.exp2(-(gap_y * gap_y)) * usable
                wpx, wpy, wdx, wdy = wy * px, wy * py, wy * dx, wy * dy
                rows = (wy, wpx, wpy, wdx, wdy, wpx * px, wpx * py, wpy * py, wdx * px, wdx * py, wdy * px, wdy * py)
                for f in range(0, FEATS, 2):
                    high, low = split_pair(jnp.concatenate(rows[f : f + 2], axis=0))
                    feat_ref[g, f * ER : (f + 2) * ER, chunk] = high.astype(jnp.bfloat16)
                    feat_ref[g, NF + f * ER : NF + (f + 2) * ER, chunk] = low.astype(jnp.bfloat16)
                gap_x = px * scale - vertex_scaled
                wx = jnp.exp2(-(gap_x * gap_x)) * band
                high, low = split_pair(wx)
                weight_ref[g, 0:NV, chunk] = high.astype(jnp.bfloat16)
                weight_ref[g, LANES : LANES + NV, chunk] = low.astype(jnp.bfloat16)
        both = lax.dot_general(
            feat_ref[g], weight_ref[g], (((1,), (1,)), ((), ())), preferred_element_type=jnp.float32
        )
        both = both[:NF] + both[NF:]
        totals.append(both[:, :LANES] + both[:, LANES:])

    lane = lax.broadcasted_iota(jnp.int32, (1, LANES), 1)
    per_group = GROUP_PX // SP
    affines = []
    for h in range(halves):
        moments = None
        vertex_group = 2 * h + lane // per_group
        for g in range(groups):
            start = g * per_group - LANES // SP - h * LANES
            if start + NV <= 0 or start >= LANES:
                continue
            part = pltpu.roll(totals[g], start % LANES, axis=1)
            inside = ((lane >= start) & (lane < start + NV)).astype(jnp.float32)
            move = ((g - vertex_group) * (GROUP_PX // height)).astype(jnp.float32)
            part = [part[f * ER : (f + 1) * ER] * inside for f in range(FEATS)]
            part[5] = part[5] + move * (2.0 * part[1] + move * part[0])
            part[6] = part[6] + move * part[2]
            part[8] = part[8] + move * part[3]
            part[10] = part[10] + move * part[4]
            part[1] = part[1] + move * part[0]
            moments = part if moments is None else [x + y for x, y in zip(moments, part)]
        inverse = 1.0 / moments[0]
        mean_px, mean_py, mean_dx, mean_dy = [moments[i] * inverse for i in range(1, 5)]
        cov_xx = moments[5] * inverse - mean_px * mean_px + RIDGE_TERM
        cov_xy = moments[6] * inverse - mean_px * mean_py
        cov_yy = moments[7] * inverse - mean_py * mean_py + RIDGE_TERM
        cross_xx = moments[8] * inverse - mean_dx * mean_px - RIDGE_TERM
        cross_xy = moments[9] * inverse - mean_dx * mean_py
        cross_yx = moments[10] * inverse - mean_dy * mean_px
        cross_yy = moments[11] * inverse - mean_dy * mean_py - RIDGE_TERM
        over = 1.0 / (cov_xx * cov_yy - cov_xy * cov_xy)
        lin_xx = (cross_xx * cov_yy - cross_xy * cov_xy) * over
        lin_xy = (cross_xy * cov_xx - cross_xx * cov_xy) * over
        lin_yx = (cross_yx * cov_yy - cross_yy * cov_xy) * over
        lin_yy = (cross_yy * cov_xx - cross_yx * cov_xy) * over
        vertex_x = ((lane % per_group * SP).astype(jnp.float32) + (SP - GROUP_PX) / 2.0) / height
        delta_x = vertex_x - mean_px
        delta_y = vertex_y - mean_py
        shift_x = mean_dx + lin_xx * delta_x + lin_xy * delta_y
        shift_y = mean_dy + lin_yx * delta_x + lin_yy * delta_y
        results = (lin_xx + 1.0, lin_xy, lin_yx, lin_yy + 1.0, shift_x, shift_y)
        for i, value in enumerate(results):
            affine_ref[i, :, h * LANES : (h + 1) * LANES] = value[1 : VR + 1]
        affines.append((shift_x, shift_y))

    ext = lax.broadcasted_iota(jnp.int32, (ER, LANES), 0)
    spread = lax.broadcasted_iota(jnp.int32, (8, LANES), 0) * (LANES // SP) + lax.broadcasted_iota(jnp.int32, (8, LANES), 1) // SP
    along = (lane % SP).astype(jnp.float32) / SP - 0.5
    left_side = along < 0.0
    for comp in range(2):
        rows = []
        for h in range(halves):
            value = affines[h][comp] * float(height)
            value = jnp.where((ext == 0) & (tile == 0), jnp.broadcast_to(value[1:2], value.shape), value)
            value = jnp.where((ext == VR + 1) & (tile == strips - 1), jnp.broadcast_to(value[VR : VR + 1], value.shape), value)
            rows.append(value)
        for h in range(halves):
            value = rows[h]
            prior = rows[h - 1] if h > 0 else value
            later = rows[h + 1] if h + 1 < halves else value
            first = jnp.broadcast_to(prior[:, LANES - 1 :] if h > 0 else value[:, :1], value.shape)
            last = jnp.broadcast_to(later[:, :1] if h + 1 < halves else value[:, LANES - 1 :], value.shape)
            before = jnp.where(lane == 0, first, pltpu.roll(value, 1, axis=1))
            after = jnp.where(lane == LANES - 1, last, pltpu.roll(value, LANES - 1, axis=1))
            rise = value - before
            climb = after - value
            for e in range(VR + 2):
                at = jnp.take_along_axis(jnp.broadcast_to(value[e : e + 1], (8, LANES)), spread, axis=1)
                low = jnp.take_along_axis(jnp.broadcast_to(rise[e : e + 1], (8, LANES)), spread, axis=1)
                high = jnp.take_along_axis(jnp.broadcast_to(climb[e : e + 1], (8, LANES)), spread, axis=1)
                shift_ref[comp, e, h * 8 : (h + 1) * 8, :] = at + along * jnp.where(left_side, low, high)
            if comp == 1:
                least = jnp.min(jnp.minimum(value, jnp.minimum(before, after)), axis=1, keepdims=True)
                most = jnp.max(jnp.maximum(value, jnp.maximum(before, after)), axis=1, keepdims=True)
                for e in range(VR + 2):
                    bound_ref[0, h * ER + e] = least[e, 0]
                    bound_ref[1, h * ER + e] = most[e, 0]

    last_row = 3.0 * height
    lane_x = fiota((8, LANES), 1) + LANES / 2.0

    def bounds(e, h, row, ratio):
        at = h * ER + e
        low = row + (1.0 - ratio) * bound_ref[0, at] + ratio * bound_ref[0, at + 1]
        top = row + (1.0 - ratio) * bound_ref[1, at] + ratio * bound_ref[1, at + 1]
        low = jnp.clip(low - 0.01, -1.5, last_row + 0.5)
        top = jnp.clip(top + 0.01, -1.5, last_row + 0.5)
        low = (low + 64.0).astype(jnp.int32) - 64
        top = (top + 64.0).astype(jnp.int32) - 64
        return low, top

    def positions(e, h, row, ratio):
        blocks_of = slice(h * 8, h * 8 + 8)
        sample_x = lane_x + ((1.0 - ratio) * shift_ref[0, e, blocks_of, :] + ratio * shift_ref[0, e + 1, blocks_of, :])
        sample_y = row + ((1.0 - ratio) * shift_ref[1, e, blocks_of, :] + ratio * shift_ref[1, e + 1, blocks_of, :])
        return sample_x, sample_y

    def render(e, h, row, ratio, start):
        sample_x, sample_y = positions(e, h, row, ratio)
        floor_x = jnp.floor(sample_x)
        floor_y = jnp.floor(sample_y)
        part_x = sample_x - floor_x
        part_y = sample_y - floor_y
        floor_y = jnp.clip(floor_y, -2.0, last_row)
        floor_x = jnp.clip(floor_x, -2.0, 2.0 * LANES)
        weight_0 = jnp.where((floor_x >= 0.0) & (floor_x < 2.0 * LANES), 1.0 - part_x, 0.0)
        weight_1 = jnp.where((floor_x >= -1.0) & (floor_x < 2.0 * LANES - 1.0), part_x, 0.0)
        index = floor_x.astype(jnp.int32)
        index_0 = index & (LANES - 1)
        index_1 = (index + 1) & (LANES - 1)
        in_0 = floor_x < float(LANES)
        in_1 = floor_x < float(LANES - 1)
        step = floor_y.astype(jnp.int32) - start
        zero = jnp.zeros((8, LANES), jnp.float32)
        top_0 = top_1 = low_0 = low_1 = zero
        before = step == -1
        for j in range(TAPS):
            at = (start + (TOP_PAD + j)) * pitch + h * 8
            near = slab_ref[pl.ds(at, 8), :]
            next_one = slab_ref[pl.ds(at + 1, 8), :]
            value_0 = jnp.where(
                in_0, jnp.take_along_axis(near, index_0, axis=1), jnp.take_along_axis(next_one, index_0, axis=1)
            )
            value_1 = jnp.where(
                in_1, jnp.take_along_axis(near, index_1, axis=1), jnp.take_along_axis(next_one, index_1, axis=1)
            )
            here = step == j
            top_0 = jnp.where(here, value_0, top_0)
            top_1 = jnp.where(here, value_1, top_1)
            low_0 = jnp.where(before, value_0, low_0)
            low_1 = jnp.where(before, value_1, low_1)
            before = here
        upper = weight_0 * top_0 + weight_1 * top_1
        lower = weight_0 * low_0 + weight_1 * low_1
        return upper + part_y * (lower - upper)

    def each(q, todo):
        e = (q + 1) // 2
        for s in range(4):
            row = q * 4 + s
            ratio = (row - SP * e + SP // 2).astype(jnp.float32) * (1.0 / SP)
            for h in range(halves):
                todo(e, h, row, row.astype(jnp.float32) + float(height), ratio)

    def main_body(q, carry):
        most = jnp.int32(0)

        def todo(e, h, row, place_y, ratio):
            nonlocal most
            low, top = bounds(e, h, place_y, ratio)
            mixed_ref[pl.ds(row * blocks + h * 8, 8), :] = render(e, h, place_y, ratio, low)
            most = jnp.maximum(most, top - low)

        each(q, todo)
        bound_ref[2, q] = most.astype(jnp.float32)
        return carry

    lax.fori_loop(0, height // 4, main_body, 0)

    def rest_body(q, carry):
        @pl.when(bound_ref[2, q] > TAPS - 2.0)
        def _():
            def todo(e, h, row, place_y, ratio):
                low, top = bounds(e, h, place_y, ratio)

                def more(i, c):
                    at = pl.ds(row * blocks + h * 8, 8)
                    mixed_ref[at, :] = mixed_ref[at, :] + render(e, h, place_y, ratio, low + i * TAPS)
                    return c

                lax.fori_loop(1, (top - low + 1 + TAPS) // TAPS, more, 0)

            each(q, todo)

        return carry

    lax.fori_loop(0, height // 4, rest_body, 0)

    for part in range(height // 16):
        for b in range(blocks):
            value = mixed_ref[pl.ds(part * 16 * blocks + b, 16, stride=blocks), :]
            out_ref[part * 16 : part * 16 + 16, b * LANES : (b + 1) * LANES] = value.astype(jnp.bfloat16)


def per_device(points, source, slab_first, slab_count):
    strips = lax.axis_size("ty")
    height, width = source.shape
    tile_len = points.shape[1]
    blocks = width // LANES
    in_chip = [(i, i ^ 1) for i in range(strips)]
    across = []
    for i in range(1, strips - 1, 2):
        across.extend([(i, i + 1), (i + 1, i)])
    vmem = pl.BlockSpec(memory_space=pltpu.VMEM)
    smem = pl.BlockSpec(memory_space=pltpu.SMEM)
    mate_points = lax.ppermute(points, "ty", in_chip)
    packed_rows = width // tile_len * height + 16
    packed = pl.pallas_call(
        pack_kernel,
        out_shape=jax.ShapeDtypeStruct((packed_rows, tile_len), jnp.bfloat16),
        in_specs=[vmem] * 3,
        out_specs=vmem,
    )(points, mate_points, source)
    arrived = lax.ppermute(packed, "ty", across)
    mate_source = lax.ppermute(source, "ty", in_chip)
    far = lax.ppermute(arrived[packed_rows - 16 : packed_rows - 8], "ty", in_chip)
    groups = width // GROUP_PX
    points_axis = 5 * tile_len // groups
    pitch = (blocks + 1 + 7) // 8 * 8
    return pl.pallas_call(
        functools.partial(main_kernel, strips),
        out_shape=(
            jax.ShapeDtypeStruct((height, width), jnp.bfloat16),
            jax.ShapeDtypeStruct((6, VR, width // SP), jnp.float32),
        ),
        in_specs=[smem, smem] + [vmem] * 6,
        out_specs=(vmem, vmem),
        scratch_shapes=[
            pltpu.VMEM((groups, 2 * NF, points_axis), jnp.bfloat16),
            pltpu.VMEM((groups, 2 * LANES, points_axis), jnp.bfloat16),
            pltpu.VMEM(((TOP_PAD + 3 * height + LOW_PAD) * pitch, LANES), jnp.float32),
            pltpu.VMEM((2, VR + 2, blocks, LANES), jnp.float32),
            pltpu.VMEM((height * blocks, LANES), jnp.float32),
            pltpu.SMEM((3, 2 * ER), jnp.float32),
        ],
        compiler_params=pltpu.CompilerParams(vmem_limit_bytes=32 * 1024 * 1024),
    )(slab_first, slab_count, points, mate_points, source, mate_source, arrived, far)


def solution(mesh):
    return jax.shard_map(
        per_device,
        mesh=mesh,
        in_specs=(
            P(None, ("sec", "ty")),
            P(("sec", "ty"), None),
            P(("sec", "ty")),
            P(("sec", "ty")),
        ),
        out_specs=(P(("sec", "ty"), None), P(None, ("sec", "ty"), None)),
        check_vma=False,
    )
```

```python
import functools

import jax
import jax.numpy as jnp
import numpy as np
from jax import lax
from jax.experimental import pallas as pl
from jax.experimental.pallas import tpu as pltpu
from jax.sharding import PartitionSpec as P

BH = 16
PC = 4
SP = 8
VR = 4
LANES = 128
CELL = 16
RIDGE_TERM = 0.01
FEATS = 12
ER = 8
NF = FEATS * ER
GROUP_PX = LANES // PC * CELL
NV = GROUP_PX // SP + 2 * LANES // SP
EXP2_SCALE = 2.0 * float(np.log2(np.e))
TAPS = 8


def fiota(shape, dim):
    return lax.broadcasted_iota(jnp.int32, shape, dim).astype(jnp.float32)


def local_points(pts, tile, cell_cols, height):
    lane = lax.broadcasted_iota(jnp.int32, (1, pts.shape[1]), 1)
    cell = lane // PC
    base_x = (cell % cell_cols * CELL).astype(jnp.float32)
    base_y = (tile * height + cell // cell_cols * CELL).astype(jnp.float32)
    fixed_x, fixed_y = pts[0:1], pts[1:2]
    return jnp.concatenate(
        [fixed_x - base_x, fixed_y - base_y, pts[2:3] - fixed_x, pts[3:4] - fixed_y], axis=0
    )


def split_pair(value):
    high = value.astype(jnp.bfloat16).astype(jnp.float32)
    return high, value - high


def pack_kernel(own_ref, mate_ref, source_ref, packed_ref):
    height, width = source_ref.shape
    half = packed_ref.shape[1]
    tile = lax.axis_index("ty")
    for part in range(width // half):
        packed_ref[part * height : (part + 1) * height, :] = source_ref[:, part * half : (part + 1) * half]
    rows = []
    for ref, owner in ((own_ref, tile), (mate_ref, tile + 1 - 2 * (tile % 2))):
        rows.extend(split_pair(local_points(ref[...], owner, width // CELL, height)))
    base = width // half * height
    packed_ref[base : base + 16, :] = jnp.concatenate(rows, axis=0).astype(jnp.bfloat16)


def main_kernel(
    strips,
    first_ref,
    count_ref,
    own_ref,
    mate_ref,
    source_ref,
    mate_source_ref,
    packed_ref,
    far_ref,
    out_ref,
    affine_ref,
    feat_ref,
    weight_ref,
    slab_ref,
    sample_ref,
    base_ref,
    span_ref,
    mixed_ref,
):
    height, width = source_ref.shape
    tile_len = own_ref.shape[1]
    cell_cols = width // CELL
    cell_rows = height // CELL
    groups = width // GROUP_PX
    blocks = width // LANES
    halves = blocks // 8
    tile = lax.axis_index("ty")
    odd = tile % 2
    toward = 1 - 2 * odd
    mate = tile + toward
    partner = tile - toward
    partner_mate = tile - 2 * toward
    beyond = tile + 2 * toward

    slots_from = first_ref[0] * BH - (tile - 1) * height
    slots_to = slots_from + count_ref[0] * BH
    left_half = lax.broadcasted_iota(jnp.int32, (1, LANES), 1) < LANES // 2
    half_cols = packed_ref.shape[1]
    slab_ref[3 * height :, :] = jnp.zeros((slab_ref.shape[0] - 3 * height, slab_ref.shape[1]), jnp.bfloat16)

    def place(load, row_start, chunk):
        local = row_start + chunk * 16
        row = lax.broadcasted_iota(jnp.int32, (16, 1), 0) + local
        live = ((row >= slots_from) & (row < slots_to)).astype(jnp.float32)
        before = jnp.zeros((16, LANES), jnp.float32)
        for b in range(blocks + 1):
            if b < blocks:
                now = pltpu.roll(load(b).astype(jnp.float32) * live, LANES // 2, axis=1)
            else:
                now = jnp.zeros((16, LANES), jnp.float32)
            merged = jnp.where(left_half, before, now).astype(jnp.bfloat16)
            slab_ref[pl.ds(pl.multiple_of(local, 16), 16), b * LANES : (b + 1) * LANES] = merged
            before = now

    for chunk in range(height // 16):
        rows = slice(chunk * 16, chunk * 16 + 16)
        place(lambda b: source_ref[rows, b * LANES : (b + 1) * LANES], height, chunk)
        place(lambda b: mate_source_ref[rows, b * LANES : (b + 1) * LANES], height + toward * height, chunk)

        def from_packed(b):
            part = b * LANES // half_cols
            lane = b * LANES - part * half_cols
            return packed_ref[part * height + chunk * 16 : part * height + chunk * 16 + 16, lane : lane + LANES]

        place(from_packed, height - toward * height, chunk)

    point_rows = packed_ref[packed_ref.shape[0] - 16 :, :].astype(jnp.float32)
    far_rows = far_ref[...].astype(jnp.float32)
    sets = (
        (local_points(own_ref[...], tile, cell_cols, height), tile),
        (local_points(mate_ref[...], mate, cell_cols, height), mate),
        (point_rows[0:4] + point_rows[4:8], partner),
        (point_rows[8:12] + point_rows[12:16], partner_mate),
        (far_rows[0:4] + far_rows[4:8], beyond),
    )
    ext_row = lax.broadcasted_iota(jnp.int32, (ER, 1), 0)
    vertex_y = (fiota((ER, 1), 0) * SP + (SP / 2.0 - SP - height / 2.0)) / height
    ext_tile = tile + jnp.where(ext_row == 0, -1, jnp.where(ext_row == VR + 1, 1, 0))
    scale = float(np.sqrt(EXP2_SCALE))
    lane_px = fiota((1, LANES), 1)
    lane_px = (lax.broadcasted_iota(jnp.int32, (1, LANES), 1) // PC * CELL).astype(jnp.float32) - GROUP_PX / 2.0
    vertex_ids = lax.broadcasted_iota(jnp.int32, (NV, LANES), 0)
    point_block = lax.broadcasted_iota(jnp.int32, (NV, LANES), 1) // (LANES // CELL * PC)
    band = (jnp.abs(vertex_ids // (LANES // SP) - 1 - point_block) <= 1).astype(jnp.float32)
    vertex_scaled = (fiota((NV, 1), 0) * SP + (SP / 2.0 - LANES - GROUP_PX / 2.0)) * (scale / height)
    zero_rows = jnp.zeros((LANES - NV, weight_ref.shape[2]), jnp.bfloat16)

    totals = []
    for g in range(groups):
        weight_ref[g, NV:LANES, :] = zero_rows
        weight_ref[g, LANES + NV :, :] = zero_rows
        for s, (pts, owner) in enumerate(sets):
            usable = (jnp.abs(owner - ext_tile) <= 1) & (owner >= 0) & (owner < strips)
            usable = usable.astype(jnp.float32)
            for c in range(cell_rows):
                lanes = slice(c * cell_cols * PC + g * LANES, c * cell_cols * PC + (g + 1) * LANES)
                chunk = slice((s * cell_rows + c) * LANES, (s * cell_rows + c + 1) * LANES)
                px = (pts[0:1, lanes] + lane_px) / height
                py = (pts[1:2, lanes] + ((owner - tile) * height + c * CELL).astype(jnp.float32)) / height - 0.5
                dx = pts[2:3, lanes] / height
                dy = pts[3:4, lanes] / height
                gap_y = (py - vertex_y) * scale
                wy = jnp.exp2(-(gap_y * gap_y)) * usable
                wpx, wpy, wdx, wdy = wy * px, wy * py, wy * dx, wy * dy
                rows = (wy, wpx, wpy, wdx, wdy, wpx * px, wpx * py, wpy * py, wdx * px, wdx * py, wdy * px, wdy * py)
                for f in range(0, FEATS, 2):
                    high, low = split_pair(jnp.concatenate(rows[f : f + 2], axis=0))
                    feat_ref[g, f * ER : (f + 2) * ER, chunk] = high.astype(jnp.bfloat16)
                    feat_ref[g, NF + f * ER : NF + (f + 2) * ER, chunk] = low.astype(jnp.bfloat16)
                gap_x = px * scale - vertex_scaled
                wx = jnp.exp2(-(gap_x * gap_x)) * band
                high, low = split_pair(wx)
                weight_ref[g, 0:NV, chunk] = high.astype(jnp.bfloat16)
                weight_ref[g, LANES : LANES + NV, chunk] = low.astype(jnp.bfloat16)
        both = lax.dot_general(
            feat_ref[g], weight_ref[g], (((1,), (1,)), ((), ())), preferred_element_type=jnp.float32
        )
        both = both[:NF] + both[NF:]
        totals.append(both[:, :LANES] + both[:, LANES:])

    lane = lax.broadcasted_iota(jnp.int32, (1, LANES), 1)
    per_group = GROUP_PX // SP
    affines = []
    for h in range(halves):
        moments = None
        vertex_group = 2 * h + lane // per_group
        for g in range(groups):
            start = g * per_group - LANES // SP - h * LANES
            if start + NV <= 0 or start >= LANES:
                continue
            part = pltpu.roll(totals[g], start % LANES, axis=1)
            inside = ((lane >= start) & (lane < start + NV)).astype(jnp.float32)
            move = ((g - vertex_group) * (GROUP_PX // height)).astype(jnp.float32)
            part = [part[f * ER : (f + 1) * ER] * inside for f in range(FEATS)]
            part[5] = part[5] + move * (2.0 * part[1] + move * part[0])
            part[6] = part[6] + move * part[2]
            part[8] = part[8] + move * part[3]
            part[10] = part[10] + move * part[4]
            part[1] = part[1] + move * part[0]
            moments = part if moments is None else [x + y for x, y in zip(moments, part)]
        inverse = 1.0 / moments[0]
        mean_px, mean_py, mean_dx, mean_dy = [moments[i] * inverse for i in range(1, 5)]
        cov_xx = moments[5] * inverse - mean_px * mean_px + RIDGE_TERM
        cov_xy = moments[6] * inverse - mean_px * mean_py
        cov_yy = moments[7] * inverse - mean_py * mean_py + RIDGE_TERM
        cross_xx = moments[8] * inverse - mean_dx * mean_px - RIDGE_TERM
        cross_xy = moments[9] * inverse - mean_dx * mean_py
        cross_yx = moments[10] * inverse - mean_dy * mean_px
        cross_yy = moments[11] * inverse - mean_dy * mean_py - RIDGE_TERM
        over = 1.0 / (cov_xx * cov_yy - cov_xy * cov_xy)
        lin_xx = (cross_xx * cov_yy - cross_xy * cov_xy) * over
        lin_xy = (cross_xy * cov_xx - cross_xx * cov_xy) * over
        lin_yx = (cross_yx * cov_yy - cross_yy * cov_xy) * over
        lin_yy = (cross_yy * cov_xx - cross_yx * cov_xy) * over
        vertex_x = ((lane % per_group * SP).astype(jnp.float32) + (SP - GROUP_PX) / 2.0) / height
        delta_x = vertex_x - mean_px
        delta_y = vertex_y - mean_py
        shift_x = mean_dx + lin_xx * delta_x + lin_xy * delta_y
        shift_y = mean_dy + lin_yx * delta_x + lin_yy * delta_y
        results = (lin_xx + 1.0, lin_xy, lin_yx, lin_yy + 1.0, shift_x, shift_y)
        for i, value in enumerate(results):
            affine_ref[i, :, h * LANES : (h + 1) * LANES] = value[1 : VR + 1]
        affines.append((shift_x, shift_y))

    ext = lax.broadcasted_iota(jnp.int32, (ER, LANES), 0)
    along = (lane % SP).astype(jnp.float32) / SP - 0.5
    left_side = along < 0.0
    vertex_rows = []
    for comp in range(2):
        rows = []
        for h in range(halves):
            value = affines[h][comp] * float(height)
            value = jnp.where((ext == 0) & (tile == 0), jnp.broadcast_to(value[1:2], value.shape), value)
            value = jnp.where((ext == VR + 1) & (tile == strips - 1), jnp.broadcast_to(value[VR : VR + 1], value.shape), value)
            rows.append(value)
        steps = []
        for h in range(halves):
            value = rows[h]
            first = jnp.broadcast_to(rows[h - 1][:, LANES - 1 :] if h > 0 else value[:, :1], value.shape)
            last = jnp.broadcast_to(rows[h + 1][:, :1] if h + 1 < halves else value[:, LANES - 1 :], value.shape)
            before = jnp.where(lane == 0, first, pltpu.roll(value, 1, axis=1))
            after = jnp.where(lane == LANES - 1, last, pltpu.roll(value, LANES - 1, axis=1))
            steps.append((value, value - before, after - value))
        vertex_rows.append(steps)

    sub = lax.broadcasted_iota(jnp.int32, (8, LANES), 0).astype(jnp.float32)
    lane_full = fiota((8, LANES), 1)
    tents = (
        jnp.maximum(0.0, 0.5 - sub / SP),
        1.0 - jnp.abs(sub - SP / 2.0) / SP,
        jnp.maximum(0.0, sub / SP - 0.5),
    )
    last_row = 3.0 * height
    spans = None

    def clipped_floor(sample_y):
        return jnp.clip(jnp.floor(sample_y), -2.0, last_row)

    def one_hot(base, k, offset):
        return jnp.where(lane_full - base == float(offset), 1.0, 0.0)

    def tap_rows(bases, offset, slab):
        picks = [
            jnp.concatenate([one_hot(bases[k], k, offset + j) for k in range(len(bases))], axis=0).astype(jnp.bfloat16)
            for j in range(TAPS)
        ]
        return jnp.dot(jnp.concatenate(picks, axis=0), slab, preferred_element_type=jnp.float32)

    def render(sample_x, sample_y, base, taken, k, count, offset):
        floor_x = jnp.floor(sample_x)
        part_x = sample_x - floor_x
        part_y = sample_y - jnp.floor(sample_y)
        floor_x = jnp.clip(floor_x, -2.0, 2.0 * LANES)
        weight_0 = jnp.where((floor_x >= 0.0) & (floor_x < 2.0 * LANES), 1.0 - part_x, 0.0)
        weight_1 = jnp.where((floor_x >= -1.0) & (floor_x < 2.0 * LANES - 1.0), part_x, 0.0)
        index = floor_x.astype(jnp.int32)
        index_0 = index & (LANES - 1)
        index_1 = (index + 1) & (LANES - 1)
        in_0 = floor_x < float(LANES)
        in_1 = floor_x < float(LANES - 1)
        step = clipped_floor(sample_y) - base
        at = [slice((j * count + k) * 8, (j * count + k) * 8 + 8) for j in range(TAPS)]
        near_0 = [jnp.take_along_axis(taken[i, :LANES], index_0, axis=1) for i in at]
        next_0 = [jnp.take_along_axis(taken[i, LANES:], index_0, axis=1) for i in at]
        near_1 = [jnp.take_along_axis(taken[i, :LANES], index_1, axis=1) for i in at]
        next_1 = [jnp.take_along_axis(taken[i, LANES:], index_1, axis=1) for i in at]
        top_0 = top_1 = low_0 = low_1 = jnp.zeros((8, LANES), jnp.float32)
        before = step == float(offset - 1)
        for j in range(TAPS):
            value_0 = jnp.where(in_0, near_0[j], next_0[j])
            value_1 = jnp.where(in_1, near_1[j], next_1[j])
            here = step == float(offset + j)
            top_0 = jnp.where(here, value_0, top_0)
            top_1 = jnp.where(here, value_1, top_1)
            low_0 = jnp.where(before, value_0, low_0)
            low_1 = jnp.where(before, value_1, low_1)
            before = here
        upper = weight_0 * top_0 + weight_1 * top_1
        lower = weight_0 * low_0 + weight_1 * low_1
        return upper + part_y * (lower - upper)

    row_groups = height // 8
    block_spans = []
    for b in range(blocks):
        spread = (b % 8) * (LANES // SP) + lax.broadcasted_iota(jnp.int32, (8, LANES), 1) // SP
        expanded = []
        for comp in range(2):
            value, rise, climb = vertex_rows[comp][b // 8]
            at = jnp.take_along_axis(value, spread, axis=1)
            low = jnp.take_along_axis(rise, spread, axis=1)
            high = jnp.take_along_axis(climb, spread, axis=1)
            expanded.append(at + along * jnp.where(left_side, low, high))
        columns = slice(b * LANES, (b + 1) * LANES)
        span = None
        for k in range(row_groups):
            moved = [
                tents[0] * ex[k : k + 1] + tents[1] * ex[k + 1 : k + 2] + tents[2] * ex[k + 2 : k + 3] for ex in expanded
            ]
            sample_x = lane_full + (moved[0] + LANES / 2.0)
            sample_y = sub + (moved[1] + float(k * 8 + height))
            rows = slice(k * 8, k * 8 + 8)
            sample_ref[0, rows, columns] = sample_x
            sample_ref[1, rows, columns] = sample_y
            floor_y = clipped_floor(sample_y)
            base = jnp.min(floor_y, axis=1, keepdims=True)
            base_ref[b, rows, :] = jnp.broadcast_to(base, (8, LANES))
            span = floor_y - base if span is None else jnp.maximum(span, floor_y - base)
        span_ref[b] = span
        spans = span if spans is None else jnp.maximum(spans, span)

    for b in range(blocks):
        columns = slice(b * LANES, (b + 1) * LANES)
        bases = [base_ref[b, k * 8 : k * 8 + 8, :] for k in range(row_groups)]
        taken = tap_rows(bases, 0, slab_ref[:, b * LANES : (b + 2) * LANES])
        for k in range(row_groups):
            rows = slice(k * 8, k * 8 + 8)
            mixed_ref[rows, columns] = render(
                sample_ref[0, rows, columns], sample_ref[1, rows, columns], bases[k], taken, k, row_groups, 0
            )

    @pl.when(jnp.max(spans) > TAPS - 2.0)
    def _():
        def rest(b, carry):
            widest = jnp.max(span_ref[b])

            @pl.when(widest > TAPS - 2.0)
            def _():
                start = pl.multiple_of(b * LANES, LANES)
                columns = pl.ds(start, LANES)
                bases = [base_ref[b, k * 8 : k * 8 + 8, :] for k in range(row_groups)]

                def more(i, c):
                    moved_bases = [base + (i * TAPS).astype(jnp.float32) for base in bases]
                    taken = tap_rows(moved_bases, 0, slab_ref[:, pl.ds(start, 2 * LANES)])
                    for k in range(row_groups):
                        rows = slice(k * 8, k * 8 + 8)
                        mixed_ref[rows, columns] = mixed_ref[rows, columns] + render(
                            sample_ref[0, rows, columns],
                            sample_ref[1, rows, columns],
                            moved_bases[k],
                            taken,
                            k,
                            row_groups,
                            0,
                        )
                    return c

                lax.fori_loop(1, (widest.astype(jnp.int32) + 1 + TAPS) // TAPS, more, 0)

            return carry

        lax.fori_loop(0, blocks, rest, 0)

    out_ref[...] = mixed_ref[...].astype(jnp.bfloat16)


def per_device(points, source, slab_first, slab_count):
    strips = lax.axis_size("ty")
    height, width = source.shape
    tile_len = points.shape[1]
    blocks = width // LANES
    in_chip = [(i, i ^ 1) for i in range(strips)]
    across = []
    for i in range(1, strips - 1, 2):
        across.extend([(i, i + 1), (i + 1, i)])
    vmem = pl.BlockSpec(memory_space=pltpu.VMEM)
    smem = pl.BlockSpec(memory_space=pltpu.SMEM)
    mate_points = lax.ppermute(points, "ty", in_chip)
    packed_rows = width // tile_len * height + 16
    packed = pl.pallas_call(
        pack_kernel,
        out_shape=jax.ShapeDtypeStruct((packed_rows, tile_len), jnp.bfloat16),
        in_specs=[vmem] * 3,
        out_specs=vmem,
    )(points, mate_points, source)
    arrived = lax.ppermute(packed, "ty", across)
    mate_source = lax.ppermute(source, "ty", in_chip)
    far = lax.ppermute(arrived[packed_rows - 16 : packed_rows - 8], "ty", in_chip)
    groups = width // GROUP_PX
    points_axis = 5 * tile_len // groups
    return pl.pallas_call(
        functools.partial(main_kernel, strips),
        out_shape=(
            jax.ShapeDtypeStruct((height, width), jnp.bfloat16),
            jax.ShapeDtypeStruct((6, VR, width // SP), jnp.float32),
        ),
        in_specs=[smem, smem] + [vmem] * 6,
        out_specs=(vmem, vmem),
        scratch_shapes=[
            pltpu.VMEM((groups, 2 * NF, points_axis), jnp.bfloat16),
            pltpu.VMEM((groups, 2 * LANES, points_axis), jnp.bfloat16),
            pltpu.VMEM((LANES, width + LANES), jnp.bfloat16),
            pltpu.VMEM((2, height, width), jnp.float32),
            pltpu.VMEM((blocks, height, LANES), jnp.float32),
            pltpu.VMEM((blocks, 8, LANES), jnp.float32),
            pltpu.VMEM((height, width), jnp.float32),
        ],
        compiler_params=pltpu.CompilerParams(vmem_limit_bytes=32 * 1024 * 1024),
    )(slab_first, slab_count, points, mate_points, source, mate_source, arrived, far)


def solution(mesh):
    return jax.shard_map(
        per_device,
        mesh=mesh,
        in_specs=(
            P(None, ("sec", "ty")),
            P(("sec", "ty"), None),
            P(("sec", "ty")),
            P(("sec", "ty")),
        ),
        out_specs=(P(("sec", "ty"), None), P(None, ("sec", "ty"), None)),
        check_vma=False,
    )
```

```python
import functools

import jax
import jax.numpy as jnp
import numpy as np
from jax import lax
from jax.experimental import pallas as pl
from jax.experimental.pallas import tpu as pltpu
from jax.sharding import PartitionSpec as P

BH = 16
PC = 4
SP = 8
VR = 4
LANES = 128
CELL = 16
RIDGE_TERM = 0.01
FEATS = 12
ER = 8
NF = FEATS * ER
GROUP_PX = LANES // PC * CELL
NV = GROUP_PX // SP + 2 * LANES // SP
EXP2_SCALE = 2.0 * float(np.log2(np.e))
TAPS = 8


def fiota(shape, dim):
    return lax.broadcasted_iota(jnp.int32, shape, dim).astype(jnp.float32)


def local_points(pts, tile, cell_cols, height):
    lane = lax.broadcasted_iota(jnp.int32, (1, pts.shape[1]), 1)
    cell = lane // PC
    base_x = (cell % cell_cols * CELL).astype(jnp.float32)
    base_y = (tile * height + cell // cell_cols * CELL).astype(jnp.float32)
    fixed_x, fixed_y = pts[0:1], pts[1:2]
    return jnp.concatenate(
        [fixed_x - base_x, fixed_y - base_y, pts[2:3] - fixed_x, pts[3:4] - fixed_y], axis=0
    )


def split_pair(value):
    high = value.astype(jnp.bfloat16).astype(jnp.float32)
    return high, value - high


def pack_kernel(own_ref, mate_ref, source_ref, packed_ref):
    height, width = source_ref.shape
    half = packed_ref.shape[1]
    tile = lax.axis_index("ty")
    for part in range(width // half):
        packed_ref[part * height : (part + 1) * height, :] = source_ref[:, part * half : (part + 1) * half]
    rows = []
    for ref, owner in ((own_ref, tile), (mate_ref, tile + 1 - 2 * (tile % 2))):
        rows.extend(split_pair(local_points(ref[...], owner, width // CELL, height)))
    base = width // half * height
    packed_ref[base : base + 16, :] = jnp.concatenate(rows, axis=0).astype(jnp.bfloat16)


def main_kernel(
    strips,
    first_ref,
    count_ref,
    own_ref,
    mate_ref,
    source_ref,
    mate_source_ref,
    packed_ref,
    far_ref,
    out_ref,
    affine_ref,
    feat_ref,
    weight_ref,
    slab_ref,
    sample_ref,
    base_ref,
    span_ref,
    taken_ref,
    mixed_ref,
    widest_ref,
):
    height, width = source_ref.shape
    tile_len = own_ref.shape[1]
    cell_cols = width // CELL
    cell_rows = height // CELL
    groups = width // GROUP_PX
    blocks = width // LANES
    halves = blocks // 8
    tile = lax.axis_index("ty")
    odd = tile % 2
    toward = 1 - 2 * odd
    mate = tile + toward
    partner = tile - toward
    partner_mate = tile - 2 * toward
    beyond = tile + 2 * toward

    slots_from = first_ref[0] * BH - (tile - 1) * height
    slots_to = slots_from + count_ref[0] * BH
    left_half = lax.broadcasted_iota(jnp.int32, (1, LANES), 1) < LANES // 2
    half_cols = packed_ref.shape[1]
    slab_ref[3 * height :, :] = jnp.zeros((slab_ref.shape[0] - 3 * height, slab_ref.shape[1]), jnp.bfloat16)

    def place(load, row_start, chunk):
        local = row_start + chunk * 16
        row = lax.broadcasted_iota(jnp.int32, (16, 1), 0) + local
        live = ((row >= slots_from) & (row < slots_to)).astype(jnp.float32)
        before = jnp.zeros((16, LANES), jnp.float32)
        for b in range(blocks + 1):
            if b < blocks:
                now = pltpu.roll(load(b).astype(jnp.float32) * live, LANES // 2, axis=1)
            else:
                now = jnp.zeros((16, LANES), jnp.float32)
            merged = jnp.where(left_half, before, now).astype(jnp.bfloat16)
            slab_ref[pl.ds(pl.multiple_of(local, 16), 16), b * LANES : (b + 1) * LANES] = merged
            before = now

    for chunk in range(height // 16):
        rows = slice(chunk * 16, chunk * 16 + 16)
        place(lambda b: source_ref[rows, b * LANES : (b + 1) * LANES], height, chunk)
        place(lambda b: mate_source_ref[rows, b * LANES : (b + 1) * LANES], height + toward * height, chunk)

        def from_packed(b):
            part = b * LANES // half_cols
            lane = b * LANES - part * half_cols
            return packed_ref[part * height + chunk * 16 : part * height + chunk * 16 + 16, lane : lane + LANES]

        place(from_packed, height - toward * height, chunk)

    point_rows = packed_ref[packed_ref.shape[0] - 16 :, :].astype(jnp.float32)
    far_rows = far_ref[...].astype(jnp.float32)
    sets = (
        (local_points(own_ref[...], tile, cell_cols, height), tile),
        (local_points(mate_ref[...], mate, cell_cols, height), mate),
        (point_rows[0:4] + point_rows[4:8], partner),
        (point_rows[8:12] + point_rows[12:16], partner_mate),
        (far_rows[0:4] + far_rows[4:8], beyond),
    )
    ext_row = lax.broadcasted_iota(jnp.int32, (ER, 1), 0)
    vertex_y = (fiota((ER, 1), 0) * SP + (SP / 2.0 - SP - height / 2.0)) / height
    ext_tile = tile + jnp.where(ext_row == 0, -1, jnp.where(ext_row == VR + 1, 1, 0))
    scale = float(np.sqrt(EXP2_SCALE))
    lane_px = fiota((1, LANES), 1)
    lane_px = (lax.broadcasted_iota(jnp.int32, (1, LANES), 1) // PC * CELL).astype(jnp.float32) - GROUP_PX / 2.0
    vertex_ids = lax.broadcasted_iota(jnp.int32, (NV, LANES), 0)
    point_block = lax.broadcasted_iota(jnp.int32, (NV, LANES), 1) // (LANES // CELL * PC)
    band = (jnp.abs(vertex_ids // (LANES // SP) - 1 - point_block) <= 1).astype(jnp.float32)
    vertex_scaled = (fiota((NV, 1), 0) * SP + (SP / 2.0 - LANES - GROUP_PX / 2.0)) * (scale / height)
    zero_rows = jnp.zeros((LANES - NV, weight_ref.shape[2]), jnp.bfloat16)

    totals = []
    for g in range(groups):
        weight_ref[g, NV:LANES, :] = zero_rows
        weight_ref[g, LANES + NV :, :] = zero_rows
        for s, (pts, owner) in enumerate(sets):
            usable = (jnp.abs(owner - ext_tile) <= 1) & (owner >= 0) & (owner < strips)
            usable = usable.astype(jnp.float32)
            for c in range(cell_rows):
                lanes = slice(c * cell_cols * PC + g * LANES, c * cell_cols * PC + (g + 1) * LANES)
                chunk = slice((s * cell_rows + c) * LANES, (s * cell_rows + c + 1) * LANES)
                px = (pts[0:1, lanes] + lane_px) / height
                py = (pts[1:2, lanes] + ((owner - tile) * height + c * CELL).astype(jnp.float32)) / height - 0.5
                dx = pts[2:3, lanes] / height
                dy = pts[3:4, lanes] / height
                gap_y = (py - vertex_y) * scale
                wy = jnp.exp2(-(gap_y * gap_y)) * usable
                wpx, wpy, wdx, wdy = wy * px, wy * py, wy * dx, wy * dy
                rows = (wy, wpx, wpy, wdx, wdy, wpx * px, wpx * py, wpy * py, wdx * px, wdx * py, wdy * px, wdy * py)
                for f in range(0, FEATS, 2):
                    high, low = split_pair(jnp.concatenate(rows[f : f + 2], axis=0))
                    feat_ref[g, f * ER : (f + 2) * ER, chunk] = high.astype(jnp.bfloat16)
                    feat_ref[g, NF + f * ER : NF + (f + 2) * ER, chunk] = low.astype(jnp.bfloat16)
                gap_x = px * scale - vertex_scaled
                wx = jnp.exp2(-(gap_x * gap_x)) * band
                high, low = split_pair(wx)
                weight_ref[g, 0:NV, chunk] = high.astype(jnp.bfloat16)
                weight_ref[g, LANES : LANES + NV, chunk] = low.astype(jnp.bfloat16)
        both = lax.dot_general(
            feat_ref[g], weight_ref[g], (((1,), (1,)), ((), ())), preferred_element_type=jnp.float32
        )
        both = both[:NF] + both[NF:]
        totals.append(both[:, :LANES] + both[:, LANES:])

    lane = lax.broadcasted_iota(jnp.int32, (1, LANES), 1)
    per_group = GROUP_PX // SP
    affines = []
    for h in range(halves):
        moments = None
        vertex_group = 2 * h + lane // per_group
        for g in range(groups):
            start = g * per_group - LANES // SP - h * LANES
            if start + NV <= 0 or start >= LANES:
                continue
            part = pltpu.roll(totals[g], start % LANES, axis=1)
            inside = ((lane >= start) & (lane < start + NV)).astype(jnp.float32)
            move = ((g - vertex_group) * (GROUP_PX // height)).astype(jnp.float32)
            part = [part[f * ER : (f + 1) * ER] * inside for f in range(FEATS)]
            part[5] = part[5] + move * (2.0 * part[1] + move * part[0])
            part[6] = part[6] + move * part[2]
            part[8] = part[8] + move * part[3]
            part[10] = part[10] + move * part[4]
            part[1] = part[1] + move * part[0]
            moments = part if moments is None else [x + y for x, y in zip(moments, part)]
        inverse = 1.0 / moments[0]
        mean_px, mean_py, mean_dx, mean_dy = [moments[i] * inverse for i in range(1, 5)]
        cov_xx = moments[5] * inverse - mean_px * mean_px + RIDGE_TERM
        cov_xy = moments[6] * inverse - mean_px * mean_py
        cov_yy = moments[7] * inverse - mean_py * mean_py + RIDGE_TERM
        cross_xx = moments[8] * inverse - mean_dx * mean_px - RIDGE_TERM
        cross_xy = moments[9] * inverse - mean_dx * mean_py
        cross_yx = moments[10] * inverse - mean_dy * mean_px
        cross_yy = moments[11] * inverse - mean_dy * mean_py - RIDGE_TERM
        over = 1.0 / (cov_xx * cov_yy - cov_xy * cov_xy)
        lin_xx = (cross_xx * cov_yy - cross_xy * cov_xy) * over
        lin_xy = (cross_xy * cov_xx - cross_xx * cov_xy) * over
        lin_yx = (cross_yx * cov_yy - cross_yy * cov_xy) * over
        lin_yy = (cross_yy * cov_xx - cross_yx * cov_xy) * over
        vertex_x = ((lane % per_group * SP).astype(jnp.float32) + (SP - GROUP_PX) / 2.0) / height
        delta_x = vertex_x - mean_px
        delta_y = vertex_y - mean_py
        shift_x = mean_dx + lin_xx * delta_x + lin_xy * delta_y
        shift_y = mean_dy + lin_yx * delta_x + lin_yy * delta_y
        results = (lin_xx + 1.0, lin_xy, lin_yx, lin_yy + 1.0, shift_x, shift_y)
        for i, value in enumerate(results):
            affine_ref[i, :, h * LANES : (h + 1) * LANES] = value[1 : VR + 1]
        affines.append((shift_x, shift_y))

    ext = lax.broadcasted_iota(jnp.int32, (ER, LANES), 0)
    along = (lane % SP).astype(jnp.float32) / SP - 0.5
    left_side = along < 0.0
    vertex_rows = []
    for comp in range(2):
        rows = []
        for h in range(halves):
            value = affines[h][comp] * float(height)
            value = jnp.where((ext == 0) & (tile == 0), jnp.broadcast_to(value[1:2], value.shape), value)
            value = jnp.where((ext == VR + 1) & (tile == strips - 1), jnp.broadcast_to(value[VR : VR + 1], value.shape), value)
            rows.append(value)
        steps = []
        for h in range(halves):
            value = rows[h]
            first = jnp.broadcast_to(rows[h - 1][:, LANES - 1 :] if h > 0 else value[:, :1], value.shape)
            last = jnp.broadcast_to(rows[h + 1][:, :1] if h + 1 < halves else value[:, LANES - 1 :], value.shape)
            before = jnp.where(lane == 0, first, pltpu.roll(value, 1, axis=1))
            after = jnp.where(lane == LANES - 1, last, pltpu.roll(value, LANES - 1, axis=1))
            steps.append((value, value - before, after - value))
        vertex_rows.append(steps)

    sub = lax.broadcasted_iota(jnp.int32, (8, LANES), 0).astype(jnp.float32)
    lane_full = fiota((8, LANES), 1)
    tents = (
        jnp.maximum(0.0, 0.5 - sub / SP),
        1.0 - jnp.abs(sub - SP / 2.0) / SP,
        jnp.maximum(0.0, sub / SP - 0.5),
    )
    last_row = 3.0 * height
    spans = None

    def clipped_floor(sample_y):
        return jnp.clip(jnp.floor(sample_y), -2.0, last_row)

    def one_hot(base, k, offset):
        return jnp.where(lane_full - base == float(offset), 1.0, 0.0)

    def tap_rows(bases, offset, slab):
        picks = [
            jnp.concatenate([one_hot(bases[k], k, offset + j) for k in range(len(bases))], axis=0).astype(jnp.bfloat16)
            for j in range(TAPS)
        ]
        return jnp.dot(jnp.concatenate(picks, axis=0), slab, preferred_element_type=jnp.float32)

    def render(sample_x, sample_y, base, taken, k, count, offset):
        floor_x = jnp.floor(sample_x)
        part_x = sample_x - floor_x
        part_y = sample_y - jnp.floor(sample_y)
        floor_x = jnp.clip(floor_x, -2.0, 2.0 * LANES)
        weight_0 = jnp.where((floor_x >= 0.0) & (floor_x < 2.0 * LANES), 1.0 - part_x, 0.0)
        weight_1 = jnp.where((floor_x >= -1.0) & (floor_x < 2.0 * LANES - 1.0), part_x, 0.0)
        index = floor_x.astype(jnp.int32)
        index_0 = index & (LANES - 1)
        index_1 = (index + 1) & (LANES - 1)
        in_0 = floor_x < float(LANES)
        in_1 = floor_x < float(LANES - 1)
        step = clipped_floor(sample_y) - base
        near, after = taken
        at = [slice((j * count + k) * 8, (j * count + k) * 8 + 8) for j in range(TAPS)]
        near_0 = [jnp.take_along_axis(near(i), index_0, axis=1) for i in at]
        next_0 = [jnp.take_along_axis(after(i), index_0, axis=1) for i in at]
        near_1 = [jnp.take_along_axis(near(i), index_1, axis=1) for i in at]
        next_1 = [jnp.take_along_axis(after(i), index_1, axis=1) for i in at]
        top_0 = top_1 = low_0 = low_1 = jnp.zeros((8, LANES), jnp.float32)
        before = step == float(offset - 1)
        for j in range(TAPS):
            value_0 = jnp.where(in_0, near_0[j], next_0[j])
            value_1 = jnp.where(in_1, near_1[j], next_1[j])
            here = step == float(offset + j)
            top_0 = jnp.where(here, value_0, top_0)
            top_1 = jnp.where(here, value_1, top_1)
            low_0 = jnp.where(before, value_0, low_0)
            low_1 = jnp.where(before, value_1, low_1)
            before = here
        upper = weight_0 * top_0 + weight_1 * top_1
        lower = weight_0 * low_0 + weight_1 * low_1
        return upper + part_y * (lower - upper)

    row_groups = height // 8
    block_spans = []
    for b in range(blocks):
        spread = (b % 8) * (LANES // SP) + lax.broadcasted_iota(jnp.int32, (8, LANES), 1) // SP
        expanded = []
        for comp in range(2):
            value, rise, climb = vertex_rows[comp][b // 8]
            at = jnp.take_along_axis(value, spread, axis=1)
            low = jnp.take_along_axis(rise, spread, axis=1)
            high = jnp.take_along_axis(climb, spread, axis=1)
            expanded.append(at + along * jnp.where(left_side, low, high))
        columns = slice(b * LANES, (b + 1) * LANES)
        span = None
        for k in range(row_groups):
            moved = [
                tents[0] * ex[k : k + 1] + tents[1] * ex[k + 1 : k + 2] + tents[2] * ex[k + 2 : k + 3] for ex in expanded
            ]
            sample_x = lane_full + (moved[0] + LANES / 2.0)
            sample_y = sub + (moved[1] + float(k * 8 + height))
            rows = slice(k * 8, k * 8 + 8)
            sample_ref[0, rows, columns] = sample_x
            sample_ref[1, rows, columns] = sample_y
            floor_y = clipped_floor(sample_y)
            base = jnp.min(floor_y, axis=1, keepdims=True)
            base_ref[b, rows, :] = jnp.broadcast_to(base, (8, LANES))
            span = floor_y - base if span is None else jnp.maximum(span, floor_y - base)
        span_ref[b] = span
        spans = span if spans is None else jnp.maximum(spans, span)

    for b in range(blocks):
        columns = slice(b * LANES, (b + 1) * LANES)
        bases = [base_ref[b, k * 8 : k * 8 + 8, :] for k in range(row_groups)]
        taken_ref[b] = tap_rows(bases, 0, slab_ref[:, b * LANES : (b + 2) * LANES])

    for b in range(blocks):
        columns = slice(b * LANES, (b + 1) * LANES)
        bases = [base_ref[b, k * 8 : k * 8 + 8, :] for k in range(row_groups)]
        taken = (lambda i: taken_ref[b, i, :LANES]), (lambda i: taken_ref[b, i, LANES:])
        for k in range(row_groups):
            rows = slice(k * 8, k * 8 + 8)
            mixed_ref[rows, columns] = render(
                sample_ref[0, rows, columns], sample_ref[1, rows, columns], bases[k], taken, k, row_groups, 0
            )

    @pl.when(jnp.max(spans) > TAPS - 2.0)
    def _():
        for b in range(blocks):
            widest_ref[b] = jnp.max(span_ref[b]).astype(jnp.int32)

        def rest(b, carry):
            widest = widest_ref[b]

            @pl.when(widest > TAPS - 2)
            def _():
                start = pl.multiple_of(b * LANES, LANES)
                columns = pl.ds(start, LANES)
                bases = [base_ref[b, k * 8 : k * 8 + 8, :] for k in range(row_groups)]

                def more(i, c):
                    moved_bases = [base + (i * TAPS).astype(jnp.float32) for base in bases]
                    rows_taken = tap_rows(moved_bases, 0, slab_ref[:, pl.ds(start, 2 * LANES)])
                    taken = (lambda i: rows_taken[i, :LANES]), (lambda i: rows_taken[i, LANES:])
                    for k in range(row_groups):
                        rows = slice(k * 8, k * 8 + 8)
                        mixed_ref[rows, columns] = mixed_ref[rows, columns] + render(
                            sample_ref[0, rows, columns],
                            sample_ref[1, rows, columns],
                            moved_bases[k],
                            taken,
                            k,
                            row_groups,
                            0,
                        )
                    return c

                lax.fori_loop(1, (widest + 1 + TAPS) // TAPS, more, 0)

            return carry

        lax.fori_loop(0, blocks, rest, 0)

    out_ref[...] = mixed_ref[...].astype(jnp.bfloat16)


def per_device(points, source, slab_first, slab_count):
    strips = lax.axis_size("ty")
    height, width = source.shape
    tile_len = points.shape[1]
    blocks = width // LANES
    in_chip = [(i, i ^ 1) for i in range(strips)]
    across = []
    for i in range(1, strips - 1, 2):
        across.extend([(i, i + 1), (i + 1, i)])
    vmem = pl.BlockSpec(memory_space=pltpu.VMEM)
    smem = pl.BlockSpec(memory_space=pltpu.SMEM)
    mate_points = lax.ppermute(points, "ty", in_chip)
    packed_rows = width // tile_len * height + 16
    packed = pl.pallas_call(
        pack_kernel,
        out_shape=jax.ShapeDtypeStruct((packed_rows, tile_len), jnp.bfloat16),
        in_specs=[vmem] * 3,
        out_specs=vmem,
    )(points, mate_points, source)
    arrived = lax.ppermute(packed, "ty", across)
    mate_source = lax.ppermute(source, "ty", in_chip)
    far = lax.ppermute(arrived[packed_rows - 16 : packed_rows - 8], "ty", in_chip)
    groups = width // GROUP_PX
    points_axis = 5 * tile_len // groups
    return pl.pallas_call(
        functools.partial(main_kernel, strips),
        out_shape=(
            jax.ShapeDtypeStruct((height, width), jnp.bfloat16),
            jax.ShapeDtypeStruct((6, VR, width // SP), jnp.float32),
        ),
        in_specs=[smem, smem] + [vmem] * 6,
        out_specs=(vmem, vmem),
        scratch_shapes=[
            pltpu.VMEM((groups, 2 * NF, points_axis), jnp.bfloat16),
            pltpu.VMEM((groups, 2 * LANES, points_axis), jnp.bfloat16),
            pltpu.VMEM((LANES, width + LANES), jnp.bfloat16),
            pltpu.VMEM((2, height, width), jnp.float32),
            pltpu.VMEM((blocks, height, LANES), jnp.float32),
            pltpu.VMEM((blocks, 8, LANES), jnp.float32),
            pltpu.VMEM((blocks, TAPS * height, 2 * LANES), jnp.float32),
            pltpu.VMEM((height, width), jnp.float32),
            pltpu.SMEM((blocks,), jnp.int32),
        ],
        compiler_params=pltpu.CompilerParams(vmem_limit_bytes=32 * 1024 * 1024),
    )(slab_first, slab_count, points, mate_points, source, mate_source, arrived, far)


def solution(mesh):
    return jax.shard_map(
        per_device,
        mesh=mesh,
        in_specs=(
            P(None, ("sec", "ty")),
            P(("sec", "ty"), None),
            P(("sec", "ty")),
            P(("sec", "ty")),
        ),
        out_specs=(P(("sec", "ty"), None), P(None, ("sec", "ty"), None)),
        check_vma=False,
    )
```

```python
import functools

import jax
import jax.numpy as jnp
import numpy as np
from jax import lax
from jax.experimental import pallas as pl
from jax.experimental.pallas import tpu as pltpu
from jax.sharding import PartitionSpec as P

BH = 16
PC = 4
SP = 8
VR = 4
LANES = 128
CELL = 16
RIDGE_TERM = 0.01
FEATS = 12
ER = 8
NF = FEATS * ER
GROUP_PX = LANES // PC * CELL
NV = GROUP_PX // SP + 2 * LANES // SP
EXP2_SCALE = 2.0 * float(np.log2(np.e))
TAPS = 8


def fiota(shape, dim):
    return lax.broadcasted_iota(jnp.int32, shape, dim).astype(jnp.float32)


def local_points(pts, tile, cell_cols, height):
    lane = lax.broadcasted_iota(jnp.int32, (1, pts.shape[1]), 1)
    cell = lane // PC
    base_x = (cell % cell_cols * CELL).astype(jnp.float32)
    base_y = (tile * height + cell // cell_cols * CELL).astype(jnp.float32)
    fixed_x, fixed_y = pts[0:1], pts[1:2]
    return jnp.concatenate(
        [fixed_x - base_x, fixed_y - base_y, pts[2:3] - fixed_x, pts[3:4] - fixed_y], axis=0
    )


def split_pair(value):
    high = value.astype(jnp.bfloat16).astype(jnp.float32)
    return high, value - high


def lay_source_kernel(source_ref, packed_ref):
    height, width = source_ref.shape
    half = packed_ref.shape[1]
    for part in range(width // half):
        packed_ref[part * height : (part + 1) * height, :] = source_ref[:, part * half : (part + 1) * half]


def lay_points_kernel(height, width, own_ref, mate_ref, laid_ref, packed_ref, rows_ref, sem):
    tile = lax.axis_index("ty")
    rows = []
    for ref, owner in ((own_ref, tile), (mate_ref, tile + 1 - 2 * (tile % 2))):
        rows.extend(split_pair(local_points(ref[...], owner, width // CELL, height)))
    rows_ref[...] = jnp.concatenate(rows, axis=0).astype(jnp.bfloat16)
    base = packed_ref.shape[0] - 16
    copy = pltpu.make_async_copy(rows_ref, packed_ref.at[base : base + 16, :], sem)
    copy.start()
    copy.wait()


def group_totals(sets, tile, strips, height, width, feat_ref, weight_ref):
    cell_cols = width // CELL
    cell_rows = height // CELL
    groups = width // GROUP_PX
    ext_row = lax.broadcasted_iota(jnp.int32, (ER, 1), 0)
    vertex_y = (fiota((ER, 1), 0) * SP + (SP / 2.0 - SP - height / 2.0)) / height
    ext_tile = tile + jnp.where(ext_row == 0, -1, jnp.where(ext_row == VR + 1, 1, 0))
    scale = float(np.sqrt(EXP2_SCALE))
    lane_px = (lax.broadcasted_iota(jnp.int32, (1, LANES), 1) // PC * CELL).astype(jnp.float32) - GROUP_PX / 2.0
    vertex_ids = lax.broadcasted_iota(jnp.int32, (NV, LANES), 0)
    point_block = lax.broadcasted_iota(jnp.int32, (NV, LANES), 1) // (LANES // CELL * PC)
    band = (jnp.abs(vertex_ids // (LANES // SP) - 1 - point_block) <= 1).astype(jnp.float32)
    vertex_scaled = (fiota((NV, 1), 0) * SP + (SP / 2.0 - LANES - GROUP_PX / 2.0)) * (scale / height)
    zero_rows = jnp.zeros((LANES - NV, weight_ref.shape[2]), jnp.bfloat16)

    totals = []
    for g in range(groups):
        weight_ref[g, NV:LANES, :] = zero_rows
        weight_ref[g, LANES + NV :, :] = zero_rows
        for s, (pts, owner) in enumerate(sets):
            usable = (jnp.abs(owner - ext_tile) <= 1) & (owner >= 0) & (owner < strips)
            usable = usable.astype(jnp.float32)
            for c in range(cell_rows):
                lanes = slice(c * cell_cols * PC + g * LANES, c * cell_cols * PC + (g + 1) * LANES)
                chunk = slice((s * cell_rows + c) * LANES, (s * cell_rows + c + 1) * LANES)
                px = (pts[0:1, lanes] + lane_px) / height
                py = (pts[1:2, lanes] + ((owner - tile) * height + c * CELL).astype(jnp.float32)) / height - 0.5
                dx = pts[2:3, lanes] / height
                dy = pts[3:4, lanes] / height
                gap_y = (py - vertex_y) * scale
                wy = jnp.exp2(-(gap_y * gap_y)) * usable
                wpx, wpy, wdx, wdy = wy * px, wy * py, wy * dx, wy * dy
                rows = (wy, wpx, wpy, wdx, wdy, wpx * px, wpx * py, wpy * py, wdx * px, wdx * py, wdy * px, wdy * py)
                for f in range(0, FEATS, 2):
                    high, low = split_pair(jnp.concatenate(rows[f : f + 2], axis=0))
                    feat_ref[g, f * ER : (f + 2) * ER, chunk] = high.astype(jnp.bfloat16)
                    feat_ref[g, NF + f * ER : NF + (f + 2) * ER, chunk] = low.astype(jnp.bfloat16)
                gap_x = px * scale - vertex_scaled
                wx = jnp.exp2(-(gap_x * gap_x)) * band
                high, low = split_pair(wx)
                weight_ref[g, 0:NV, chunk] = high.astype(jnp.bfloat16)
                weight_ref[g, LANES : LANES + NV, chunk] = low.astype(jnp.bfloat16)
        both = lax.dot_general(
            feat_ref[g], weight_ref[g], (((1,), (1,)), ((), ())), preferred_element_type=jnp.float32
        )
        both = both[:NF] + both[NF:]
        totals.append(both[:, :LANES] + both[:, LANES:])
    return totals


def near_kernel(strips, height, width, own_ref, mate_ref, totals_ref, feat_ref, weight_ref):
    tile = lax.axis_index("ty")
    mate = tile + 1 - 2 * (tile % 2)
    cell_cols = width // CELL
    sets = (
        (local_points(own_ref[...], tile, cell_cols, height), tile),
        (local_points(mate_ref[...], mate, cell_cols, height), mate),
    )
    for g, value in enumerate(group_totals(sets, tile, strips, height, width, feat_ref, weight_ref)):
        totals_ref[g] = value


def main_kernel(
    strips,
    first_ref,
    count_ref,
    totals_ref,
    source_ref,
    mate_source_ref,
    packed_ref,
    far_ref,
    out_ref,
    affine_ref,
    feat_ref,
    weight_ref,
    slab_ref,
    sample_ref,
    base_ref,
    span_ref,
    taken_ref,
    mixed_ref,
    widest_ref,
):
    height, width = source_ref.shape
    groups = width // GROUP_PX
    blocks = width // LANES
    halves = blocks // 8
    tile = lax.axis_index("ty")
    odd = tile % 2
    toward = 1 - 2 * odd
    partner = tile - toward
    partner_mate = tile - 2 * toward
    beyond = tile + 2 * toward

    slots_from = first_ref[0] * BH - (tile - 1) * height
    slots_to = slots_from + count_ref[0] * BH
    left_half = lax.broadcasted_iota(jnp.int32, (1, LANES), 1) < LANES // 2
    half_cols = packed_ref.shape[1]
    slab_ref[3 * height :, :] = jnp.zeros((slab_ref.shape[0] - 3 * height, slab_ref.shape[1]), jnp.bfloat16)

    def place(load, row_start, chunk):
        local = row_start + chunk * 16
        row = lax.broadcasted_iota(jnp.int32, (16, 1), 0) + local
        live = ((row >= slots_from) & (row < slots_to)).astype(jnp.float32)
        before = jnp.zeros((16, LANES), jnp.float32)
        for b in range(blocks + 1):
            if b < blocks:
                now = pltpu.roll(load(b).astype(jnp.float32) * live, LANES // 2, axis=1)
            else:
                now = jnp.zeros((16, LANES), jnp.float32)
            merged = jnp.where(left_half, before, now).astype(jnp.bfloat16)
            slab_ref[pl.ds(pl.multiple_of(local, 16), 16), b * LANES : (b + 1) * LANES] = merged
            before = now

    for chunk in range(height // 16):
        rows = slice(chunk * 16, chunk * 16 + 16)
        place(lambda b: source_ref[rows, b * LANES : (b + 1) * LANES], height, chunk)
        place(lambda b: mate_source_ref[rows, b * LANES : (b + 1) * LANES], height + toward * height, chunk)

        def from_packed(b):
            part = b * LANES // half_cols
            lane = b * LANES - part * half_cols
            return packed_ref[part * height + chunk * 16 : part * height + chunk * 16 + 16, lane : lane + LANES]

        place(from_packed, height - toward * height, chunk)

    point_rows = packed_ref[packed_ref.shape[0] - 16 :, :].astype(jnp.float32)
    far_rows = far_ref[...].astype(jnp.float32)
    sets = (
        (point_rows[0:4] + point_rows[4:8], partner),
        (point_rows[8:12] + point_rows[12:16], partner_mate),
        (far_rows[0:4] + far_rows[4:8], beyond),
    )
    vertex_y = (fiota((ER, 1), 0) * SP + (SP / 2.0 - SP - height / 2.0)) / height
    totals = group_totals(sets, tile, strips, height, width, feat_ref, weight_ref)
    totals = [totals[g] + totals_ref[g] for g in range(groups)]

    lane = lax.broadcasted_iota(jnp.int32, (1, LANES), 1)
    per_group = GROUP_PX // SP
    affines = []
    for h in range(halves):
        moments = None
        vertex_group = 2 * h + lane // per_group
        for g in range(groups):
            start = g * per_group - LANES // SP - h * LANES
            if start + NV <= 0 or start >= LANES:
                continue
            part = pltpu.roll(totals[g], start % LANES, axis=1)
            inside = ((lane >= start) & (lane < start + NV)).astype(jnp.float32)
            move = ((g - vertex_group) * (GROUP_PX // height)).astype(jnp.float32)
            part = [part[f * ER : (f + 1) * ER] * inside for f in range(FEATS)]
            part[5] = part[5] + move * (2.0 * part[1] + move * part[0])
            part[6] = part[6] + move * part[2]
            part[8] = part[8] + move * part[3]
            part[10] = part[10] + move * part[4]
            part[1] = part[1] + move * part[0]
            moments = part if moments is None else [x + y for x, y in zip(moments, part)]
        inverse = 1.0 / moments[0]
        mean_px, mean_py, mean_dx, mean_dy = [moments[i] * inverse for i in range(1, 5)]
        cov_xx = moments[5] * inverse - mean_px * mean_px + RIDGE_TERM
        cov_xy = moments[6] * inverse - mean_px * mean_py
        cov_yy = moments[7] * inverse - mean_py * mean_py + RIDGE_TERM
        cross_xx = moments[8] * inverse - mean_dx * mean_px - RIDGE_TERM
        cross_xy = moments[9] * inverse - mean_dx * mean_py
        cross_yx = moments[10] * inverse - mean_dy * mean_px
        cross_yy = moments[11] * inverse - mean_dy * mean_py - RIDGE_TERM
        over = 1.0 / (cov_xx * cov_yy - cov_xy * cov_xy)
        lin_xx = (cross_xx * cov_yy - cross_xy * cov_xy) * over
        lin_xy = (cross_xy * cov_xx - cross_xx * cov_xy) * over
        lin_yx = (cross_yx * cov_yy - cross_yy * cov_xy) * over
        lin_yy = (cross_yy * cov_xx - cross_yx * cov_xy) * over
        vertex_x = ((lane % per_group * SP).astype(jnp.float32) + (SP - GROUP_PX) / 2.0) / height
        delta_x = vertex_x - mean_px
        delta_y = vertex_y - mean_py
        shift_x = mean_dx + lin_xx * delta_x + lin_xy * delta_y
        shift_y = mean_dy + lin_yx * delta_x + lin_yy * delta_y
        results = (lin_xx + 1.0, lin_xy, lin_yx, lin_yy + 1.0, shift_x, shift_y)
        for i, value in enumerate(results):
            affine_ref[i, :, h * LANES : (h + 1) * LANES] = value[1 : VR + 1]
        affines.append((shift_x, shift_y))

    ext = lax.broadcasted_iota(jnp.int32, (ER, LANES), 0)
    along = (lane % SP).astype(jnp.float32) / SP - 0.5
    left_side = along < 0.0
    vertex_rows = []
    for comp in range(2):
        rows = []
        for h in range(halves):
            value = affines[h][comp] * float(height)
            value = jnp.where((ext == 0) & (tile == 0), jnp.broadcast_to(value[1:2], value.shape), value)
            value = jnp.where((ext == VR + 1) & (tile == strips - 1), jnp.broadcast_to(value[VR : VR + 1], value.shape), value)
            rows.append(value)
        steps = []
        for h in range(halves):
            value = rows[h]
            first = jnp.broadcast_to(rows[h - 1][:, LANES - 1 :] if h > 0 else value[:, :1], value.shape)
            last = jnp.broadcast_to(rows[h + 1][:, :1] if h + 1 < halves else value[:, LANES - 1 :], value.shape)
            before = jnp.where(lane == 0, first, pltpu.roll(value, 1, axis=1))
            after = jnp.where(lane == LANES - 1, last, pltpu.roll(value, LANES - 1, axis=1))
            steps.append((value, value - before, after - value))
        vertex_rows.append(steps)

    sub = lax.broadcasted_iota(jnp.int32, (8, LANES), 0).astype(jnp.float32)
    lane_full = fiota((8, LANES), 1)
    tents = (
        jnp.maximum(0.0, 0.5 - sub / SP),
        1.0 - jnp.abs(sub - SP / 2.0) / SP,
        jnp.maximum(0.0, sub / SP - 0.5),
    )
    last_row = 3.0 * height
    spans = None

    def clipped_floor(sample_y):
        return jnp.clip(jnp.floor(sample_y), -2.0, last_row)

    def one_hot(base, k, offset):
        return jnp.where(lane_full - base == float(offset), 1.0, 0.0)

    def tap_rows(bases, offset, slab):
        picks = [
            jnp.concatenate([one_hot(bases[k], k, offset + j) for k in range(len(bases))], axis=0).astype(jnp.bfloat16)
            for j in range(TAPS)
        ]
        return jnp.dot(jnp.concatenate(picks, axis=0), slab, preferred_element_type=jnp.float32)

    def render(sample_x, sample_y, base, taken, k, count, offset):
        floor_x = jnp.floor(sample_x)
        part_x = sample_x - floor_x
        part_y = sample_y - jnp.floor(sample_y)
        floor_x = jnp.clip(floor_x, -2.0, 2.0 * LANES)
        weight_0 = jnp.where((floor_x >= 0.0) & (floor_x < 2.0 * LANES), 1.0 - part_x, 0.0)
        weight_1 = jnp.where((floor_x >= -1.0) & (floor_x < 2.0 * LANES - 1.0), part_x, 0.0)
        index = floor_x.astype(jnp.int32)
        index_0 = index & (LANES - 1)
        index_1 = (index + 1) & (LANES - 1)
        in_0 = floor_x < float(LANES)
        in_1 = floor_x < float(LANES - 1)
        step = clipped_floor(sample_y) - base
        near, after = taken
        at = [slice((j * count + k) * 8, (j * count + k) * 8 + 8) for j in range(TAPS)]
        near_0 = [jnp.take_along_axis(near(i), index_0, axis=1) for i in at]
        next_0 = [jnp.take_along_axis(after(i), index_0, axis=1) for i in at]
        near_1 = [jnp.take_along_axis(near(i), index_1, axis=1) for i in at]
        next_1 = [jnp.take_along_axis(after(i), index_1, axis=1) for i in at]
        top_0 = top_1 = low_0 = low_1 = jnp.zeros((8, LANES), jnp.float32)
        before = step == float(offset - 1)
        for j in range(TAPS):
            value_0 = jnp.where(in_0, near_0[j], next_0[j])
            value_1 = jnp.where(in_1, near_1[j], next_1[j])
            here = step == float(offset + j)
            top_0 = jnp.where(here, value_0, top_0)
            top_1 = jnp.where(here, value_1, top_1)
            low_0 = jnp.where(before, value_0, low_0)
            low_1 = jnp.where(before, value_1, low_1)
            before = here
        upper = weight_0 * top_0 + weight_1 * top_1
        lower = weight_0 * low_0 + weight_1 * low_1
        return upper + part_y * (lower - upper)

    row_groups = height // 8
    block_spans = []
    for b in range(blocks):
        spread = (b % 8) * (LANES // SP) + lax.broadcasted_iota(jnp.int32, (8, LANES), 1) // SP
        expanded = []
        for comp in range(2):
            value, rise, climb = vertex_rows[comp][b // 8]
            at = jnp.take_along_axis(value, spread, axis=1)
            low = jnp.take_along_axis(rise, spread, axis=1)
            high = jnp.take_along_axis(climb, spread, axis=1)
            expanded.append(at + along * jnp.where(left_side, low, high))
        columns = slice(b * LANES, (b + 1) * LANES)
        span = None
        for k in range(row_groups):
            moved = [
                tents[0] * ex[k : k + 1] + tents[1] * ex[k + 1 : k + 2] + tents[2] * ex[k + 2 : k + 3] for ex in expanded
            ]
            sample_x = lane_full + (moved[0] + LANES / 2.0)
            sample_y = sub + (moved[1] + float(k * 8 + height))
            rows = slice(k * 8, k * 8 + 8)
            sample_ref[0, rows, columns] = sample_x
            sample_ref[1, rows, columns] = sample_y
            floor_y = clipped_floor(sample_y)
            base = jnp.min(floor_y, axis=1, keepdims=True)
            base_ref[b, rows, :] = jnp.broadcast_to(base, (8, LANES))
            span = floor_y - base if span is None else jnp.maximum(span, floor_y - base)
        span_ref[b] = span
        spans = span if spans is None else jnp.maximum(spans, span)

    for b in range(blocks):
        columns = slice(b * LANES, (b + 1) * LANES)
        bases = [base_ref[b, k * 8 : k * 8 + 8, :] for k in range(row_groups)]
        taken_ref[b] = tap_rows(bases, 0, slab_ref[:, b * LANES : (b + 2) * LANES])

    for b in range(blocks):
        columns = slice(b * LANES, (b + 1) * LANES)
        bases = [base_ref[b, k * 8 : k * 8 + 8, :] for k in range(row_groups)]
        taken = (lambda i: taken_ref[b, i, :LANES]), (lambda i: taken_ref[b, i, LANES:])
        for k in range(row_groups):
            rows = slice(k * 8, k * 8 + 8)
            mixed_ref[rows, columns] = render(
                sample_ref[0, rows, columns], sample_ref[1, rows, columns], bases[k], taken, k, row_groups, 0
            )

    @pl.when(jnp.max(spans) > TAPS - 2.0)
    def _():
        for b in range(blocks):
            widest_ref[b] = jnp.max(span_ref[b]).astype(jnp.int32)

        def rest(b, carry):
            widest = widest_ref[b]

            @pl.when(widest > TAPS - 2)
            def _():
                start = pl.multiple_of(b * LANES, LANES)
                columns = pl.ds(start, LANES)
                bases = [base_ref[b, k * 8 : k * 8 + 8, :] for k in range(row_groups)]

                def more(i, c):
                    moved_bases = [base + (i * TAPS).astype(jnp.float32) for base in bases]
                    rows_taken = tap_rows(moved_bases, 0, slab_ref[:, pl.ds(start, 2 * LANES)])
                    taken = (lambda i: rows_taken[i, :LANES]), (lambda i: rows_taken[i, LANES:])
                    for k in range(row_groups):
                        rows = slice(k * 8, k * 8 + 8)
                        mixed_ref[rows, columns] = mixed_ref[rows, columns] + render(
                            sample_ref[0, rows, columns],
                            sample_ref[1, rows, columns],
                            moved_bases[k],
                            taken,
                            k,
                            row_groups,
                            0,
                        )
                    return c

                lax.fori_loop(1, (widest + 1 + TAPS) // TAPS, more, 0)

            return carry

        lax.fori_loop(0, blocks, rest, 0)

    out_ref[...] = mixed_ref[...].astype(jnp.bfloat16)


def per_device(points, source, slab_first, slab_count):
    strips = lax.axis_size("ty")
    height, width = source.shape
    tile_len = points.shape[1]
    blocks = width // LANES
    in_chip = [(i, i ^ 1) for i in range(strips)]
    across = []
    for i in range(1, strips - 1, 2):
        across.extend([(i, i + 1), (i + 1, i)])
    vmem = pl.BlockSpec(memory_space=pltpu.VMEM)
    smem = pl.BlockSpec(memory_space=pltpu.SMEM)
    anywhere = pl.BlockSpec(memory_space=pl.ANY)
    params = pltpu.CompilerParams(vmem_limit_bytes=32 * 1024 * 1024)
    small = pltpu.CompilerParams(vmem_limit_bytes=4 * 1024 * 1024)
    mate_points = lax.ppermute(points, "ty", in_chip)
    packed_rows = width // tile_len * height + 16
    packed_shape = jax.ShapeDtypeStruct((packed_rows, tile_len), jnp.bfloat16)
    laid = pl.pallas_call(
        lay_source_kernel,
        out_shape=packed_shape,
        in_specs=[vmem],
        out_specs=vmem,
        compiler_params=small,
        cost_estimate=pl.CostEstimate(flops=0, bytes_accessed=4 * source.size, transcendentals=0),
    )(source)
    packed = pl.pallas_call(
        functools.partial(lay_points_kernel, height, width),
        out_shape=packed_shape,
        in_specs=[vmem, vmem, anywhere],
        out_specs=anywhere,
        input_output_aliases={2: 0},
        scratch_shapes=[pltpu.VMEM((16, tile_len), jnp.bfloat16), pltpu.SemaphoreType.DMA],
        compiler_params=small,
    )(points, mate_points, laid)
    arrived = lax.ppermute(packed, "ty", across)
    mate_source = lax.ppermute(source, "ty", in_chip)
    groups = width // GROUP_PX

    def moment_scratch(sets):
        length = sets * tile_len // groups
        return [
            pltpu.VMEM((groups, 2 * NF, length), jnp.bfloat16),
            pltpu.VMEM((groups, 2 * LANES, length), jnp.bfloat16),
        ]

    totals = pl.pallas_call(
        functools.partial(near_kernel, strips, height, width),
        out_shape=jax.ShapeDtypeStruct((groups, NF, LANES), jnp.float32),
        in_specs=[vmem, vmem],
        out_specs=vmem,
        scratch_shapes=moment_scratch(2),
        compiler_params=params,
        cost_estimate=pl.CostEstimate(flops=4 * NF * LANES * 2 * tile_len * 4, bytes_accessed=10**6, transcendentals=2 * tile_len * NV),
    )(points, mate_points)
    arrived, totals = lax.optimization_barrier((arrived, totals))
    far = lax.ppermute(arrived[packed_rows - 16 : packed_rows - 8], "ty", in_chip)
    return pl.pallas_call(
        functools.partial(main_kernel, strips),
        out_shape=(
            jax.ShapeDtypeStruct((height, width), jnp.bfloat16),
            jax.ShapeDtypeStruct((6, VR, width // SP), jnp.float32),
        ),
        in_specs=[smem, smem] + [vmem] * 5,
        out_specs=(vmem, vmem),
        scratch_shapes=moment_scratch(3)
        + [
            pltpu.VMEM((LANES, width + LANES), jnp.bfloat16),
            pltpu.VMEM((2, height, width), jnp.float32),
            pltpu.VMEM((blocks, height, LANES), jnp.float32),
            pltpu.VMEM((blocks, 8, LANES), jnp.float32),
            pltpu.VMEM((blocks, TAPS * height, 2 * LANES), jnp.float32),
            pltpu.VMEM((height, width), jnp.float32),
            pltpu.SMEM((blocks,), jnp.int32),
        ],
        compiler_params=params,
    )(slab_first, slab_count, totals, source, mate_source, arrived, far)


def solution(mesh):
    return jax.shard_map(
        per_device,
        mesh=mesh,
        in_specs=(
            P(None, ("sec", "ty")),
            P(("sec", "ty"), None),
            P(("sec", "ty")),
            P(("sec", "ty")),
        ),
        out_specs=(P(("sec", "ty"), None), P(None, ("sec", "ty"), None)),
        check_vma=False,
    )
```

```python
import functools

import jax
import jax.numpy as jnp
import numpy as np
from jax import lax
from jax.experimental import pallas as pl
from jax.experimental.pallas import tpu as pltpu
from jax.sharding import PartitionSpec as P

BH = 16
PC = 4
SP = 8
VR = 4
LANES = 128
CELL = 16
RIDGE_TERM = 0.01
FEATS = 12
ER = 8
NF = FEATS * ER
GROUP_PX = LANES // PC * CELL
NV = GROUP_PX // SP + 2 * LANES // SP
EXP2_SCALE = 2.0 * float(np.log2(np.e))
TAPS = 12


def fiota(shape, dim):
    return lax.broadcasted_iota(jnp.int32, shape, dim).astype(jnp.float32)


def local_points(pts, tile, cell_cols, height):
    lane = lax.broadcasted_iota(jnp.int32, (1, pts.shape[1]), 1)
    cell = lane // PC
    base_x = (cell % cell_cols * CELL).astype(jnp.float32)
    base_y = (tile * height + cell // cell_cols * CELL).astype(jnp.float32)
    fixed_x, fixed_y = pts[0:1], pts[1:2]
    return jnp.concatenate(
        [fixed_x - base_x, fixed_y - base_y, pts[2:3] - fixed_x, pts[3:4] - fixed_y], axis=0
    )


def lookup(values, index):
    numbers = lax.GatherDimensionNumbers(
        offset_dims=(),
        collapsed_slice_dims=(1,),
        start_index_map=(1,),
        operand_batching_dims=(0,),
        start_indices_batching_dims=(0,),
    )
    return lax.gather(values, index[..., None], numbers, (1, 1), mode=lax.GatherScatterMode.PROMISE_IN_BOUNDS)


def split_pair(value):
    high = value.astype(jnp.bfloat16).astype(jnp.float32)
    return high, value - high


def lay_source_kernel(source_ref, packed_ref):
    height, width = source_ref.shape
    half = packed_ref.shape[1]
    for part in range(width // half):
        packed_ref[part * height : (part + 1) * height, :] = source_ref[:, part * half : (part + 1) * half]


def lay_points_kernel(height, width, own_ref, mate_ref, laid_ref, packed_ref, rows_ref, sem):
    tile = lax.axis_index("ty")
    rows = []
    for ref, owner in ((own_ref, tile), (mate_ref, tile + 1 - 2 * (tile % 2))):
        rows.extend(split_pair(local_points(ref[...], owner, width // CELL, height)))
    rows_ref[...] = jnp.concatenate(rows, axis=0).astype(jnp.bfloat16)
    base = packed_ref.shape[0] - 16
    copy = pltpu.make_async_copy(rows_ref, packed_ref.at[base : base + 16, :], sem)
    copy.start()
    copy.wait()


def group_totals(sets, tile, strips, height, width, feat_ref, weight_ref):
    cell_cols = width // CELL
    cell_rows = height // CELL
    groups = width // GROUP_PX
    ext_row = lax.broadcasted_iota(jnp.int32, (ER, 1), 0)
    vertex_y = (fiota((ER, 1), 0) * SP + (SP / 2.0 - SP - height / 2.0)) / height
    ext_tile = tile + jnp.where(ext_row == 0, -1, jnp.where(ext_row == VR + 1, 1, 0))
    scale = float(np.sqrt(EXP2_SCALE))
    lane_px = (lax.broadcasted_iota(jnp.int32, (1, LANES), 1) // PC * CELL).astype(jnp.float32) - GROUP_PX / 2.0
    vertex_ids = lax.broadcasted_iota(jnp.int32, (NV, LANES), 0)
    point_block = lax.broadcasted_iota(jnp.int32, (NV, LANES), 1) // (LANES // CELL * PC)
    band = (jnp.abs(vertex_ids // (LANES // SP) - 1 - point_block) <= 1).astype(jnp.float32)
    vertex_scaled = (fiota((NV, 1), 0) * SP + (SP / 2.0 - LANES - GROUP_PX / 2.0)) * (scale / height)
    zero_rows = jnp.zeros((LANES - NV, weight_ref.shape[2]), jnp.bfloat16)

    totals = []
    for g in range(groups):
        weight_ref[g, NV:LANES, :] = zero_rows
        weight_ref[g, LANES + NV :, :] = zero_rows
        for s, (pts, owner) in enumerate(sets):
            usable = (jnp.abs(owner - ext_tile) <= 1) & (owner >= 0) & (owner < strips)
            usable = usable.astype(jnp.float32)
            for c in range(cell_rows):
                lanes = slice(c * cell_cols * PC + g * LANES, c * cell_cols * PC + (g + 1) * LANES)
                chunk = slice((s * cell_rows + c) * LANES, (s * cell_rows + c + 1) * LANES)
                px = (pts[0:1, lanes] + lane_px) / height
                py = (pts[1:2, lanes] + ((owner - tile) * height + c * CELL).astype(jnp.float32)) / height - 0.5
                dx = pts[2:3, lanes] / height
                dy = pts[3:4, lanes] / height
                gap_y = (py - vertex_y) * scale
                wy = jnp.exp2(-(gap_y * gap_y)) * usable
                wpx, wpy, wdx, wdy = wy * px, wy * py, wy * dx, wy * dy
                rows = (wy, wpx, wpy, wdx, wdy, wpx * px, wpx * py, wpy * py, wdx * px, wdx * py, wdy * px, wdy * py)
                for f in range(0, FEATS, 2):
                    high, low = split_pair(jnp.concatenate(rows[f : f + 2], axis=0))
                    feat_ref[g, f * ER : (f + 2) * ER, chunk] = high.astype(jnp.bfloat16)
                    feat_ref[g, NF + f * ER : NF + (f + 2) * ER, chunk] = low.astype(jnp.bfloat16)
                gap_x = px * scale - vertex_scaled
                wx = jnp.exp2(-(gap_x * gap_x)) * band
                high, low = split_pair(wx)
                weight_ref[g, 0:NV, chunk] = high.astype(jnp.bfloat16)
                weight_ref[g, LANES : LANES + NV, chunk] = low.astype(jnp.bfloat16)
        both = lax.dot_general(
            feat_ref[g], weight_ref[g], (((1,), (1,)), ((), ())), preferred_element_type=jnp.float32
        )
        both = both[:NF] + both[NF:]
        totals.append(both[:, :LANES] + both[:, LANES:])
    return totals


def near_kernel(strips, height, width, own_ref, mate_ref, totals_ref, feat_ref, weight_ref):
    tile = lax.axis_index("ty")
    mate = tile + 1 - 2 * (tile % 2)
    cell_cols = width // CELL
    sets = (
        (local_points(own_ref[...], tile, cell_cols, height), tile),
        (local_points(mate_ref[...], mate, cell_cols, height), mate),
    )
    for g, value in enumerate(group_totals(sets, tile, strips, height, width, feat_ref, weight_ref)):
        totals_ref[g] = value


def main_kernel(
    strips,
    first_ref,
    count_ref,
    totals_ref,
    source_ref,
    mate_source_ref,
    packed_ref,
    far_ref,
    out_ref,
    affine_ref,
    feat_ref,
    weight_ref,
    slab_ref,
    sample_ref,
    base_ref,
    span_ref,
    taken_ref,
    mixed_ref,
    widest_ref,
):
    height, width = source_ref.shape
    groups = width // GROUP_PX
    blocks = width // LANES
    halves = blocks // 8
    tile = lax.axis_index("ty")
    odd = tile % 2
    toward = 1 - 2 * odd
    partner = tile - toward
    partner_mate = tile - 2 * toward
    beyond = tile + 2 * toward

    slots_from = first_ref[0] * BH - (tile - 1) * height
    slots_to = slots_from + count_ref[0] * BH
    left_half = lax.broadcasted_iota(jnp.int32, (1, LANES), 1) < LANES // 2
    half_cols = packed_ref.shape[1]
    slab_ref[3 * height :, :] = jnp.zeros((slab_ref.shape[0] - 3 * height, slab_ref.shape[1]), jnp.bfloat16)

    def place(load, row_start, chunk):
        local = row_start + chunk * 16
        row = lax.broadcasted_iota(jnp.int32, (16, 1), 0) + local
        live = ((row >= slots_from) & (row < slots_to)).astype(jnp.float32)
        before = jnp.zeros((16, LANES), jnp.float32)
        for b in range(blocks + 1):
            if b < blocks:
                now = pltpu.roll(load(b).astype(jnp.float32) * live, LANES // 2, axis=1)
            else:
                now = jnp.zeros((16, LANES), jnp.float32)
            merged = jnp.where(left_half, before, now).astype(jnp.bfloat16)
            slab_ref[pl.ds(pl.multiple_of(local, 16), 16), b * LANES : (b + 1) * LANES] = merged
            before = now

    for chunk in range(height // 16):
        rows = slice(chunk * 16, chunk * 16 + 16)
        place(lambda b: source_ref[rows, b * LANES : (b + 1) * LANES], height, chunk)
        place(lambda b: mate_source_ref[rows, b * LANES : (b + 1) * LANES], height + toward * height, chunk)

        def from_packed(b):
            part = b * LANES // half_cols
            lane = b * LANES - part * half_cols
            return packed_ref[part * height + chunk * 16 : part * height + chunk * 16 + 16, lane : lane + LANES]

        place(from_packed, height - toward * height, chunk)

    point_rows = packed_ref[packed_ref.shape[0] - 16 :, :].astype(jnp.float32)
    far_rows = far_ref[...].astype(jnp.float32)
    sets = (
        (point_rows[0:4] + point_rows[4:8], partner),
        (point_rows[8:12] + point_rows[12:16], partner_mate),
        (far_rows[0:4] + far_rows[4:8], beyond),
    )
    vertex_y = (fiota((ER, 1), 0) * SP + (SP / 2.0 - SP - height / 2.0)) / height
    totals = group_totals(sets, tile, strips, height, width, feat_ref, weight_ref)
    totals = [totals[g] + totals_ref[g] for g in range(groups)]

    lane = lax.broadcasted_iota(jnp.int32, (1, LANES), 1)
    per_group = GROUP_PX // SP
    affines = []
    for h in range(halves):
        moments = None
        vertex_group = 2 * h + lane // per_group
        for g in range(groups):
            start = g * per_group - LANES // SP - h * LANES
            if start + NV <= 0 or start >= LANES:
                continue
            part = pltpu.roll(totals[g], start % LANES, axis=1)
            inside = ((lane >= start) & (lane < start + NV)).astype(jnp.float32)
            move = ((g - vertex_group) * (GROUP_PX // height)).astype(jnp.float32)
            part = [part[f * ER : (f + 1) * ER] * inside for f in range(FEATS)]
            part[5] = part[5] + move * (2.0 * part[1] + move * part[0])
            part[6] = part[6] + move * part[2]
            part[8] = part[8] + move * part[3]
            part[10] = part[10] + move * part[4]
            part[1] = part[1] + move * part[0]
            moments = part if moments is None else [x + y for x, y in zip(moments, part)]
        inverse = 1.0 / moments[0]
        mean_px, mean_py, mean_dx, mean_dy = [moments[i] * inverse for i in range(1, 5)]
        cov_xx = moments[5] * inverse - mean_px * mean_px + RIDGE_TERM
        cov_xy = moments[6] * inverse - mean_px * mean_py
        cov_yy = moments[7] * inverse - mean_py * mean_py + RIDGE_TERM
        cross_xx = moments[8] * inverse - mean_dx * mean_px - RIDGE_TERM
        cross_xy = moments[9] * inverse - mean_dx * mean_py
        cross_yx = moments[10] * inverse - mean_dy * mean_px
        cross_yy = moments[11] * inverse - mean_dy * mean_py - RIDGE_TERM
        over = 1.0 / (cov_xx * cov_yy - cov_xy * cov_xy)
        lin_xx = (cross_xx * cov_yy - cross_xy * cov_xy) * over
        lin_xy = (cross_xy * cov_xx - cross_xx * cov_xy) * over
        lin_yx = (cross_yx * cov_yy - cross_yy * cov_xy) * over
        lin_yy = (cross_yy * cov_xx - cross_yx * cov_xy) * over
        vertex_x = ((lane % per_group * SP).astype(jnp.float32) + (SP - GROUP_PX) / 2.0) / height
        delta_x = vertex_x - mean_px
        delta_y = vertex_y - mean_py
        shift_x = mean_dx + lin_xx * delta_x + lin_xy * delta_y
        shift_y = mean_dy + lin_yx * delta_x + lin_yy * delta_y
        results = (lin_xx + 1.0, lin_xy, lin_yx, lin_yy + 1.0, shift_x, shift_y)
        for i, value in enumerate(results):
            affine_ref[i, :, h * LANES : (h + 1) * LANES] = value[1 : VR + 1]
        affines.append((shift_x, shift_y))

    ext = lax.broadcasted_iota(jnp.int32, (ER, LANES), 0)
    along = (lane % SP).astype(jnp.float32) / SP - 0.5
    left_side = along < 0.0
    vertex_rows = []
    for comp in range(2):
        rows = []
        for h in range(halves):
            value = affines[h][comp] * float(height)
            value = jnp.where((ext == 0) & (tile == 0), jnp.broadcast_to(value[1:2], value.shape), value)
            value = jnp.where((ext == VR + 1) & (tile == strips - 1), jnp.broadcast_to(value[VR : VR + 1], value.shape), value)
            rows.append(value)
        steps = []
        for h in range(halves):
            value = rows[h]
            first = jnp.broadcast_to(rows[h - 1][:, LANES - 1 :] if h > 0 else value[:, :1], value.shape)
            last = jnp.broadcast_to(rows[h + 1][:, :1] if h + 1 < halves else value[:, LANES - 1 :], value.shape)
            before = jnp.where(lane == 0, first, pltpu.roll(value, 1, axis=1))
            after = jnp.where(lane == LANES - 1, last, pltpu.roll(value, LANES - 1, axis=1))
            steps.append((value, value - before, after - value))
        vertex_rows.append(steps)

    sub = lax.broadcasted_iota(jnp.int32, (8, LANES), 0).astype(jnp.float32)
    lane_full = fiota((8, LANES), 1)
    tents = (
        jnp.maximum(0.0, 0.5 - sub / SP),
        1.0 - jnp.abs(sub - SP / 2.0) / SP,
        jnp.maximum(0.0, sub / SP - 0.5),
    )
    last_row = 3.0 * height
    spans = None

    def clipped_floor(sample_y):
        return jnp.clip(jnp.floor(sample_y), -2.0, last_row)

    def one_hot(base, k, offset):
        return jnp.where(lane_full - base == float(offset), 1.0, 0.0)

    def tap_rows(bases, offset, slab):
        picks = [
            jnp.concatenate([one_hot(bases[k], k, offset + j) for k in range(len(bases))], axis=0).astype(jnp.bfloat16)
            for j in range(TAPS)
        ]
        return jnp.dot(jnp.concatenate(picks, axis=0), slab, preferred_element_type=jnp.float32).astype(jnp.bfloat16)

    def render(sample_x, sample_y, base, taken, k):
        floor_x = jnp.floor(sample_x)
        part_x = sample_x - floor_x
        part_y = sample_y - jnp.floor(sample_y)
        floor_x = jnp.clip(floor_x, -2.0, 2.0 * LANES)
        weight_0 = jnp.where((floor_x >= 0.0) & (floor_x < 2.0 * LANES), 1.0 - part_x, 0.0)
        weight_1 = jnp.where((floor_x >= -1.0) & (floor_x < 2.0 * LANES - 1.0), part_x, 0.0)
        index = floor_x.astype(jnp.int32)
        index_0 = (index & (LANES - 1)).astype(jnp.int16)
        index_1 = ((index + 1) & (LANES - 1)).astype(jnp.int16)
        index = index.astype(jnp.int16)
        in_0 = index < LANES
        in_1 = index < LANES - 1
        step = (clipped_floor(sample_y) - base).astype(jnp.int32).astype(jnp.int16)
        near, after = taken
        at = [slice(j * height + k * 16, j * height + k * 16 + 16) for j in range(TAPS)]
        near_0 = [lookup(near(i), index_0) for i in at]
        next_0 = [lookup(after(i), index_0) for i in at]
        near_1 = [lookup(near(i), index_1) for i in at]
        next_1 = [lookup(after(i), index_1) for i in at]
        top_0 = top_1 = low_0 = low_1 = jnp.zeros((16, LANES), jnp.bfloat16)
        before = step == -1
        for j in range(TAPS):
            value_0 = jnp.where(in_0, near_0[j], next_0[j])
            value_1 = jnp.where(in_1, near_1[j], next_1[j])
            here = step == j
            top_0 = jnp.where(here, value_0, top_0)
            top_1 = jnp.where(here, value_1, top_1)
            low_0 = jnp.where(before, value_0, low_0)
            low_1 = jnp.where(before, value_1, low_1)
            before = here
        upper = weight_0 * top_0.astype(jnp.float32) + weight_1 * top_1.astype(jnp.float32)
        lower = weight_0 * low_0.astype(jnp.float32) + weight_1 * low_1.astype(jnp.float32)
        return upper + part_y * (lower - upper)

    row_groups = height // 8
    block_spans = []
    for b in range(blocks):
        spread = (b % 8) * (LANES // SP) + lax.broadcasted_iota(jnp.int32, (8, LANES), 1) // SP
        expanded = []
        for comp in range(2):
            value, rise, climb = vertex_rows[comp][b // 8]
            at = jnp.take_along_axis(value, spread, axis=1)
            low = jnp.take_along_axis(rise, spread, axis=1)
            high = jnp.take_along_axis(climb, spread, axis=1)
            expanded.append(at + along * jnp.where(left_side, low, high))
        columns = slice(b * LANES, (b + 1) * LANES)
        span = None
        for k in range(row_groups):
            moved = [
                tents[0] * ex[k : k + 1] + tents[1] * ex[k + 1 : k + 2] + tents[2] * ex[k + 2 : k + 3] for ex in expanded
            ]
            sample_x = lane_full + (moved[0] + LANES / 2.0)
            sample_y = sub + (moved[1] + float(k * 8 + height))
            rows = slice(k * 8, k * 8 + 8)
            sample_ref[0, rows, columns] = sample_x
            sample_ref[1, rows, columns] = sample_y
            floor_y = clipped_floor(sample_y)
            base = jnp.min(floor_y, axis=1, keepdims=True)
            base_ref[b, rows, :] = jnp.broadcast_to(base, (8, LANES))
            span = floor_y - base if span is None else jnp.maximum(span, floor_y - base)
        span_ref[b] = span
        spans = span if spans is None else jnp.maximum(spans, span)

    for b in range(blocks):
        columns = slice(b * LANES, (b + 1) * LANES)
        bases = [base_ref[b, k * 8 : k * 8 + 8, :] for k in range(row_groups)]
        taken_ref[b] = tap_rows(bases, 0, slab_ref[:, b * LANES : (b + 2) * LANES])

    for b in range(blocks):
        columns = slice(b * LANES, (b + 1) * LANES)
        taken = (lambda i: taken_ref[b, i, :LANES]), (lambda i: taken_ref[b, i, LANES:])
        for k in range(height // 16):
            rows = slice(k * 16, k * 16 + 16)
            mixed_ref[rows, columns] = render(
                sample_ref[0, rows, columns], sample_ref[1, rows, columns], base_ref[b, rows, :], taken, k
            )

    @pl.when(jnp.max(spans) > TAPS - 2.0)
    def _():
        for b in range(blocks):
            widest_ref[b] = jnp.max(span_ref[b]).astype(jnp.int32)

        def rest(b, carry):
            widest = widest_ref[b]

            @pl.when(widest > TAPS - 2)
            def _():
                start = pl.multiple_of(b * LANES, LANES)
                columns = pl.ds(start, LANES)
                bases = [base_ref[b, k * 8 : k * 8 + 8, :] for k in range(row_groups)]

                def more(i, c):
                    moved_bases = [base + (i * TAPS).astype(jnp.float32) for base in bases]
                    rows_taken = tap_rows(moved_bases, 0, slab_ref[:, pl.ds(start, 2 * LANES)])
                    taken = (lambda i: rows_taken[i, :LANES]), (lambda i: rows_taken[i, LANES:])
                    for k in range(height // 16):
                        rows = slice(k * 16, k * 16 + 16)
                        mixed_ref[rows, columns] = mixed_ref[rows, columns] + render(
                            sample_ref[0, rows, columns],
                            sample_ref[1, rows, columns],
                            base_ref[b, rows, :] + (i * TAPS).astype(jnp.float32),
                            taken,
                            k,
                        )
                    return c

                lax.fori_loop(1, (widest + 1 + TAPS) // TAPS, more, 0)

            return carry

        lax.fori_loop(0, blocks, rest, 0)

    out_ref[...] = mixed_ref[...].astype(jnp.bfloat16)


def per_device(points, source, slab_first, slab_count):
    strips = lax.axis_size("ty")
    height, width = source.shape
    tile_len = points.shape[1]
    blocks = width // LANES
    in_chip = [(i, i ^ 1) for i in range(strips)]
    across = []
    for i in range(1, strips - 1, 2):
        across.extend([(i, i + 1), (i + 1, i)])
    vmem = pl.BlockSpec(memory_space=pltpu.VMEM)
    smem = pl.BlockSpec(memory_space=pltpu.SMEM)
    anywhere = pl.BlockSpec(memory_space=pl.ANY)
    params = pltpu.CompilerParams(vmem_limit_bytes=32 * 1024 * 1024)
    small = pltpu.CompilerParams(vmem_limit_bytes=4 * 1024 * 1024)
    mate_points = lax.ppermute(points, "ty", in_chip)
    packed_rows = width // tile_len * height + 16
    packed_shape = jax.ShapeDtypeStruct((packed_rows, tile_len), jnp.bfloat16)
    laid = pl.pallas_call(
        lay_source_kernel,
        out_shape=packed_shape,
        in_specs=[vmem],
        out_specs=vmem,
        compiler_params=small,
        cost_estimate=pl.CostEstimate(flops=0, bytes_accessed=4 * source.size, transcendentals=0),
    )(source)
    packed = pl.pallas_call(
        functools.partial(lay_points_kernel, height, width),
        out_shape=packed_shape,
        in_specs=[vmem, vmem, anywhere],
        out_specs=anywhere,
        input_output_aliases={2: 0},
        scratch_shapes=[pltpu.VMEM((16, tile_len), jnp.bfloat16), pltpu.SemaphoreType.DMA],
        compiler_params=small,
    )(points, mate_points, laid)
    arrived = lax.ppermute(packed, "ty", across)
    mate_source = lax.ppermute(source, "ty", in_chip)
    groups = width // GROUP_PX

    def moment_scratch(sets):
        length = sets * tile_len // groups
        return [
            pltpu.VMEM((groups, 2 * NF, length), jnp.bfloat16),
            pltpu.VMEM((groups, 2 * LANES, length), jnp.bfloat16),
        ]

    totals = pl.pallas_call(
        functools.partial(near_kernel, strips, height, width),
        out_shape=jax.ShapeDtypeStruct((groups, NF, LANES), jnp.float32),
        in_specs=[vmem, vmem],
        out_specs=vmem,
        scratch_shapes=moment_scratch(2),
        compiler_params=params,
        cost_estimate=pl.CostEstimate(flops=4 * NF * LANES * 2 * tile_len * 4, bytes_accessed=10**6, transcendentals=2 * tile_len * NV),
    )(points, mate_points)
    arrived, totals = lax.optimization_barrier((arrived, totals))
    far = lax.ppermute(arrived[packed_rows - 16 : packed_rows - 8], "ty", in_chip)
    return pl.pallas_call(
        functools.partial(main_kernel, strips),
        out_shape=(
            jax.ShapeDtypeStruct((height, width), jnp.bfloat16),
            jax.ShapeDtypeStruct((6, VR, width // SP), jnp.float32),
        ),
        in_specs=[smem, smem] + [vmem] * 5,
        out_specs=(vmem, vmem),
        scratch_shapes=moment_scratch(3)
        + [
            pltpu.VMEM((LANES, width + LANES), jnp.bfloat16),
            pltpu.VMEM((2, height, width), jnp.float32),
            pltpu.VMEM((blocks, height, LANES), jnp.float32),
            pltpu.VMEM((blocks, 8, LANES), jnp.float32),
            pltpu.VMEM((blocks, TAPS * height, 2 * LANES), jnp.bfloat16),
            pltpu.VMEM((height, width), jnp.float32),
            pltpu.SMEM((blocks,), jnp.int32),
        ],
        compiler_params=params,
    )(slab_first, slab_count, totals, source, mate_source, arrived, far)


def solution(mesh):
    return jax.shard_map(
        per_device,
        mesh=mesh,
        in_specs=(
            P(None, ("sec", "ty")),
            P(("sec", "ty"), None),
            P(("sec", "ty")),
            P(("sec", "ty")),
        ),
        out_specs=(P(("sec", "ty"), None), P(None, ("sec", "ty"), None)),
        check_vma=False,
    )
```

```python
import functools

import jax
import jax.numpy as jnp
import numpy as np
from jax import lax
from jax.experimental import pallas as pl
from jax.experimental.pallas import tpu as pltpu
from jax.sharding import PartitionSpec as P

BH = 16
PC = 4
SP = 8
VR = 4
LANES = 128
CELL = 16
RIDGE_TERM = 0.01
FEATS = 12
ER = 8
NF = FEATS * ER
GROUP_PX = LANES // PC * CELL
NV = GROUP_PX // SP + 2 * LANES // SP
EXP2_SCALE = 2.0 * float(np.log2(np.e))
TAPS = 12


def fiota(shape, dim):
    return lax.broadcasted_iota(jnp.int32, shape, dim).astype(jnp.float32)


def local_points(pts, tile, cell_cols, height):
    lane = lax.broadcasted_iota(jnp.int32, (1, pts.shape[1]), 1)
    cell = lane // PC
    base_x = (cell % cell_cols * CELL).astype(jnp.float32)
    base_y = (tile * height + cell // cell_cols * CELL).astype(jnp.float32)
    fixed_x, fixed_y = pts[0:1], pts[1:2]
    return jnp.concatenate(
        [fixed_x - base_x, fixed_y - base_y, pts[2:3] - fixed_x, pts[3:4] - fixed_y], axis=0
    )


def lookup(values, index):
    numbers = lax.GatherDimensionNumbers(
        offset_dims=(),
        collapsed_slice_dims=(1,),
        start_index_map=(1,),
        operand_batching_dims=(0,),
        start_indices_batching_dims=(0,),
    )
    return lax.gather(values, index[..., None], numbers, (1, 1), mode=lax.GatherScatterMode.PROMISE_IN_BOUNDS)


def split_pair(value):
    high = value.astype(jnp.bfloat16).astype(jnp.float32)
    return high, value - high


def shifts_of(local):
    return jnp.concatenate([local[0:2], local[2:4] - local[0:2]], axis=0)


def lay_own_kernel(local_ref, source_ref, packed_ref, rows_ref):
    height, width = source_ref.shape
    half = packed_ref.shape[1]
    for part in range(width // half):
        packed_ref[part * height : (part + 1) * height, :] = source_ref[:, part * half : (part + 1) * half]
    rows_ref[...] = jnp.concatenate(split_pair(shifts_of(local_ref[...])), axis=0)


def lay_mate_kernel(height, width, own_rows_ref, mate_ref, laid_ref, packed_ref, rows_ref, sem):
    tile = lax.axis_index("ty")
    mate = split_pair(local_points(mate_ref[...], tile + 1 - 2 * (tile % 2), width // CELL, height))
    rows_ref[...] = jnp.concatenate([own_rows_ref[...], *mate], axis=0).astype(jnp.bfloat16)
    base = packed_ref.shape[0] - 16
    copy = pltpu.make_async_copy(rows_ref, packed_ref.at[base : base + 16, :], sem)
    copy.start()
    copy.wait()


def group_totals(sets, tile, strips, height, width, feat_ref, weight_ref):
    cell_cols = width // CELL
    cell_rows = height // CELL
    groups = width // GROUP_PX
    ext_row = lax.broadcasted_iota(jnp.int32, (ER, 1), 0)
    vertex_y = (fiota((ER, 1), 0) * SP + (SP / 2.0 - SP - height / 2.0)) / height
    ext_tile = tile + jnp.where(ext_row == 0, -1, jnp.where(ext_row == VR + 1, 1, 0))
    scale = float(np.sqrt(EXP2_SCALE))
    lane_px = (lax.broadcasted_iota(jnp.int32, (1, LANES), 1) // PC * CELL).astype(jnp.float32) - GROUP_PX / 2.0
    per_block = LANES // SP
    block_lanes = LANES // CELL * PC
    reach = 3 * per_block
    lane_ids = lax.broadcasted_iota(jnp.int32, (1, LANES), 1)
    block_px = (lane_ids % block_lanes // PC * CELL).astype(jnp.float32) + (LANES - SP / 2.0)
    vertex_px = fiota((reach, 1), 0) * SP
    lane_block = (lax.broadcasted_iota(jnp.int32, (per_block, LANES), 1) // block_lanes).astype(jnp.int16)
    in_block = [lane_block == j for j in range(LANES // block_lanes)]
    nothing = jnp.zeros((per_block, LANES), jnp.bfloat16)

    def spread_out(near, i):
        result = nothing
        for m in range(3):
            if 0 <= i - m < len(in_block):
                result = jnp.where(in_block[i - m], near[m * per_block : (m + 1) * per_block], result)
        return result

    zero_rows = jnp.zeros((LANES - NV, weight_ref.shape[2]), jnp.bfloat16)

    totals = []
    for g in range(groups):
        weight_ref[g, NV:LANES, :] = zero_rows
        weight_ref[g, LANES + NV :, :] = zero_rows
        for s, (pts, owner) in enumerate(sets):
            usable = (jnp.abs(owner - ext_tile) <= 1) & (owner >= 0) & (owner < strips)
            usable = usable.astype(jnp.float32)
            for c in range(cell_rows):
                lanes = slice(c * cell_cols * PC + g * LANES, c * cell_cols * PC + (g + 1) * LANES)
                chunk = slice((s * cell_rows + c) * LANES, (s * cell_rows + c + 1) * LANES)
                px = (pts[0:1, lanes] + lane_px) / height
                py = (pts[1:2, lanes] + ((owner - tile) * height + c * CELL).astype(jnp.float32)) / height - 0.5
                dx = pts[2:3, lanes] / height
                dy = pts[3:4, lanes] / height
                gap_y = (py - vertex_y) * scale
                wy = jnp.exp2(-(gap_y * gap_y)) * usable
                wpx, wpy, wdx, wdy = wy * px, wy * py, wy * dx, wy * dy
                rows = (wy, wpx, wpy, wdx, wdy, wpx * px, wpx * py, wpy * py, wdx * px, wdx * py, wdy * px, wdy * py)
                for f in range(0, FEATS, 2):
                    high, low = split_pair(jnp.concatenate(rows[f : f + 2], axis=0))
                    feat_ref[g, f * ER : (f + 2) * ER, chunk] = high.astype(jnp.bfloat16)
                    feat_ref[g, NF + f * ER : NF + (f + 2) * ER, chunk] = low.astype(jnp.bfloat16)
                gap_x = (pts[0:1, lanes] + block_px - vertex_px) * (scale / height)
                high, low = split_pair(jnp.exp2(-(gap_x * gap_x)))
                for row, near in ((0, high.astype(jnp.bfloat16)), (LANES, low.astype(jnp.bfloat16))):
                    for i in range(NV // per_block):
                        start = row + i * per_block
                        weight_ref[g, start : start + per_block, chunk] = spread_out(near, i)
        both = lax.dot_general(
            feat_ref[g], weight_ref[g], (((1,), (1,)), ((), ())), preferred_element_type=jnp.float32
        )
        both = both[:NF] + both[NF:]
        totals.append(both[:, :LANES] + both[:, LANES:])
    return totals


def near_kernel(strips, height, width, own_ref, mate_ref, totals_ref, feat_ref, weight_ref):
    tile = lax.axis_index("ty")
    mate = tile + 1 - 2 * (tile % 2)
    cell_cols = width // CELL
    sets = (
        (shifts_of(own_ref[...]), tile),
        (local_points(mate_ref[...], mate, cell_cols, height), mate),
    )
    for g, value in enumerate(group_totals(sets, tile, strips, height, width, feat_ref, weight_ref)):
        totals_ref[g] = value


def main_kernel(
    strips,
    first_ref,
    count_ref,
    totals_ref,
    source_ref,
    mate_source_ref,
    packed_ref,
    far_ref,
    out_ref,
    affine_ref,
    feat_ref,
    weight_ref,
    slab_ref,
    sample_ref,
    base_ref,
    span_ref,
    taken_ref,
    mixed_ref,
    widest_ref,
):
    height, width = source_ref.shape
    groups = width // GROUP_PX
    blocks = width // LANES
    halves = blocks // 8
    tile = lax.axis_index("ty")
    odd = tile % 2
    toward = 1 - 2 * odd
    partner = tile - toward
    partner_mate = tile - 2 * toward
    beyond = tile + 2 * toward

    slots_from = first_ref[0] * BH - (tile - 1) * height
    slots_to = slots_from + count_ref[0] * BH
    left_half = lax.broadcasted_iota(jnp.int32, (1, LANES), 1) < LANES // 2
    half_cols = packed_ref.shape[1]
    slab_ref[3 * height :, :] = jnp.zeros((slab_ref.shape[0] - 3 * height, slab_ref.shape[1]), jnp.bfloat16)

    def place(load, row_start, chunk):
        local = row_start + chunk * 16
        row = lax.broadcasted_iota(jnp.int32, (16, 1), 0) + local
        live = ((row >= slots_from) & (row < slots_to)).astype(jnp.float32)
        before = jnp.zeros((16, LANES), jnp.float32)
        for b in range(blocks + 1):
            if b < blocks:
                now = pltpu.roll(load(b).astype(jnp.float32) * live, LANES // 2, axis=1)
            else:
                now = jnp.zeros((16, LANES), jnp.float32)
            merged = jnp.where(left_half, before, now).astype(jnp.bfloat16)
            slab_ref[pl.ds(pl.multiple_of(local, 16), 16), b * LANES : (b + 1) * LANES] = merged
            before = now

    for chunk in range(height // 16):
        rows = slice(chunk * 16, chunk * 16 + 16)
        place(lambda b: source_ref[rows, b * LANES : (b + 1) * LANES], height, chunk)
        place(lambda b: mate_source_ref[rows, b * LANES : (b + 1) * LANES], height + toward * height, chunk)

        def from_packed(b):
            part = b * LANES // half_cols
            lane = b * LANES - part * half_cols
            return packed_ref[part * height + chunk * 16 : part * height + chunk * 16 + 16, lane : lane + LANES]

        place(from_packed, height - toward * height, chunk)

    point_rows = packed_ref[packed_ref.shape[0] - 16 :, :].astype(jnp.float32)
    far_rows = far_ref[...].astype(jnp.float32)
    sets = (
        (point_rows[0:4] + point_rows[4:8], partner),
        (point_rows[8:12] + point_rows[12:16], partner_mate),
        (far_rows[0:4] + far_rows[4:8], beyond),
    )
    vertex_y = (fiota((ER, 1), 0) * SP + (SP / 2.0 - SP - height / 2.0)) / height
    totals = group_totals(sets, tile, strips, height, width, feat_ref, weight_ref)
    totals = [totals[g] + totals_ref[g] for g in range(groups)]

    lane = lax.broadcasted_iota(jnp.int32, (1, LANES), 1)
    per_group = GROUP_PX // SP
    affines = []
    for h in range(halves):
        moments = None
        vertex_group = 2 * h + lane // per_group
        for g in range(groups):
            start = g * per_group - LANES // SP - h * LANES
            if start + NV <= 0 or start >= LANES:
                continue
            part = pltpu.roll(totals[g], start % LANES, axis=1)
            inside = ((lane >= start) & (lane < start + NV)).astype(jnp.float32)
            move = ((g - vertex_group) * (GROUP_PX // height)).astype(jnp.float32)
            part = [part[f * ER : (f + 1) * ER] * inside for f in range(FEATS)]
            part[5] = part[5] + move * (2.0 * part[1] + move * part[0])
            part[6] = part[6] + move * part[2]
            part[8] = part[8] + move * part[3]
            part[10] = part[10] + move * part[4]
            part[1] = part[1] + move * part[0]
            moments = part if moments is None else [x + y for x, y in zip(moments, part)]
        inverse = 1.0 / moments[0]
        mean_px, mean_py, mean_dx, mean_dy = [moments[i] * inverse for i in range(1, 5)]
        cov_xx = moments[5] * inverse - mean_px * mean_px + RIDGE_TERM
        cov_xy = moments[6] * inverse - mean_px * mean_py
        cov_yy = moments[7] * inverse - mean_py * mean_py + RIDGE_TERM
        cross_xx = moments[8] * inverse - mean_dx * mean_px - RIDGE_TERM
        cross_xy = moments[9] * inverse - mean_dx * mean_py
        cross_yx = moments[10] * inverse - mean_dy * mean_px
        cross_yy = moments[11] * inverse - mean_dy * mean_py - RIDGE_TERM
        over = 1.0 / (cov_xx * cov_yy - cov_xy * cov_xy)
        lin_xx = (cross_xx * cov_yy - cross_xy * cov_xy) * over
        lin_xy = (cross_xy * cov_xx - cross_xx * cov_xy) * over
        lin_yx = (cross_yx * cov_yy - cross_yy * cov_xy) * over
        lin_yy = (cross_yy * cov_xx - cross_yx * cov_xy) * over
        vertex_x = ((lane % per_group * SP).astype(jnp.float32) + (SP - GROUP_PX) / 2.0) / height
        delta_x = vertex_x - mean_px
        delta_y = vertex_y - mean_py
        shift_x = mean_dx + lin_xx * delta_x + lin_xy * delta_y
        shift_y = mean_dy + lin_yx * delta_x + lin_yy * delta_y
        results = (lin_xx + 1.0, lin_xy, lin_yx, lin_yy + 1.0, shift_x, shift_y)
        for i, value in enumerate(results):
            affine_ref[i, :, h * LANES : (h + 1) * LANES] = value[1 : VR + 1]
        affines.append((shift_x, shift_y))

    ext = lax.broadcasted_iota(jnp.int32, (ER, LANES), 0)
    along = (lane % SP).astype(jnp.float32) / SP - 0.5
    left_side = along < 0.0
    vertex_rows = []
    for comp in range(2):
        rows = []
        for h in range(halves):
            value = affines[h][comp] * float(height)
            value = jnp.where((ext == 0) & (tile == 0), jnp.broadcast_to(value[1:2], value.shape), value)
            value = jnp.where((ext == VR + 1) & (tile == strips - 1), jnp.broadcast_to(value[VR : VR + 1], value.shape), value)
            rows.append(value)
        steps = []
        for h in range(halves):
            value = rows[h]
            first = jnp.broadcast_to(rows[h - 1][:, LANES - 1 :] if h > 0 else value[:, :1], value.shape)
            last = jnp.broadcast_to(rows[h + 1][:, :1] if h + 1 < halves else value[:, LANES - 1 :], value.shape)
            before = jnp.where(lane == 0, first, pltpu.roll(value, 1, axis=1))
            after = jnp.where(lane == LANES - 1, last, pltpu.roll(value, LANES - 1, axis=1))
            steps.append((value, value - before, after - value))
        vertex_rows.append(steps)

    sub = lax.broadcasted_iota(jnp.int32, (8, LANES), 0).astype(jnp.float32)
    lane_full = fiota((8, LANES), 1)
    tents = (
        jnp.maximum(0.0, 0.5 - sub / SP),
        1.0 - jnp.abs(sub - SP / 2.0) / SP,
        jnp.maximum(0.0, sub / SP - 0.5),
    )
    last_row = 3.0 * height
    spans = None

    def clipped_floor(sample_y):
        return jnp.clip(jnp.floor(sample_y), -2.0, last_row)

    lanes_16 = fiota((16, LANES), 1)

    def tap_rows(bases, slab):
        away = [(lanes_16 - base).astype(jnp.int32).astype(jnp.int16) for base in bases]
        one, none = jnp.ones((16, LANES), jnp.bfloat16), jnp.zeros((16, LANES), jnp.bfloat16)
        picks = [jnp.where(gap == j, one, none) for j in range(TAPS) for gap in away]
        return jnp.dot(jnp.concatenate(picks, axis=0), slab, preferred_element_type=jnp.float32).astype(jnp.bfloat16)

    def render(sample_x, sample_y, base, taken, k):
        floor_x = jnp.floor(sample_x)
        part_x = sample_x - floor_x
        part_y = sample_y - jnp.floor(sample_y)
        floor_x = jnp.clip(floor_x, -2.0, 2.0 * LANES)
        weight_0 = jnp.where((floor_x >= 0.0) & (floor_x < 2.0 * LANES), 1.0 - part_x, 0.0)
        weight_1 = jnp.where((floor_x >= -1.0) & (floor_x < 2.0 * LANES - 1.0), part_x, 0.0)
        index = floor_x.astype(jnp.int32)
        index_0 = (index & (LANES - 1)).astype(jnp.int16)
        index_1 = ((index + 1) & (LANES - 1)).astype(jnp.int16)
        index = index.astype(jnp.int16)
        in_0 = index < LANES
        in_1 = index < LANES - 1
        step = (clipped_floor(sample_y) - base).astype(jnp.int32).astype(jnp.int16)
        near, after = taken
        at = [slice(j * height + k * 16, j * height + k * 16 + 16) for j in range(TAPS)]
        near_0 = [lookup(near(i), index_0) for i in at]
        next_0 = [lookup(after(i), index_0) for i in at]
        near_1 = [lookup(near(i), index_1) for i in at]
        next_1 = [lookup(after(i), index_1) for i in at]
        top_0 = top_1 = low_0 = low_1 = jnp.zeros((16, LANES), jnp.bfloat16)
        before = step == -1
        for j in range(TAPS):
            value_0 = jnp.where(in_0, near_0[j], next_0[j])
            value_1 = jnp.where(in_1, near_1[j], next_1[j])
            here = step == j
            top_0 = jnp.where(here, value_0, top_0)
            top_1 = jnp.where(here, value_1, top_1)
            low_0 = jnp.where(before, value_0, low_0)
            low_1 = jnp.where(before, value_1, low_1)
            before = here
        upper = weight_0 * top_0.astype(jnp.float32) + weight_1 * top_1.astype(jnp.float32)
        lower = weight_0 * low_0.astype(jnp.float32) + weight_1 * low_1.astype(jnp.float32)
        return upper + part_y * (lower - upper)

    row_groups = height // 8
    block_spans = []
    for b in range(blocks):
        spread = (b % 8) * (LANES // SP) + lax.broadcasted_iota(jnp.int32, (8, LANES), 1) // SP
        expanded = []
        for comp in range(2):
            value, rise, climb = vertex_rows[comp][b // 8]
            at = jnp.take_along_axis(value, spread, axis=1)
            low = jnp.take_along_axis(rise, spread, axis=1)
            high = jnp.take_along_axis(climb, spread, axis=1)
            expanded.append(at + along * jnp.where(left_side, low, high))
        columns = slice(b * LANES, (b + 1) * LANES)
        span = None
        for k in range(row_groups):
            moved = [
                tents[0] * ex[k : k + 1] + tents[1] * ex[k + 1 : k + 2] + tents[2] * ex[k + 2 : k + 3] for ex in expanded
            ]
            sample_x = lane_full + (moved[0] + LANES / 2.0)
            sample_y = sub + (moved[1] + float(k * 8 + height))
            rows = slice(k * 8, k * 8 + 8)
            sample_ref[0, rows, columns] = sample_x
            sample_ref[1, rows, columns] = sample_y
            floor_y = clipped_floor(sample_y)
            base = jnp.min(floor_y, axis=1, keepdims=True)
            base_ref[b, rows, :] = jnp.broadcast_to(base, (8, LANES))
            span = floor_y - base if span is None else jnp.maximum(span, floor_y - base)
        span_ref[b] = span
        spans = span if spans is None else jnp.maximum(spans, span)

    for b in range(blocks):
        columns = slice(b * LANES, (b + 1) * LANES)
        bases = [base_ref[b, k * 16 : k * 16 + 16, :] for k in range(height // 16)]
        taken_ref[b] = tap_rows(bases, slab_ref[:, b * LANES : (b + 2) * LANES])

    for b in range(blocks):
        columns = slice(b * LANES, (b + 1) * LANES)
        taken = (lambda i: taken_ref[b, i, :LANES]), (lambda i: taken_ref[b, i, LANES:])
        for k in range(height // 16):
            rows = slice(k * 16, k * 16 + 16)
            mixed_ref[rows, columns] = render(
                sample_ref[0, rows, columns], sample_ref[1, rows, columns], base_ref[b, rows, :], taken, k
            )

    @pl.when(jnp.max(spans) > TAPS - 2.0)
    def _():
        for b in range(blocks):
            widest_ref[b] = jnp.max(span_ref[b]).astype(jnp.int32)

        def rest(b, carry):
            widest = widest_ref[b]

            @pl.when(widest > TAPS - 2)
            def _():
                start = pl.multiple_of(b * LANES, LANES)
                columns = pl.ds(start, LANES)
                bases = [base_ref[b, k * 16 : k * 16 + 16, :] for k in range(height // 16)]

                def more(i, c):
                    moved_bases = [base + (i * TAPS).astype(jnp.float32) for base in bases]
                    rows_taken = tap_rows(moved_bases, slab_ref[:, pl.ds(start, 2 * LANES)])
                    taken = (lambda i: rows_taken[i, :LANES]), (lambda i: rows_taken[i, LANES:])
                    for k in range(height // 16):
                        rows = slice(k * 16, k * 16 + 16)
                        mixed_ref[rows, columns] = mixed_ref[rows, columns] + render(
                            sample_ref[0, rows, columns],
                            sample_ref[1, rows, columns],
                            base_ref[b, rows, :] + (i * TAPS).astype(jnp.float32),
                            taken,
                            k,
                        )
                    return c

                lax.fori_loop(1, (widest + 1 + TAPS) // TAPS, more, 0)

            return carry

        lax.fori_loop(0, blocks, rest, 0)

    out_ref[...] = mixed_ref[...].astype(jnp.bfloat16)


def per_device(points, source, slab_first, slab_count):
    strips = lax.axis_size("ty")
    height, width = source.shape
    tile_len = points.shape[1]
    blocks = width // LANES
    in_chip = [(i, i ^ 1) for i in range(strips)]
    across = []
    for i in range(1, strips - 1, 2):
        across.extend([(i, i + 1), (i + 1, i)])
    vmem = pl.BlockSpec(memory_space=pltpu.VMEM)
    smem = pl.BlockSpec(memory_space=pltpu.SMEM)
    anywhere = pl.BlockSpec(memory_space=pl.ANY)
    params = pltpu.CompilerParams(vmem_limit_bytes=32 * 1024 * 1024)
    small = pltpu.CompilerParams(vmem_limit_bytes=4 * 1024 * 1024)
    mate_points = lax.ppermute(points, "ty", in_chip)
    packed_rows = width // tile_len * height + 16
    packed_shape = jax.ShapeDtypeStruct((packed_rows, tile_len), jnp.bfloat16)
    tile = lax.axis_index("ty")
    cell = lax.broadcasted_iota(jnp.int32, points.shape, 1) // PC
    cell_cols = width // CELL
    origin_x = cell % cell_cols * CELL
    origin_y = tile * height + cell // cell_cols * CELL
    is_x = lax.broadcasted_iota(jnp.int32, points.shape, 0) % 2 == 0
    local = points - jnp.where(is_x, origin_x, origin_y).astype(jnp.float32)
    laid, own_rows = pl.pallas_call(
        lay_own_kernel,
        out_shape=(packed_shape, jax.ShapeDtypeStruct((8, tile_len), jnp.float32)),
        in_specs=[vmem, vmem],
        out_specs=(vmem, vmem),
        compiler_params=small,
        cost_estimate=pl.CostEstimate(flops=0, bytes_accessed=4 * source.size, transcendentals=0),
    )(local, source)
    packed = pl.pallas_call(
        functools.partial(lay_mate_kernel, height, width),
        out_shape=packed_shape,
        in_specs=[vmem, vmem, anywhere],
        out_specs=anywhere,
        input_output_aliases={2: 0},
        scratch_shapes=[pltpu.VMEM((16, tile_len), jnp.bfloat16), pltpu.SemaphoreType.DMA],
        compiler_params=small,
    )(own_rows, mate_points, laid)
    arrived = lax.ppermute(packed, "ty", across)
    mate_source = lax.ppermute(source, "ty", in_chip)
    groups = width // GROUP_PX

    def moment_scratch(sets):
        length = sets * tile_len // groups
        return [
            pltpu.VMEM((groups, 2 * NF, length), jnp.bfloat16),
            pltpu.VMEM((groups, 2 * LANES, length), jnp.bfloat16),
        ]

    totals = pl.pallas_call(
        functools.partial(near_kernel, strips, height, width),
        out_shape=jax.ShapeDtypeStruct((groups, NF, LANES), jnp.float32),
        in_specs=[vmem, vmem],
        out_specs=vmem,
        scratch_shapes=moment_scratch(2),
        compiler_params=params,
        cost_estimate=pl.CostEstimate(flops=4 * NF * LANES * 2 * tile_len * 4, bytes_accessed=10**6, transcendentals=2 * tile_len * NV),
    )(local, mate_points)
    arrived, totals = lax.optimization_barrier((arrived, totals))
    far = lax.ppermute(arrived[packed_rows - 16 : packed_rows - 8], "ty", in_chip)
    return pl.pallas_call(
        functools.partial(main_kernel, strips),
        out_shape=(
            jax.ShapeDtypeStruct((height, width), jnp.bfloat16),
            jax.ShapeDtypeStruct((6, VR, width // SP), jnp.float32),
        ),
        in_specs=[smem, smem] + [vmem] * 5,
        out_specs=(vmem, vmem),
        scratch_shapes=moment_scratch(3)
        + [
            pltpu.VMEM((LANES, width + LANES), jnp.bfloat16),
            pltpu.VMEM((2, height, width), jnp.float32),
            pltpu.VMEM((blocks, height, LANES), jnp.float32),
            pltpu.VMEM((blocks, 8, LANES), jnp.float32),
            pltpu.VMEM((blocks, TAPS * height, 2 * LANES), jnp.bfloat16),
            pltpu.VMEM((height, width), jnp.float32),
            pltpu.SMEM((blocks,), jnp.int32),
        ],
        compiler_params=params,
    )(slab_first, slab_count, totals, source, mate_source, arrived, far)


def solution(mesh):
    return jax.shard_map(
        per_device,
        mesh=mesh,
        in_specs=(
            P(None, ("sec", "ty")),
            P(("sec", "ty"), None),
            P(("sec", "ty")),
            P(("sec", "ty")),
        ),
        out_specs=(P(("sec", "ty"), None), P(None, ("sec", "ty"), None)),
        check_vma=False,
    )
```

```python
import functools

import jax
import jax.numpy as jnp
import numpy as np
from jax import lax
from jax.experimental import pallas as pl
from jax.experimental.pallas import tpu as pltpu
from jax.sharding import PartitionSpec as P

BH = 16
PC = 4
SP = 8
VR = 4
LANES = 128
CELL = 16
RIDGE_TERM = 0.01
FEATS = 12
ER = 8
NF = FEATS * ER
GROUP_PX = LANES // PC * CELL
NV = GROUP_PX // SP + 2 * LANES // SP
EXP2_SCALE = 2.0 * float(np.log2(np.e))
TAPS = 13


def fiota(shape, dim):
    return lax.broadcasted_iota(jnp.int32, shape, dim).astype(jnp.float32)


def local_points(pts, tile, cell_cols, height):
    lane = lax.broadcasted_iota(jnp.int32, (1, pts.shape[1]), 1)
    cell = lane // PC
    base_x = (cell % cell_cols * CELL).astype(jnp.float32)
    base_y = (tile * height + cell // cell_cols * CELL).astype(jnp.float32)
    fixed_x, fixed_y = pts[0:1], pts[1:2]
    return jnp.concatenate(
        [fixed_x - base_x, fixed_y - base_y, pts[2:3] - fixed_x, pts[3:4] - fixed_y], axis=0
    )


def lookup(values, index):
    numbers = lax.GatherDimensionNumbers(
        offset_dims=(),
        collapsed_slice_dims=(1,),
        start_index_map=(1,),
        operand_batching_dims=(0,),
        start_indices_batching_dims=(0,),
    )
    return lax.gather(values, index[..., None], numbers, (1, 1), mode=lax.GatherScatterMode.PROMISE_IN_BOUNDS)


def split_pair(value):
    high = value.astype(jnp.bfloat16).astype(jnp.float32)
    return high, value - high


def shifts_of(local):
    return jnp.concatenate([local[0:2], local[2:4] - local[0:2]], axis=0)


def lay_own_kernel(local_ref, source_ref, packed_ref, rows_ref):
    height, width = source_ref.shape
    half = packed_ref.shape[1]
    for part in range(width // half):
        packed_ref[part * height : (part + 1) * height, :] = source_ref[:, part * half : (part + 1) * half]
    rows_ref[...] = jnp.concatenate(split_pair(shifts_of(local_ref[...])), axis=0)


def lay_mate_kernel(height, width, own_rows_ref, mate_ref, laid_ref, packed_ref, rows_ref, sem):
    tile = lax.axis_index("ty")
    mate = split_pair(local_points(mate_ref[...], tile + 1 - 2 * (tile % 2), width // CELL, height))
    rows_ref[...] = jnp.concatenate([own_rows_ref[...], *mate], axis=0).astype(jnp.bfloat16)
    base = packed_ref.shape[0] - 16
    copy = pltpu.make_async_copy(rows_ref, packed_ref.at[base : base + 16, :], sem)
    copy.start()
    copy.wait()


def group_totals(sets, tile, strips, height, width, feat_ref, weight_ref):
    cell_cols = width // CELL
    cell_rows = height // CELL
    groups = width // GROUP_PX
    ext_row = lax.broadcasted_iota(jnp.int32, (ER, 1), 0)
    vertex_y = (fiota((ER, 1), 0) * SP + (SP / 2.0 - SP - height / 2.0)) / height
    ext_tile = tile + jnp.where(ext_row == 0, -1, jnp.where(ext_row == VR + 1, 1, 0))
    scale = float(np.sqrt(EXP2_SCALE))
    lane_px = (lax.broadcasted_iota(jnp.int32, (1, LANES), 1) // PC * CELL).astype(jnp.float32) - GROUP_PX / 2.0
    per_block = LANES // SP
    block_lanes = LANES // CELL * PC
    reach = 3 * per_block
    lane_ids = lax.broadcasted_iota(jnp.int32, (1, LANES), 1)
    block_px = (lane_ids % block_lanes // PC * CELL).astype(jnp.float32) + (LANES - SP / 2.0)
    vertex_px = fiota((reach, 1), 0) * SP
    lane_block = (lax.broadcasted_iota(jnp.int32, (per_block, LANES), 1) // block_lanes).astype(jnp.int16)
    in_block = [lane_block == j for j in range(LANES // block_lanes)]
    nothing = jnp.zeros((per_block, LANES), jnp.bfloat16)

    def spread_out(near, i):
        result = nothing
        for m in range(3):
            if 0 <= i - m < len(in_block):
                result = jnp.where(in_block[i - m], near[m * per_block : (m + 1) * per_block], result)
        return result

    zero_rows = jnp.zeros((LANES - NV, weight_ref.shape[2]), jnp.bfloat16)

    totals = []
    for g in range(groups):
        weight_ref[g, NV:LANES, :] = zero_rows
        weight_ref[g, LANES + NV :, :] = zero_rows
        for s, (pts, owner) in enumerate(sets):
            usable = (jnp.abs(owner - ext_tile) <= 1) & (owner >= 0) & (owner < strips)
            usable = usable.astype(jnp.float32)
            for c in range(cell_rows):
                lanes = slice(c * cell_cols * PC + g * LANES, c * cell_cols * PC + (g + 1) * LANES)
                chunk = slice((s * cell_rows + c) * LANES, (s * cell_rows + c + 1) * LANES)
                px = (pts[0:1, lanes] + lane_px) / height
                py = (pts[1:2, lanes] + ((owner - tile) * height + c * CELL).astype(jnp.float32)) / height - 0.5
                dx = pts[2:3, lanes] / height
                dy = pts[3:4, lanes] / height
                gap_y = (py - vertex_y) * scale
                wy = jnp.exp2(-(gap_y * gap_y)) * usable
                wpx, wpy, wdx, wdy = wy * px, wy * py, wy * dx, wy * dy
                rows = (wy, wpx, wpy, wdx, wdy, wpx * px, wpx * py, wpy * py, wdx * px, wdx * py, wdy * px, wdy * py)
                for f in range(0, FEATS, 2):
                    high, low = split_pair(jnp.concatenate(rows[f : f + 2], axis=0))
                    feat_ref[g, f * ER : (f + 2) * ER, chunk] = high.astype(jnp.bfloat16)
                    feat_ref[g, NF + f * ER : NF + (f + 2) * ER, chunk] = low.astype(jnp.bfloat16)
                gap_x = (pts[0:1, lanes] + block_px - vertex_px) * (scale / height)
                high, low = split_pair(jnp.exp2(-(gap_x * gap_x)))
                for row, near in ((0, high.astype(jnp.bfloat16)), (LANES, low.astype(jnp.bfloat16))):
                    for i in range(NV // per_block):
                        start = row + i * per_block
                        weight_ref[g, start : start + per_block, chunk] = spread_out(near, i)
        both = lax.dot_general(
            feat_ref[g], weight_ref[g], (((1,), (1,)), ((), ())), preferred_element_type=jnp.float32
        )
        both = both[:NF] + both[NF:]
        totals.append(both[:, :LANES] + both[:, LANES:])
    return totals


def near_kernel(strips, height, width, own_ref, mate_ref, totals_ref, feat_ref, weight_ref):
    tile = lax.axis_index("ty")
    mate = tile + 1 - 2 * (tile % 2)
    cell_cols = width // CELL
    sets = (
        (shifts_of(own_ref[...]), tile),
        (local_points(mate_ref[...], mate, cell_cols, height), mate),
    )
    for g, value in enumerate(group_totals(sets, tile, strips, height, width, feat_ref, weight_ref)):
        totals_ref[g] = value


def main_kernel(
    strips,
    first_ref,
    count_ref,
    totals_ref,
    source_ref,
    mate_source_ref,
    packed_ref,
    far_ref,
    out_ref,
    affine_ref,
    feat_ref,
    weight_ref,
    slab_ref,
    sample_ref,
    base_ref,
    span_ref,
    taken_ref,
    mixed_ref,
    widest_ref,
):
    height, width = source_ref.shape
    groups = width // GROUP_PX
    blocks = width // LANES
    halves = blocks // 8
    tile = lax.axis_index("ty")
    odd = tile % 2
    toward = 1 - 2 * odd
    partner = tile - toward
    partner_mate = tile - 2 * toward
    beyond = tile + 2 * toward

    slots_from = first_ref[0] * BH - (tile - 1) * height
    slots_to = slots_from + count_ref[0] * BH
    left_half = lax.broadcasted_iota(jnp.int32, (1, LANES), 1) < LANES // 2
    half_cols = packed_ref.shape[1]
    slab_ref[3 * height :, :] = jnp.zeros((slab_ref.shape[0] - 3 * height, slab_ref.shape[1]), jnp.bfloat16)

    def place(load, row_start, chunk):
        local = row_start + chunk * 16
        row = lax.broadcasted_iota(jnp.int32, (16, 1), 0) + local
        live = ((row >= slots_from) & (row < slots_to)).astype(jnp.float32)
        before = jnp.zeros((16, LANES), jnp.float32)
        for b in range(blocks + 1):
            if b < blocks:
                now = pltpu.roll(load(b).astype(jnp.float32) * live, LANES // 2, axis=1)
            else:
                now = jnp.zeros((16, LANES), jnp.float32)
            merged = jnp.where(left_half, before, now).astype(jnp.bfloat16)
            slab_ref[pl.ds(pl.multiple_of(local, 16), 16), b * LANES : (b + 1) * LANES] = merged
            before = now

    for chunk in range(height // 16):
        rows = slice(chunk * 16, chunk * 16 + 16)
        place(lambda b: source_ref[rows, b * LANES : (b + 1) * LANES], height, chunk)
        place(lambda b: mate_source_ref[rows, b * LANES : (b + 1) * LANES], height + toward * height, chunk)

        def from_packed(b):
            part = b * LANES // half_cols
            lane = b * LANES - part * half_cols
            return packed_ref[part * height + chunk * 16 : part * height + chunk * 16 + 16, lane : lane + LANES]

        place(from_packed, height - toward * height, chunk)

    point_rows = packed_ref[packed_ref.shape[0] - 16 :, :].astype(jnp.float32)
    far_rows = far_ref[...].astype(jnp.float32)
    sets = (
        (point_rows[0:4] + point_rows[4:8], partner),
        (point_rows[8:12] + point_rows[12:16], partner_mate),
        (far_rows[0:4] + far_rows[4:8], beyond),
    )
    vertex_y = (fiota((ER, 1), 0) * SP + (SP / 2.0 - SP - height / 2.0)) / height
    totals = group_totals(sets, tile, strips, height, width, feat_ref, weight_ref)
    totals = [totals[g] + totals_ref[g] for g in range(groups)]

    lane = lax.broadcasted_iota(jnp.int32, (1, LANES), 1)
    per_group = GROUP_PX // SP
    affines = []
    for h in range(halves):
        moments = None
        vertex_group = 2 * h + lane // per_group
        for g in range(groups):
            start = g * per_group - LANES // SP - h * LANES
            if start + NV <= 0 or start >= LANES:
                continue
            part = pltpu.roll(totals[g], start % LANES, axis=1)
            inside = ((lane >= start) & (lane < start + NV)).astype(jnp.float32)
            move = ((g - vertex_group) * (GROUP_PX // height)).astype(jnp.float32)
            part = [part[f * ER : (f + 1) * ER] * inside for f in range(FEATS)]
            part[5] = part[5] + move * (2.0 * part[1] + move * part[0])
            part[6] = part[6] + move * part[2]
            part[8] = part[8] + move * part[3]
            part[10] = part[10] + move * part[4]
            part[1] = part[1] + move * part[0]
            moments = part if moments is None else [x + y for x, y in zip(moments, part)]
        inverse = 1.0 / moments[0]
        mean_px, mean_py, mean_dx, mean_dy = [moments[i] * inverse for i in range(1, 5)]
        cov_xx = moments[5] * inverse - mean_px * mean_px + RIDGE_TERM
        cov_xy = moments[6] * inverse - mean_px * mean_py
        cov_yy = moments[7] * inverse - mean_py * mean_py + RIDGE_TERM
        cross_xx = moments[8] * inverse - mean_dx * mean_px - RIDGE_TERM
        cross_xy = moments[9] * inverse - mean_dx * mean_py
        cross_yx = moments[10] * inverse - mean_dy * mean_px
        cross_yy = moments[11] * inverse - mean_dy * mean_py - RIDGE_TERM
        over = 1.0 / (cov_xx * cov_yy - cov_xy * cov_xy)
        lin_xx = (cross_xx * cov_yy - cross_xy * cov_xy) * over
        lin_xy = (cross_xy * cov_xx - cross_xx * cov_xy) * over
        lin_yx = (cross_yx * cov_yy - cross_yy * cov_xy) * over
        lin_yy = (cross_yy * cov_xx - cross_yx * cov_xy) * over
        vertex_x = ((lane % per_group * SP).astype(jnp.float32) + (SP - GROUP_PX) / 2.0) / height
        delta_x = vertex_x - mean_px
        delta_y = vertex_y - mean_py
        shift_x = mean_dx + lin_xx * delta_x + lin_xy * delta_y
        shift_y = mean_dy + lin_yx * delta_x + lin_yy * delta_y
        results = (lin_xx + 1.0, lin_xy, lin_yx, lin_yy + 1.0, shift_x, shift_y)
        for i, value in enumerate(results):
            affine_ref[i, :, h * LANES : (h + 1) * LANES] = value[1 : VR + 1]
        affines.append((shift_x, shift_y))

    ext = lax.broadcasted_iota(jnp.int32, (ER, LANES), 0)
    along = (lane % SP).astype(jnp.float32) / SP - 0.5
    left_side = along < 0.0
    vertex_rows = []
    for comp in range(2):
        rows = []
        for h in range(halves):
            value = affines[h][comp] * float(height)
            value = jnp.where((ext == 0) & (tile == 0), jnp.broadcast_to(value[1:2], value.shape), value)
            value = jnp.where((ext == VR + 1) & (tile == strips - 1), jnp.broadcast_to(value[VR : VR + 1], value.shape), value)
            rows.append(value)
        steps = []
        for h in range(halves):
            value = rows[h]
            first = jnp.broadcast_to(rows[h - 1][:, LANES - 1 :] if h > 0 else value[:, :1], value.shape)
            last = jnp.broadcast_to(rows[h + 1][:, :1] if h + 1 < halves else value[:, LANES - 1 :], value.shape)
            before = jnp.where(lane == 0, first, pltpu.roll(value, 1, axis=1))
            after = jnp.where(lane == LANES - 1, last, pltpu.roll(value, LANES - 1, axis=1))
            steps.append((value, value - before, after - value))
        vertex_rows.append(steps)

    sub = lax.broadcasted_iota(jnp.int32, (8, LANES), 0).astype(jnp.float32)
    lane_full = fiota((8, LANES), 1)
    tents = (
        jnp.maximum(0.0, 0.5 - sub / SP),
        1.0 - jnp.abs(sub - SP / 2.0) / SP,
        jnp.maximum(0.0, sub / SP - 0.5),
    )
    last_row = 3.0 * height
    spans = None

    def clipped_floor(sample_y):
        return jnp.clip(jnp.floor(sample_y), -2.0, last_row)

    lanes_16 = fiota((16, LANES), 1)

    def tap_rows(bases, slab):
        away = [(lanes_16 - base).astype(jnp.int32).astype(jnp.int16) for base in bases]
        one, none = jnp.ones((16, LANES), jnp.bfloat16), jnp.zeros((16, LANES), jnp.bfloat16)
        picks = [jnp.where(gap == j, one, none) for j in range(TAPS) for gap in away]
        return jnp.dot(jnp.concatenate(picks, axis=0), slab, preferred_element_type=jnp.float32).astype(jnp.bfloat16)

    def render(sample_x, sample_y, base, taken, k):
        floor_x = jnp.floor(sample_x)
        part_x = sample_x - floor_x
        part_y = sample_y - jnp.floor(sample_y)
        floor_x = jnp.clip(floor_x, -2.0, 2.0 * LANES)
        weight_0 = jnp.where((floor_x >= 0.0) & (floor_x < 2.0 * LANES), 1.0 - part_x, 0.0)
        weight_1 = jnp.where((floor_x >= -1.0) & (floor_x < 2.0 * LANES - 1.0), part_x, 0.0)
        index = floor_x.astype(jnp.int32)
        index_0 = (index & (LANES - 1)).astype(jnp.int16)
        index_1 = ((index + 1) & (LANES - 1)).astype(jnp.int16)
        index = index.astype(jnp.int16)
        in_0 = index < LANES
        in_1 = index < LANES - 1
        step = (clipped_floor(sample_y) - base).astype(jnp.int32).astype(jnp.int16)
        near, after = taken
        at = [slice(j * height + k * 16, j * height + k * 16 + 16) for j in range(TAPS)]
        near_0 = [lookup(near(i), index_0) for i in at]
        next_0 = [lookup(after(i), index_0) for i in at]
        near_1 = [lookup(near(i), index_1) for i in at]
        next_1 = [lookup(after(i), index_1) for i in at]
        top_0 = top_1 = low_0 = low_1 = jnp.zeros((16, LANES), jnp.bfloat16)
        before = step == -1
        for j in range(TAPS):
            value_0 = jnp.where(in_0, near_0[j], next_0[j])
            value_1 = jnp.where(in_1, near_1[j], next_1[j])
            here = step == j
            top_0 = jnp.where(here, value_0, top_0)
            top_1 = jnp.where(here, value_1, top_1)
            low_0 = jnp.where(before, value_0, low_0)
            low_1 = jnp.where(before, value_1, low_1)
            before = here
        upper = weight_0 * top_0.astype(jnp.float32) + weight_1 * top_1.astype(jnp.float32)
        lower = weight_0 * low_0.astype(jnp.float32) + weight_1 * low_1.astype(jnp.float32)
        return upper + part_y * (lower - upper)

    row_groups = height // 8
    block_spans = []
    for b in range(blocks):
        spread = (b % 8) * (LANES // SP) + lax.broadcasted_iota(jnp.int32, (8, LANES), 1) // SP
        expanded = []
        for comp in range(2):
            value, rise, climb = vertex_rows[comp][b // 8]
            at = jnp.take_along_axis(value, spread, axis=1)
            low = jnp.take_along_axis(rise, spread, axis=1)
            high = jnp.take_along_axis(climb, spread, axis=1)
            expanded.append(at + along * jnp.where(left_side, low, high))
        columns = slice(b * LANES, (b + 1) * LANES)
        span = None
        for k in range(row_groups):
            moved = [
                tents[0] * ex[k : k + 1] + tents[1] * ex[k + 1 : k + 2] + tents[2] * ex[k + 2 : k + 3] for ex in expanded
            ]
            sample_x = lane_full + (moved[0] + LANES / 2.0)
            sample_y = sub + (moved[1] + float(k * 8 + height))
            rows = slice(k * 8, k * 8 + 8)
            sample_ref[0, rows, columns] = sample_x
            sample_ref[1, rows, columns] = sample_y
            floor_y = clipped_floor(sample_y)
            base = jnp.min(floor_y, axis=1, keepdims=True)
            base_ref[b, rows, :] = jnp.broadcast_to(base, (8, LANES))
            span = floor_y - base if span is None else jnp.maximum(span, floor_y - base)
        span_ref[b] = span
        spans = span if spans is None else jnp.maximum(spans, span)

    for b in range(blocks):
        columns = slice(b * LANES, (b + 1) * LANES)
        bases = [base_ref[b, k * 16 : k * 16 + 16, :] for k in range(height // 16)]
        taken_ref[b] = tap_rows(bases, slab_ref[:, b * LANES : (b + 2) * LANES])

    for b in range(blocks):
        columns = slice(b * LANES, (b + 1) * LANES)
        taken = (lambda i: taken_ref[b, i, :LANES]), (lambda i: taken_ref[b, i, LANES:])
        for k in range(height // 16):
            rows = slice(k * 16, k * 16 + 16)
            mixed_ref[rows, columns] = render(
                sample_ref[0, rows, columns], sample_ref[1, rows, columns], base_ref[b, rows, :], taken, k
            )

    @pl.when(jnp.max(spans) > TAPS - 2.0)
    def _():
        for b in range(blocks):
            widest_ref[b] = jnp.max(span_ref[b]).astype(jnp.int32)

        def rest(b, carry):
            widest = widest_ref[b]

            @pl.when(widest > TAPS - 2)
            def _():
                start = pl.multiple_of(b * LANES, LANES)
                columns = pl.ds(start, LANES)
                bases = [base_ref[b, k * 16 : k * 16 + 16, :] for k in range(height // 16)]

                def more(i, c):
                    moved_bases = [base + (i * TAPS).astype(jnp.float32) for base in bases]
                    rows_taken = tap_rows(moved_bases, slab_ref[:, pl.ds(start, 2 * LANES)])
                    taken = (lambda i: rows_taken[i, :LANES]), (lambda i: rows_taken[i, LANES:])
                    for k in range(height // 16):
                        rows = slice(k * 16, k * 16 + 16)
                        mixed_ref[rows, columns] = mixed_ref[rows, columns] + render(
                            sample_ref[0, rows, columns],
                            sample_ref[1, rows, columns],
                            base_ref[b, rows, :] + (i * TAPS).astype(jnp.float32),
                            taken,
                            k,
                        )
                    return c

                lax.fori_loop(1, (widest + 1 + TAPS) // TAPS, more, 0)

            return carry

        lax.fori_loop(0, blocks, rest, 0)

    out_ref[...] = mixed_ref[...].astype(jnp.bfloat16)


def per_device(points, source, slab_first, slab_count):
    strips = lax.axis_size("ty")
    height, width = source.shape
    tile_len = points.shape[1]
    blocks = width // LANES
    in_chip = [(i, i ^ 1) for i in range(strips)]
    across = []
    for i in range(1, strips - 1, 2):
        across.extend([(i, i + 1), (i + 1, i)])
    vmem = pl.BlockSpec(memory_space=pltpu.VMEM)
    smem = pl.BlockSpec(memory_space=pltpu.SMEM)
    anywhere = pl.BlockSpec(memory_space=pl.ANY)
    params = pltpu.CompilerParams(vmem_limit_bytes=32 * 1024 * 1024)
    small = pltpu.CompilerParams(vmem_limit_bytes=4 * 1024 * 1024)
    mate_points = lax.ppermute(points, "ty", in_chip)
    packed_rows = width // tile_len * height + 16
    packed_shape = jax.ShapeDtypeStruct((packed_rows, tile_len), jnp.bfloat16)
    tile = lax.axis_index("ty")
    cell = lax.broadcasted_iota(jnp.int32, points.shape, 1) // PC
    cell_cols = width // CELL
    origin_x = cell % cell_cols * CELL
    origin_y = tile * height + cell // cell_cols * CELL
    is_x = lax.broadcasted_iota(jnp.int32, points.shape, 0) % 2 == 0
    local = points - jnp.where(is_x, origin_x, origin_y).astype(jnp.float32)
    laid, own_rows = pl.pallas_call(
        lay_own_kernel,
        out_shape=(packed_shape, jax.ShapeDtypeStruct((8, tile_len), jnp.float32)),
        in_specs=[vmem, vmem],
        out_specs=(vmem, vmem),
        compiler_params=small,
        cost_estimate=pl.CostEstimate(flops=0, bytes_accessed=4 * source.size, transcendentals=0),
    )(local, source)
    packed = pl.pallas_call(
        functools.partial(lay_mate_kernel, height, width),
        out_shape=packed_shape,
        in_specs=[vmem, vmem, anywhere],
        out_specs=anywhere,
        input_output_aliases={2: 0},
        scratch_shapes=[pltpu.VMEM((16, tile_len), jnp.bfloat16), pltpu.SemaphoreType.DMA],
        compiler_params=small,
    )(own_rows, mate_points, laid)
    arrived = lax.ppermute(packed, "ty", across)
    mate_source = lax.ppermute(source, "ty", in_chip)
    groups = width // GROUP_PX

    def moment_scratch(sets):
        length = sets * tile_len // groups
        return [
            pltpu.VMEM((groups, 2 * NF, length), jnp.bfloat16),
            pltpu.VMEM((groups, 2 * LANES, length), jnp.bfloat16),
        ]

    totals = pl.pallas_call(
        functools.partial(near_kernel, strips, height, width),
        out_shape=jax.ShapeDtypeStruct((groups, NF, LANES), jnp.float32),
        in_specs=[vmem, vmem],
        out_specs=vmem,
        scratch_shapes=moment_scratch(2),
        compiler_params=params,
        cost_estimate=pl.CostEstimate(flops=4 * NF * LANES * 2 * tile_len * 4, bytes_accessed=10**6, transcendentals=2 * tile_len * NV),
    )(local, mate_points)
    arrived, totals = lax.optimization_barrier((arrived, totals))
    far = lax.ppermute(arrived[packed_rows - 16 : packed_rows - 8], "ty", in_chip)
    return pl.pallas_call(
        functools.partial(main_kernel, strips),
        out_shape=(
            jax.ShapeDtypeStruct((height, width), jnp.bfloat16),
            jax.ShapeDtypeStruct((6, VR, width // SP), jnp.float32),
        ),
        in_specs=[smem, smem] + [vmem] * 5,
        out_specs=(vmem, vmem),
        scratch_shapes=moment_scratch(3)
        + [
            pltpu.VMEM((LANES, width + LANES), jnp.bfloat16),
            pltpu.VMEM((2, height, width), jnp.float32),
            pltpu.VMEM((blocks, height, LANES), jnp.float32),
            pltpu.VMEM((blocks, 8, LANES), jnp.float32),
            pltpu.VMEM((blocks, TAPS * height, 2 * LANES), jnp.bfloat16),
            pltpu.VMEM((height, width), jnp.float32),
            pltpu.SMEM((blocks,), jnp.int32),
        ],
        compiler_params=params,
    )(slab_first, slab_count, totals, source, mate_source, arrived, far)


def solution(mesh):
    return jax.shard_map(
        per_device,
        mesh=mesh,
        in_specs=(
            P(None, ("sec", "ty")),
            P(("sec", "ty"), None),
            P(("sec", "ty")),
            P(("sec", "ty")),
        ),
        out_specs=(P(("sec", "ty"), None), P(None, ("sec", "ty"), None)),
        check_vma=False,
    )
```

```python
import functools

import jax
import jax.numpy as jnp
import numpy as np
from jax import lax
from jax.experimental import pallas as pl
from jax.experimental.pallas import tpu as pltpu
from jax.sharding import PartitionSpec as P

BH = 16
PC = 4
SP = 8
VR = 4
LANES = 128
CELL = 16
RIDGE_TERM = 0.01
FEATS = 12
ER = 8
NF = FEATS * ER
GROUP_PX = LANES // PC * CELL
NV = GROUP_PX // SP + 2 * LANES // SP
EXP2_SCALE = 2.0 * float(np.log2(np.e))
TAPS = 12
PIECE = 4


def fiota(shape, dim):
    return lax.broadcasted_iota(jnp.int32, shape, dim).astype(jnp.float32)


def local_points(pts, tile, cell_cols, height):
    lane = lax.broadcasted_iota(jnp.int32, (1, pts.shape[1]), 1)
    cell = lane // PC
    base_x = (cell % cell_cols * CELL).astype(jnp.float32)
    base_y = (tile * height + cell // cell_cols * CELL).astype(jnp.float32)
    fixed_x, fixed_y = pts[0:1], pts[1:2]
    return jnp.concatenate(
        [fixed_x - base_x, fixed_y - base_y, pts[2:3] - fixed_x, pts[3:4] - fixed_y], axis=0
    )


def lookup(values, index):
    numbers = lax.GatherDimensionNumbers(
        offset_dims=(),
        collapsed_slice_dims=(1,),
        start_index_map=(1,),
        operand_batching_dims=(0,),
        start_indices_batching_dims=(0,),
    )
    return lax.gather(values, index[..., None], numbers, (1, 1), mode=lax.GatherScatterMode.PROMISE_IN_BOUNDS)


def split_pair(value):
    high = value.astype(jnp.bfloat16).astype(jnp.float32)
    return high, value - high


def shifts_of(local):
    return jnp.concatenate([local[0:2], local[2:4] - local[0:2]], axis=0)


def lay_own_kernel(local_ref, source_ref, packed_ref, rows_ref):
    height, width = source_ref.shape
    half = packed_ref.shape[1]
    for part in range(width // half):
        packed_ref[part * height : (part + 1) * height, :] = source_ref[:, part * half : (part + 1) * half]
    rows_ref[...] = jnp.concatenate(split_pair(shifts_of(local_ref[...])), axis=0)


def lay_mate_kernel(height, width, own_rows_ref, mate_ref, laid_ref, packed_ref, rows_ref, sem):
    tile = lax.axis_index("ty")
    mate = split_pair(local_points(mate_ref[...], tile + 1 - 2 * (tile % 2), width // CELL, height))
    rows_ref[...] = jnp.concatenate([own_rows_ref[...], *mate], axis=0).astype(jnp.bfloat16)
    base = packed_ref.shape[0] - 16
    copy = pltpu.make_async_copy(rows_ref, packed_ref.at[base : base + 16, :], sem)
    copy.start()
    copy.wait()


def group_totals(sets, tile, strips, height, width, feat_ref, weight_ref):
    cell_cols = width // CELL
    cell_rows = height // CELL
    groups = width // GROUP_PX
    ext_row = lax.broadcasted_iota(jnp.int32, (ER, 1), 0)
    vertex_y = (fiota((ER, 1), 0) * SP + (SP / 2.0 - SP - height / 2.0)) / height
    ext_tile = tile + jnp.where(ext_row == 0, -1, jnp.where(ext_row == VR + 1, 1, 0))
    scale = float(np.sqrt(EXP2_SCALE))
    lane_px = (lax.broadcasted_iota(jnp.int32, (1, LANES), 1) // PC * CELL).astype(jnp.float32) - GROUP_PX / 2.0
    per_block = LANES // SP
    block_lanes = LANES // CELL * PC
    reach = 3 * per_block
    lane_ids = lax.broadcasted_iota(jnp.int32, (1, LANES), 1)
    block_px = (lane_ids % block_lanes // PC * CELL).astype(jnp.float32) + (LANES - SP / 2.0)
    vertex_px = fiota((reach, 1), 0) * SP
    lane_block = (lax.broadcasted_iota(jnp.int32, (per_block, LANES), 1) // block_lanes).astype(jnp.int16)
    in_block = [lane_block == j for j in range(LANES // block_lanes)]
    nothing = jnp.zeros((per_block, LANES), jnp.bfloat16)

    def spread_out(near, i):
        result = nothing
        for m in range(3):
            if 0 <= i - m < len(in_block):
                result = jnp.where(in_block[i - m], near[m * per_block : (m + 1) * per_block], result)
        return result

    zero_rows = jnp.zeros((LANES - NV, weight_ref.shape[2]), jnp.bfloat16)

    totals = []
    for g in range(groups):
        weight_ref[g, NV:LANES, :] = zero_rows
        weight_ref[g, LANES + NV :, :] = zero_rows
        for s, (pts, owner) in enumerate(sets):
            usable = (jnp.abs(owner - ext_tile) <= 1) & (owner >= 0) & (owner < strips)
            usable = usable.astype(jnp.float32)
            for c in range(cell_rows):
                lanes = slice(c * cell_cols * PC + g * LANES, c * cell_cols * PC + (g + 1) * LANES)
                chunk = slice((s * cell_rows + c) * LANES, (s * cell_rows + c + 1) * LANES)
                px = (pts[0:1, lanes] + lane_px) / height
                py = (pts[1:2, lanes] + ((owner - tile) * height + c * CELL).astype(jnp.float32)) / height - 0.5
                dx = pts[2:3, lanes] / height
                dy = pts[3:4, lanes] / height
                gap_y = (py - vertex_y) * scale
                wy = jnp.exp2(-(gap_y * gap_y)) * usable
                wpx, wpy, wdx, wdy = wy * px, wy * py, wy * dx, wy * dy
                rows = (wy, wpx, wpy, wdx, wdy, wpx * px, wpx * py, wpy * py, wdx * px, wdx * py, wdy * px, wdy * py)
                for f in range(0, FEATS, 2):
                    high, low = split_pair(jnp.concatenate(rows[f : f + 2], axis=0))
                    feat_ref[g, f * ER : (f + 2) * ER, chunk] = high.astype(jnp.bfloat16)
                    feat_ref[g, NF + f * ER : NF + (f + 2) * ER, chunk] = low.astype(jnp.bfloat16)
                gap_x = (pts[0:1, lanes] + block_px - vertex_px) * (scale / height)
                high, low = split_pair(jnp.exp2(-(gap_x * gap_x)))
                for row, near in ((0, high.astype(jnp.bfloat16)), (LANES, low.astype(jnp.bfloat16))):
                    for i in range(NV // per_block):
                        start = row + i * per_block
                        weight_ref[g, start : start + per_block, chunk] = spread_out(near, i)
        both = lax.dot_general(
            feat_ref[g], weight_ref[g], (((1,), (1,)), ((), ())), preferred_element_type=jnp.float32
        )
        both = both[:NF] + both[NF:]
        totals.append(both[:, :LANES] + both[:, LANES:])
    return totals


def near_kernel(strips, height, width, own_ref, mate_ref, totals_ref, feat_ref, weight_ref):
    tile = lax.axis_index("ty")
    mate = tile + 1 - 2 * (tile % 2)
    cell_cols = width // CELL
    sets = (
        (shifts_of(own_ref[...]), tile),
        (local_points(mate_ref[...], mate, cell_cols, height), mate),
    )
    for g, value in enumerate(group_totals(sets, tile, strips, height, width, feat_ref, weight_ref)):
        totals_ref[g] = value


def main_kernel(
    strips,
    first_ref,
    count_ref,
    totals_ref,
    source_ref,
    mate_source_ref,
    packed_ref,
    far_ref,
    out_ref,
    affine_ref,
    feat_ref,
    weight_ref,
    slab_ref,
    sample_ref,
    base_ref,
    span_ref,
    taken_ref,
    mixed_ref,
    image_ref,
    fit_ref,
    widest_ref,
    sems,
):
    height, width = source_ref.shape
    groups = width // GROUP_PX
    blocks = width // LANES
    halves = blocks // 8
    tile = lax.axis_index("ty")
    odd = tile % 2
    toward = 1 - 2 * odd
    partner = tile - toward
    partner_mate = tile - 2 * toward
    beyond = tile + 2 * toward

    slots_from = first_ref[0] * BH - (tile - 1) * height
    slots_to = slots_from + count_ref[0] * BH
    left_half = lax.broadcasted_iota(jnp.int32, (1, LANES), 1) < LANES // 2
    half_cols = packed_ref.shape[1]
    slab_ref[3 * height :, :] = jnp.zeros((slab_ref.shape[0] - 3 * height, slab_ref.shape[1]), jnp.bfloat16)

    def place(load, row_start, chunk):
        local = row_start + chunk * 16
        row = lax.broadcasted_iota(jnp.int32, (16, 1), 0) + local
        live = ((row >= slots_from) & (row < slots_to)).astype(jnp.float32)
        before = jnp.zeros((16, LANES), jnp.float32)
        for b in range(blocks + 1):
            if b < blocks:
                now = pltpu.roll(load(b).astype(jnp.float32) * live, LANES // 2, axis=1)
            else:
                now = jnp.zeros((16, LANES), jnp.float32)
            merged = jnp.where(left_half, before, now).astype(jnp.bfloat16)
            slab_ref[pl.ds(pl.multiple_of(local, 16), 16), b * LANES : (b + 1) * LANES] = merged
            before = now

    for chunk in range(height // 16):
        rows = slice(chunk * 16, chunk * 16 + 16)
        place(lambda b: source_ref[rows, b * LANES : (b + 1) * LANES], height, chunk)
        place(lambda b: mate_source_ref[rows, b * LANES : (b + 1) * LANES], height + toward * height, chunk)

        def from_packed(b):
            part = b * LANES // half_cols
            lane = b * LANES - part * half_cols
            return packed_ref[part * height + chunk * 16 : part * height + chunk * 16 + 16, lane : lane + LANES]

        place(from_packed, height - toward * height, chunk)

    point_rows = packed_ref[packed_ref.shape[0] - 16 :, :].astype(jnp.float32)
    far_rows = far_ref[...].astype(jnp.float32)
    sets = (
        (point_rows[0:4] + point_rows[4:8], partner),
        (point_rows[8:12] + point_rows[12:16], partner_mate),
        (far_rows[0:4] + far_rows[4:8], beyond),
    )
    vertex_y = (fiota((ER, 1), 0) * SP + (SP / 2.0 - SP - height / 2.0)) / height
    totals = group_totals(sets, tile, strips, height, width, feat_ref, weight_ref)
    totals = [totals[g] + totals_ref[g] for g in range(groups)]

    lane = lax.broadcasted_iota(jnp.int32, (1, LANES), 1)
    per_group = GROUP_PX // SP
    affines = []
    for h in range(halves):
        moments = None
        vertex_group = 2 * h + lane // per_group
        for g in range(groups):
            start = g * per_group - LANES // SP - h * LANES
            if start + NV <= 0 or start >= LANES:
                continue
            part = pltpu.roll(totals[g], start % LANES, axis=1)
            inside = ((lane >= start) & (lane < start + NV)).astype(jnp.float32)
            move = ((g - vertex_group) * (GROUP_PX // height)).astype(jnp.float32)
            part = [part[f * ER : (f + 1) * ER] * inside for f in range(FEATS)]
            part[5] = part[5] + move * (2.0 * part[1] + move * part[0])
            part[6] = part[6] + move * part[2]
            part[8] = part[8] + move * part[3]
            part[10] = part[10] + move * part[4]
            part[1] = part[1] + move * part[0]
            moments = part if moments is None else [x + y for x, y in zip(moments, part)]
        inverse = 1.0 / moments[0]
        mean_px, mean_py, mean_dx, mean_dy = [moments[i] * inverse for i in range(1, 5)]
        cov_xx = moments[5] * inverse - mean_px * mean_px + RIDGE_TERM
        cov_xy = moments[6] * inverse - mean_px * mean_py
        cov_yy = moments[7] * inverse - mean_py * mean_py + RIDGE_TERM
        cross_xx = moments[8] * inverse - mean_dx * mean_px - RIDGE_TERM
        cross_xy = moments[9] * inverse - mean_dx * mean_py
        cross_yx = moments[10] * inverse - mean_dy * mean_px
        cross_yy = moments[11] * inverse - mean_dy * mean_py - RIDGE_TERM
        over = 1.0 / (cov_xx * cov_yy - cov_xy * cov_xy)
        lin_xx = (cross_xx * cov_yy - cross_xy * cov_xy) * over
        lin_xy = (cross_xy * cov_xx - cross_xx * cov_xy) * over
        lin_yx = (cross_yx * cov_yy - cross_yy * cov_xy) * over
        lin_yy = (cross_yy * cov_xx - cross_yx * cov_xy) * over
        vertex_x = ((lane % per_group * SP).astype(jnp.float32) + (SP - GROUP_PX) / 2.0) / height
        delta_x = vertex_x - mean_px
        delta_y = vertex_y - mean_py
        shift_x = mean_dx + lin_xx * delta_x + lin_xy * delta_y
        shift_y = mean_dy + lin_yx * delta_x + lin_yy * delta_y
        results = (lin_xx + 1.0, lin_xy, lin_yx, lin_yy + 1.0, shift_x, shift_y)
        for i, value in enumerate(results):
            fit_ref[i, :, h * LANES : (h + 1) * LANES] = value[1 : VR + 1]
        affines.append((shift_x, shift_y))

    fit_copy = pltpu.make_async_copy(fit_ref, affine_ref, sems.at[0])
    fit_copy.start()

    ext = lax.broadcasted_iota(jnp.int32, (ER, LANES), 0)
    along = (lane % SP).astype(jnp.float32) / SP - 0.5
    left_side = along < 0.0
    vertex_rows = []
    for comp in range(2):
        rows = []
        for h in range(halves):
            value = affines[h][comp] * float(height)
            value = jnp.where((ext == 0) & (tile == 0), jnp.broadcast_to(value[1:2], value.shape), value)
            value = jnp.where((ext == VR + 1) & (tile == strips - 1), jnp.broadcast_to(value[VR : VR + 1], value.shape), value)
            rows.append(value)
        steps = []
        for h in range(halves):
            value = rows[h]
            first = jnp.broadcast_to(rows[h - 1][:, LANES - 1 :] if h > 0 else value[:, :1], value.shape)
            last = jnp.broadcast_to(rows[h + 1][:, :1] if h + 1 < halves else value[:, LANES - 1 :], value.shape)
            before = jnp.where(lane == 0, first, pltpu.roll(value, 1, axis=1))
            after = jnp.where(lane == LANES - 1, last, pltpu.roll(value, LANES - 1, axis=1))
            steps.append((value, value - before, after - value))
        vertex_rows.append(steps)

    sub = lax.broadcasted_iota(jnp.int32, (8, LANES), 0).astype(jnp.float32)
    lane_full = fiota((8, LANES), 1)
    tents = (
        jnp.maximum(0.0, 0.5 - sub / SP),
        1.0 - jnp.abs(sub - SP / 2.0) / SP,
        jnp.maximum(0.0, sub / SP - 0.5),
    )
    last_row = 3.0 * height
    spans = None

    def clipped_floor(sample_y):
        return jnp.clip(jnp.floor(sample_y), -2.0, last_row)

    lanes_16 = fiota((16, LANES), 1)

    def tap_rows(bases, slab):
        away = [(lanes_16 - base).astype(jnp.int32).astype(jnp.int16) for base in bases]
        one, none = jnp.ones((16, LANES), jnp.bfloat16), jnp.zeros((16, LANES), jnp.bfloat16)
        picks = [jnp.where(gap == j, one, none) for j in range(TAPS) for gap in away]
        return jnp.dot(jnp.concatenate(picks, axis=0), slab, preferred_element_type=jnp.float32).astype(jnp.bfloat16)

    def render(sample_x, sample_y, base, taken, k):
        floor_x = jnp.floor(sample_x)
        part_x = sample_x - floor_x
        part_y = sample_y - jnp.floor(sample_y)
        floor_x = jnp.clip(floor_x, -2.0, 2.0 * LANES)
        weight_0 = jnp.where((floor_x >= 0.0) & (floor_x < 2.0 * LANES), 1.0 - part_x, 0.0)
        weight_1 = jnp.where((floor_x >= -1.0) & (floor_x < 2.0 * LANES - 1.0), part_x, 0.0)
        index = floor_x.astype(jnp.int32)
        index_0 = (index & (LANES - 1)).astype(jnp.int16)
        index_1 = ((index + 1) & (LANES - 1)).astype(jnp.int16)
        index = index.astype(jnp.int16)
        in_0 = index < LANES
        in_1 = index < LANES - 1
        step = (clipped_floor(sample_y) - base).astype(jnp.int32).astype(jnp.int16)
        near, after = taken
        at = [slice(j * height + k * 16, j * height + k * 16 + 16) for j in range(TAPS)]
        near_0 = [lookup(near(i), index_0) for i in at]
        next_0 = [lookup(after(i), index_0) for i in at]
        near_1 = [lookup(near(i), index_1) for i in at]
        next_1 = [lookup(after(i), index_1) for i in at]
        top_0 = top_1 = low_0 = low_1 = jnp.zeros((16, LANES), jnp.bfloat16)
        before = step == -1
        for j in range(TAPS):
            value_0 = jnp.where(in_0, near_0[j], next_0[j])
            value_1 = jnp.where(in_1, near_1[j], next_1[j])
            here = step == j
            top_0 = jnp.where(here, value_0, top_0)
            top_1 = jnp.where(here, value_1, top_1)
            low_0 = jnp.where(before, value_0, low_0)
            low_1 = jnp.where(before, value_1, low_1)
            before = here
        upper = weight_0 * top_0.astype(jnp.float32) + weight_1 * top_1.astype(jnp.float32)
        lower = weight_0 * low_0.astype(jnp.float32) + weight_1 * low_1.astype(jnp.float32)
        return upper + part_y * (lower - upper)

    row_groups = height // 8
    block_spans = []
    for b in range(blocks):
        spread = (b % 8) * (LANES // SP) + lax.broadcasted_iota(jnp.int32, (8, LANES), 1) // SP
        expanded = []
        for comp in range(2):
            value, rise, climb = vertex_rows[comp][b // 8]
            at = jnp.take_along_axis(value, spread, axis=1)
            low = jnp.take_along_axis(rise, spread, axis=1)
            high = jnp.take_along_axis(climb, spread, axis=1)
            expanded.append(at + along * jnp.where(left_side, low, high))
        columns = slice(b * LANES, (b + 1) * LANES)
        span = None
        for k in range(row_groups):
            moved = [
                tents[0] * ex[k : k + 1] + tents[1] * ex[k + 1 : k + 2] + tents[2] * ex[k + 2 : k + 3] for ex in expanded
            ]
            sample_x = lane_full + (moved[0] + LANES / 2.0)
            sample_y = sub + (moved[1] + float(k * 8 + height))
            rows = slice(k * 8, k * 8 + 8)
            sample_ref[0, rows, columns] = sample_x
            sample_ref[1, rows, columns] = sample_y
            floor_y = clipped_floor(sample_y)
            base = jnp.min(floor_y, axis=1, keepdims=True)
            base_ref[b, rows, :] = jnp.broadcast_to(base, (8, LANES))
            span = floor_y - base if span is None else jnp.maximum(span, floor_y - base)
        span_ref[b] = span
        spans = span if spans is None else jnp.maximum(spans, span)

    for b in range(blocks):
        columns = slice(b * LANES, (b + 1) * LANES)
        bases = [base_ref[b, k * 16 : k * 16 + 16, :] for k in range(height // 16)]
        taken_ref[b] = tap_rows(bases, slab_ref[:, b * LANES : (b + 2) * LANES])

    copies = []
    for b in range(blocks):
        columns = slice(b * LANES, (b + 1) * LANES)
        taken = (lambda i: taken_ref[b, i, :LANES]), (lambda i: taken_ref[b, i, LANES:])
        for k in range(height // 16):
            rows = slice(k * 16, k * 16 + 16)
            value = render(
                sample_ref[0, rows, columns], sample_ref[1, rows, columns], base_ref[b, rows, :], taken, k
            )
            mixed_ref[rows, columns] = value
            image_ref[rows, columns] = value.astype(jnp.bfloat16)
        if (b + 1) % PIECE == 0:
            columns = slice((b + 1 - PIECE) * LANES, (b + 1) * LANES)
            copies.append(
                pltpu.make_async_copy(image_ref.at[:, columns], out_ref.at[:, columns], sems.at[1 + len(copies)])
            )
            copies[-1].start()

    fit_copy.wait()
    for copy in copies:
        copy.wait()

    @pl.when(jnp.max(spans) > TAPS - 2.0)
    def _():
        for b in range(blocks):
            widest_ref[b] = jnp.max(span_ref[b]).astype(jnp.int32)

        def rest(b, carry):
            widest = widest_ref[b]

            @pl.when(widest > TAPS - 2)
            def _():
                start = pl.multiple_of(b * LANES, LANES)
                columns = pl.ds(start, LANES)
                bases = [base_ref[b, k * 16 : k * 16 + 16, :] for k in range(height // 16)]

                def more(i, c):
                    moved_bases = [base + (i * TAPS).astype(jnp.float32) for base in bases]
                    rows_taken = tap_rows(moved_bases, slab_ref[:, pl.ds(start, 2 * LANES)])
                    taken = (lambda i: rows_taken[i, :LANES]), (lambda i: rows_taken[i, LANES:])
                    for k in range(height // 16):
                        rows = slice(k * 16, k * 16 + 16)
                        mixed_ref[rows, columns] = mixed_ref[rows, columns] + render(
                            sample_ref[0, rows, columns],
                            sample_ref[1, rows, columns],
                            base_ref[b, rows, :] + (i * TAPS).astype(jnp.float32),
                            taken,
                            k,
                        )
                    return c

                lax.fori_loop(1, (widest + 1 + TAPS) // TAPS, more, 0)

            return carry

        lax.fori_loop(0, blocks, rest, 0)
        image_ref[...] = mixed_ref[...].astype(jnp.bfloat16)
        again = pltpu.make_async_copy(image_ref, out_ref, sems.at[1])
        again.start()
        again.wait()


def per_device(points, source, slab_first, slab_count):
    strips = lax.axis_size("ty")
    height, width = source.shape
    tile_len = points.shape[1]
    blocks = width // LANES
    in_chip = [(i, i ^ 1) for i in range(strips)]
    across = []
    for i in range(1, strips - 1, 2):
        across.extend([(i, i + 1), (i + 1, i)])
    vmem = pl.BlockSpec(memory_space=pltpu.VMEM)
    smem = pl.BlockSpec(memory_space=pltpu.SMEM)
    anywhere = pl.BlockSpec(memory_space=pl.ANY)
    params = pltpu.CompilerParams(vmem_limit_bytes=32 * 1024 * 1024)
    small = pltpu.CompilerParams(vmem_limit_bytes=4 * 1024 * 1024)
    mate_points = lax.ppermute(points, "ty", in_chip)
    packed_rows = width // tile_len * height + 16
    packed_shape = jax.ShapeDtypeStruct((packed_rows, tile_len), jnp.bfloat16)
    tile = lax.axis_index("ty")
    cell = lax.broadcasted_iota(jnp.int32, points.shape, 1) // PC
    cell_cols = width // CELL
    origin_x = cell % cell_cols * CELL
    origin_y = tile * height + cell // cell_cols * CELL
    is_x = lax.broadcasted_iota(jnp.int32, points.shape, 0) % 2 == 0
    local = points - jnp.where(is_x, origin_x, origin_y).astype(jnp.float32)
    laid, own_rows = pl.pallas_call(
        lay_own_kernel,
        out_shape=(packed_shape, jax.ShapeDtypeStruct((8, tile_len), jnp.float32)),
        in_specs=[vmem, vmem],
        out_specs=(vmem, vmem),
        compiler_params=small,
        cost_estimate=pl.CostEstimate(flops=0, bytes_accessed=4 * source.size, transcendentals=0),
    )(local, source)
    packed = pl.pallas_call(
        functools.partial(lay_mate_kernel, height, width),
        out_shape=packed_shape,
        in_specs=[vmem, vmem, anywhere],
        out_specs=anywhere,
        input_output_aliases={2: 0},
        scratch_shapes=[pltpu.VMEM((16, tile_len), jnp.bfloat16), pltpu.SemaphoreType.DMA],
        compiler_params=small,
    )(own_rows, mate_points, laid)
    arrived = lax.ppermute(packed, "ty", across)
    mate_source = lax.ppermute(source, "ty", in_chip)
    groups = width // GROUP_PX

    def moment_scratch(sets):
        length = sets * tile_len // groups
        return [
            pltpu.VMEM((groups, 2 * NF, length), jnp.bfloat16),
            pltpu.VMEM((groups, 2 * LANES, length), jnp.bfloat16),
        ]

    totals = pl.pallas_call(
        functools.partial(near_kernel, strips, height, width),
        out_shape=jax.ShapeDtypeStruct((groups, NF, LANES), jnp.float32),
        in_specs=[vmem, vmem],
        out_specs=vmem,
        scratch_shapes=moment_scratch(2),
        compiler_params=params,
        cost_estimate=pl.CostEstimate(flops=4 * NF * LANES * 2 * tile_len * 4, bytes_accessed=10**6, transcendentals=2 * tile_len * NV),
    )(local, mate_points)
    arrived, totals = lax.optimization_barrier((arrived, totals))
    far = lax.ppermute(arrived[packed_rows - 16 : packed_rows - 8], "ty", in_chip)
    return pl.pallas_call(
        functools.partial(main_kernel, strips),
        out_shape=(
            jax.ShapeDtypeStruct((height, width), jnp.bfloat16),
            jax.ShapeDtypeStruct((6, VR, width // SP), jnp.float32),
        ),
        in_specs=[smem, smem] + [vmem] * 5,
        out_specs=(anywhere, anywhere),
        scratch_shapes=moment_scratch(3)
        + [
            pltpu.VMEM((LANES, width + LANES), jnp.bfloat16),
            pltpu.VMEM((2, height, width), jnp.float32),
            pltpu.VMEM((blocks, height, LANES), jnp.float32),
            pltpu.VMEM((blocks, 8, LANES), jnp.float32),
            pltpu.VMEM((blocks, TAPS * height, 2 * LANES), jnp.bfloat16),
            pltpu.VMEM((height, width), jnp.float32),
            pltpu.VMEM((height, width), jnp.bfloat16),
            pltpu.VMEM((6, VR, width // SP), jnp.float32),
            pltpu.SMEM((blocks,), jnp.int32),
            pltpu.SemaphoreType.DMA((1 + blocks // PIECE,)),
        ],
        compiler_params=params,
    )(slab_first, slab_count, totals, source, mate_source, arrived, far)


def solution(mesh):
    return jax.shard_map(
        per_device,
        mesh=mesh,
        in_specs=(
            P(None, ("sec", "ty")),
            P(("sec", "ty"), None),
            P(("sec", "ty")),
            P(("sec", "ty")),
        ),
        out_specs=(P(("sec", "ty"), None), P(None, ("sec", "ty"), None)),
        check_vma=False,
    )
```
